32 devices in a mesh: pass: 4 (over x, core), dp: 8 (over z, y).
Axes of the slice: x: 2, y: 2, z: 4, core: 2. Of those that a mesh axis runs over, the one named last changes fastest.
Arguments:
- block_input: bfloat16 [4, 6144, 768], P('pass', 'dp'), may hold values from -6 to 6
- segments: int32 [6144], P('dp'), may hold values from 0 to 23, as said below
- pass_emb: float32 [4, 768], replicated, may hold values from -3 to 3
- gain_attn: float32 [768], replicated, may hold values from 0.1 to 1.9
- w_qkv: bfloat16 [768, 2304], replicated, may hold values from -0.21875 to 0.21875
- w_out: bfloat16 [768, 768], replicated, may hold values from -1.25 to 1.25
- gain_mlp: float32 [768], replicated, may hold values from 0.1 to 1.9
- w_up: bfloat16 [768, 3072], replicated, may hold values from -0.21875 to 0.21875
- w_down: bfloat16 [3072, 768], replicated, may hold values from -0.109375 to 0.109375
- cotangent: bfloat16 [4, 6144, 768], P('pass', 'dp'), may hold values from -6 to 6
Outputs:
- block_output: bfloat16 [4, 6144, 768], P('pass', 'dp')
- grad_input: bfloat16 [4, 6144, 768], P('pass', 'dp')
- grad_pass_emb: float32 [4, 768], replicated
- grad_gain_attn: float32 [768], replicated
- grad_w_qkv: float32 [768, 2304], replicated
- grad_w_out: float32 [768, 768], replicated
- grad_gain_mlp: float32 [768], replicated
- grad_w_up: float32 [768, 3072], replicated
- grad_w_down: float32 [3072, 768], replicated
The draws below stay inside these ranges and needn't reach their ends.
Inputs may be any that keep to these rules, and one draw needn't show every extreme that they name: `segments`: within each aligned block of 768 positions (one index of dp) the ids never fall and the block holds either one sequence of 768 positions or 3 sequences of 256 positions; different blocks have different ids. The first block holds short sequences and the second one long sequence.
All inputs are finite; a program needn't handle non-finite values.
Results may differ from the reference program's by a relative error of at most 0.015.
Values may be sent and summed in bfloat16 or wider, within the bound.
No kernel may reach another device: no remote copies, remote signals or barrier semaphores. Data moves between devices by JAX's collectives and lax.ppermute only.
A program may use at most 192 MiB of HBM per device.

```python
import jax
import jax.numpy as jnp
from jax import lax

D = 768
HEADS = 12
HEAD_DIM = 64
FF = 3072
SHORT = 256
TOK_DEV = 768
PASSES = 4
TOKENS = 6144
N_DP = 8


def draw_segments(key, part):
    blocks_all = TOKENS // TOK_DEV
    per_block = TOK_DEV // SHORT
    short_flag = jax.random.randint(key, (blocks_all,), 0, 2)
    short_flag = short_flag.at[0].set(1).at[1].set(0)
    position = jnp.arange(TOK_DEV)
    short_ids = position // SHORT
    seg_ids = jnp.where(short_flag[:, None] == 1, short_ids[None, :], per_block - 1)
    seg_ids = seg_ids + jnp.arange(blocks_all)[:, None] * per_block
    return seg_ids.reshape(-1).astype(jnp.int32)


def spiked(result, rng, source, target, parts, factor):
    def block_of(dim):
        return (jnp.arange(result.shape[dim]) // (result.shape[dim] // parts)).reshape((-1,) + (1,) * (result.ndim - 1 - dim))

    near = jax.random.permutation(rng, parts)[block_of(target)]
    second = (block_of(target) + parts // 2) % parts
    return jnp.where((block_of(source) == near) | (block_of(source) == second), factor * result, result)


def shard_levels(own_key, dims, pieces, low, high):
    loudness, own = 1.0, jax.random.fold_in(own_key, 6)
    for axis_at, blocks in pieces:
        steps = jnp.exp(jax.random.uniform(jax.random.fold_in(own, axis_at), (blocks,), jnp.float32, low / len(pieces), high / len(pieces)))
        loudness = loudness * jnp.repeat(steps, dims[axis_at] // blocks).reshape([-1 if axis == axis_at else 1 for axis in range(len(dims))])
    return loudness


def scatter_about(own_key, shape, scale, reach, cuts=(), kind=jnp.bfloat16):
    values = jax.random.normal(own_key, shape, jnp.float32) * scale
    if len(cuts) > 0:
        values = shard_levels(own_key, shape, cuts, -0.22, 0.18) * values
    return jnp.clip(values, min=-reach, max=reach).astype(kind)


def bell_draw_with(key, shape, scale, most, shards, heavy, kind=jnp.bfloat16):
    values = scale * jax.random.normal(key, shape, jnp.float32)
    if shards:
        values = values * shard_levels(key, shape, shards, -0.22, 0.18)
    return jnp.clip(spiked(values, jax.random.fold_in(key, 3), *heavy), -most, most).astype(kind)


def setup_inputs(seed: int = 0) -> dict:
    key_of = jax.random.split(jax.random.key(seed), 11)
    block_input = scatter_about(key_of[0], (PASSES, TOKENS, D), 1.0, 6.0, ((0, 4), (1, 8)))
    segments = draw_segments(jax.random.fold_in(key_of[10], 71), 0)
    pass_emb = scatter_about(key_of[2], (PASSES, D), 0.5, 3.0, (), jnp.float32)
    gain_attn = jnp.clip(1.0 + 0.18 * jax.random.normal(key_of[3], (D,), jnp.float32), 0.1, 1.9)
    w_qkv = scatter_about(key_of[4], (D, 3 * D), D ** -0.5, 0.21875)
    w_out = scatter_about(key_of[5], (D, D), (max(D // 32, 4)) ** -0.5, 1.25)
    gain_mlp = jnp.clip(1.0 + 0.18 * jax.random.normal(key_of[6], (D,), jnp.float32), 0.1, 1.9)
    w_up = scatter_about(key_of[7], (D, FF), D ** -0.5, 0.21875)
    w_down = scatter_about(key_of[8], (FF, D), FF ** -0.5, 0.109375)
    cotangent = bell_draw_with(key_of[9], (PASSES, TOKENS, D), 1.0, 6.0, ((0, 4), (1, 8)), (1, 2, 8, 2.0))
    return dict(block_input=block_input, segments=segments, pass_emb=pass_emb, gain_attn=gain_attn, w_qkv=w_qkv, w_out=w_out, gain_mlp=gain_mlp, w_up=w_up, w_down=w_down, cotangent=cotangent)


@jax.custom_vjp
def low(v):
    return lax.optimization_barrier(v.astype(jnp.bfloat16)).astype(jnp.float32)

@jax.custom_vjp
def low_back(v):
    return v

def low_keep(v):
    return (low(v), None)

def low_pass(kept, grad):
    return (grad,)

def back_keep(v):
    return (v, None)

def back_low(kept, grad):
    return (low(grad),)
low.defvjp(low_keep, low_pass)
low_back.defvjp(back_keep, back_low)

def layer_norm(hidden, gain_vec):
    center = hidden - lax.optimization_barrier(jnp.mean(hidden, axis=-1, keepdims=True))
    spread = lax.optimization_barrier(jnp.mean(center * center, axis=-1, keepdims=True))
    return center * lax.rsqrt(spread + 1e-05) * gain_vec

def matmul(left_mat, right_mat):
    return jnp.einsum('...i,ij->...j', left_mat, right_mat, precision=lax.Precision.HIGHEST)

def pack_block(x_pack, seg_pack, params):
    pass_emb, gain_attn, w_qkv, w_out, gain_mlp, w_up, w_down = params
    passes = x_pack.shape[0]
    length = x_pack.shape[1]
    rows_all = passes * length
    hidden = x_pack + pass_emb[:, None, :]
    normed = low(layer_norm(hidden, gain_attn))
    projected = low_back(low(matmul(normed, w_qkv)))
    queries = projected[..., :D].reshape(rows_all, HEADS, HEAD_DIM).transpose(1, 0, 2)
    keys = projected[..., D:2 * D].reshape(rows_all, HEADS, HEAD_DIM).transpose(1, 0, 2)
    values = projected[..., 2 * D:].reshape(rows_all, HEADS, HEAD_DIM).transpose(1, 0, 2)
    score_scale = HEAD_DIM ** (-0.5)
    row_ids = jnp.arange(rows_all)
    row_pass = row_ids // length
    row_pos = row_ids % length
    row_seg = jnp.tile(seg_pack, passes)
    allowed = (row_pass[None, :] <= row_pass[:, None]) & (row_pos[None, :] <= row_pos[:, None]) & (row_seg[None, :] == row_seg[:, None])

    def one_head(triple):
        q_head, k_head, v_head = triple
        scores = low_back(jnp.einsum('qd,kd->qk', q_head, k_head, precision=lax.Precision.HIGHEST) * score_scale)
        masked = jnp.where(allowed, scores, -1e+30)
        weights = jnp.exp(masked - jax.nn.logsumexp(masked, axis=-1, keepdims=True))
        prob_bf = low(weights)
        return jnp.einsum('qk,kd->qd', prob_bf, v_head, precision=lax.Precision.HIGHEST)
    heads_out = lax.map(jax.checkpoint(one_head), (queries, keys, values))
    attended = heads_out.transpose(1, 0, 2).reshape(passes, length, D)
    attended = low_back(low(attended))
    attn_out = low_back(matmul(attended, w_out))
    residual = hidden + attn_out
    normed2 = low(layer_norm(residual, gain_mlp))
    up_proj = low_back(matmul(normed2, w_up))
    activated = low(jax.nn.gelu(up_proj, approximate=True))
    return residual + matmul(activated, w_down)

def reference(block_input, segments, pass_emb, gain_attn, w_qkv, w_out, gain_mlp, w_up, w_down, cotangent):
    seg_packs = segments.reshape(N_DP, TOK_DEV)

    def forward(x_float, *params):
        x_packs = x_float.reshape(PASSES, N_DP, TOK_DEV, D).transpose(1, 0, 2, 3)
        block_fn = jax.checkpoint(lambda x_pack, seg_pack: pack_block(x_pack, seg_pack, params))

        def scan_step(running, inputs_pair):
            return (running, block_fn(inputs_pair[0], inputs_pair[1]))
        unused, results = lax.scan(scan_step, jnp.zeros((), jnp.float32), (x_packs, seg_packs))
        return results.transpose(1, 0, 2, 3).reshape(PASSES, TOKENS, D)
    output, pull = jax.vjp(forward, block_input.astype(jnp.float32), pass_emb, gain_attn, w_qkv.astype(jnp.float32), w_out.astype(jnp.float32), gain_mlp, w_up.astype(jnp.float32), w_down.astype(jnp.float32))
    grads = pull(cotangent.astype(jnp.float32))
    return (output.astype(jnp.bfloat16), grads[0].astype(jnp.bfloat16), grads[1], grads[2], grads[3], grads[4], grads[5], grads[6], grads[7])
```

```python
import functools
import math

import jax
import jax.numpy as jnp
from jax import lax
from jax.experimental import pallas as pl
from jax.experimental.pallas import tpu as pltpu
from jax.sharding import PartitionSpec as P

D = 768
HEADS = 12
HEAD_DIM = 64
SHORT = 256
GROUP = D // 2
HALF = GROUP // 2
EPS = 1e-05
SCALE = HEAD_DIM**-0.5
SCALE2 = SCALE * math.log2(math.e)
BF = jnp.bfloat16
F32 = jnp.float32


def dot(a, b, ca, cb):
    return lax.dot_general(a, b, (((ca,), (cb,)), ((), ())), preferred_element_type=F32)


def mask_tail(scores):
    n = scores.shape[0]
    key = lax.broadcasted_iota(jnp.int32, (SHORT, SHORT), 0)
    query = lax.broadcasted_iota(jnp.int32, (SHORT, SHORT), 1)
    diag = jnp.where(key <= query, scores[n - SHORT :], -1e30)
    return diag if n == SHORT else jnp.concatenate([scores[: n - SHORT], diag], 0)


def over_tiles(flag_ref, tiles, cross, tile):
    one_sequence = flag_ref[0] == 1
    even = 0 if cross else flag_ref[1]
    odd = 1 - even

    def run(whole):
        for at in range(tiles):
            first = 0 if whole else at
            tile(even, at, [even, odd] if cross else [even], first)
            tile(odd, at, [even, odd], first)

    pl.when(one_sequence)(lambda: run(True))
    pl.when(jnp.logical_not(one_sequence))(lambda: run(False))


def forward_kernel(flag_ref, q_ref, k_ref, v_ref, o_ref, lse_ref, *, cross):
    def tile(qp, at, keys, first):
        qs, ks = slice(at * SHORT, (at + 1) * SHORT), slice(first * SHORT, (at + 1) * SHORT)
        q = q_ref[qp, :, qs]
        scores = [mask_tail(dot(k_ref[kp, :, ks], q, 0, 0) * SCALE2) for kp in keys]
        top = functools.reduce(
            jnp.maximum, [jnp.max(s, axis=0, keepdims=True) for s in scores]
        )
        raw = [jnp.exp2(s - top) for s in scores]
        total = functools.reduce(jnp.add, [jnp.sum(p, axis=0, keepdims=True) for p in raw])
        out = functools.reduce(
            jnp.add, [dot(v_ref[kp, :, ks], p.astype(BF), 1, 0) for kp, p in zip(keys, raw)]
        )
        o_ref[qp, :, qs] = out * (1.0 / total)
        lse_ref[0, pl.ds(qp, 1), qs] = top + jnp.log2(total)

    over_tiles(flag_ref, q_ref.shape[2] // SHORT, cross, tile)


def backward_kernel(
    flag_ref, q_ref, k_ref, v_ref, g_ref, lse_ref, delta_ref, dq_ref, dk_ref, dv_ref, dk_acc, dv_acc, *, cross
):
    dk_acc[...] = jnp.zeros_like(dk_acc)
    dv_acc[...] = jnp.zeros_like(dv_acc)

    def tile(qp, at, keys, first):
        qs, ks = slice(at * SHORT, (at + 1) * SHORT), slice(first * SHORT, (at + 1) * SHORT)
        q, g = q_ref[qp, :, qs], g_ref[qp, :, qs]
        lse, delta = lse_ref[0, pl.ds(qp, 1), qs], delta_ref[0, pl.ds(qp, 1), qs]
        dq = None
        for kp in keys:
            k, v = k_ref[kp, :, ks], v_ref[kp, :, ks]
            weights = jnp.exp2(mask_tail(dot(k, q, 0, 0) * SCALE2) - lse)
            ds = (weights * (dot(v, g, 0, 0) - delta)).astype(BF)
            term = dot(k, ds, 1, 0)
            dq = term if dq is None else dq + term
            dk_acc[kp, :, ks] += dot(q, ds, 1, 1)
            dv_acc[kp, :, ks] += dot(g, weights.astype(BF), 1, 1)
        dq_ref[qp, :, qs] = (dq * SCALE).astype(dq_ref.dtype)

    over_tiles(flag_ref, q_ref.shape[2] // SHORT, cross, tile)
    dk_ref[...] = (dk_acc[...] * SCALE).astype(dk_ref.dtype)
    dv_ref[...] = dv_acc[...].astype(dv_ref.dtype)


def head_spec(length, part, heads):
    return pl.BlockSpec((2, HEAD_DIM, length), lambda h, flags: (0, part * heads + h, 0))


def row_spec(length):
    return pl.BlockSpec((1, 2, length), lambda h, flags: (h, 0, 0))


def attend(flags, queries, keys, values, cross):
    length, heads = queries[0].shape[2], HEADS // 4 if cross else HEADS // 2
    rows = heads * HEAD_DIM
    units = 4 if cross else 3
    flops = 4 * units * heads * length * length * HEAD_DIM
    return pl.pallas_call(
        functools.partial(forward_kernel, cross=cross),
        grid_spec=pltpu.PrefetchScalarGridSpec(
            num_scalar_prefetch=1,
            grid=(heads,),
            in_specs=[head_spec(length, part, heads) for _, part in (queries, keys, values)],
            out_specs=[head_spec(length, 0, heads), row_spec(length)],
        ),
        out_shape=[
            jax.ShapeDtypeStruct((2, rows, length), F32),
            jax.ShapeDtypeStruct((heads, 2, length), F32),
        ],
        cost_estimate=pl.CostEstimate(
            flops=4 * flops, bytes_accessed=2 * rows * length * 10, transcendentals=0
        ),
        compiler_params=pltpu.CompilerParams(vmem_limit_bytes=40 << 20),
        name="attend_cross" if cross else "attend_local",
    )(flags, queries[0], keys[0], values[0])


def attend_back(flags, queries, keys, values, grads, lse, delta, cross, out_type):
    length, heads = queries[0].shape[2], HEADS // 4 if cross else HEADS // 2
    rows = heads * HEAD_DIM
    units = 4 if cross else 3
    flops = 10 * units * heads * length * length * HEAD_DIM
    return pl.pallas_call(
        functools.partial(backward_kernel, cross=cross),
        grid_spec=pltpu.PrefetchScalarGridSpec(
            num_scalar_prefetch=1,
            grid=(heads,),
            in_specs=[
                head_spec(length, part, heads) for _, part in (queries, keys, values, grads)
            ]
            + [row_spec(length)] * 2,
            out_specs=[head_spec(length, 0, heads)] * 3,
            scratch_shapes=[pltpu.VMEM((2, HEAD_DIM, length), F32)] * 2,
        ),
        out_shape=[jax.ShapeDtypeStruct((2, rows, length), out_type)] * 3,
        cost_estimate=pl.CostEstimate(
            flops=3 * flops, bytes_accessed=2 * rows * length * 20, transcendentals=0
        ),
        compiler_params=pltpu.CompilerParams(vmem_limit_bytes=40 << 20),
        name="attend_back_cross" if cross else "attend_back_local",
    )(flags, queries[0], keys[0], values[0], grads[0], lse, delta)


def swap(array, step):
    axis, mask, size = step
    return lax.ppermute(array, axis, [(i, i ^ mask) for i in range(size)])


def side(step):
    axis, mask, _ = step
    return (lax.axis_index(axis) // mask) % 2


def halve(total, step):
    here, half = side(step), total.shape[0] // 2
    sent = lax.dynamic_slice_in_dim(total, (1 - here) * half, half, 0).astype(BF)
    kept = lax.dynamic_slice_in_dim(total, here * half, half, 0)
    return kept + swap(sent, step).astype(F32)


def join(own, other, step, axis=0):
    return jnp.where(
        side(step) == 0,
        jnp.concatenate([own, other], axis),
        jnp.concatenate([other, own], axis),
    )


def sum_over(total, steps):
    for step in steps:
        total = halve(total, step)
    total = total.astype(BF)
    for step in reversed(steps):
        total = join(total, swap(total, step), step)
    return total


def on_device(
    sizes, block_input, segments, pass_emb, gain_attn, w_qkv, w_out, gain_mlp, w_up, w_down, cotangent
):
    passes, n_dp = sizes
    core = ("pass", 1, passes)
    cross = ("pass", 2, passes)
    lanes = [("dp", 1 << i, n_dp) for i in range(n_dp.bit_length() - 1)]
    order_a = [cross] + lanes
    order_b = lanes[:1] + [cross] + lanes[1:]
    order_c = lanes[1:] + [cross] + lanes[:1]

    pass_here = lax.axis_index("pass")
    core_here = pass_here % 2
    early = pass_here < 2
    to_late = [(0, 2), (1, 3)]
    to_early = [(2, 0), (3, 1)]
    length = segments.shape[0]
    one_sequence = (segments[0] == segments[length - 1]).astype(jnp.int32)
    flags = jnp.stack([one_sequence, core_here.astype(jnp.int32)])

    emb_row = lax.dynamic_index_in_dim(pass_emb, pass_here, 0, keepdims=False)
    hidden = block_input[0].astype(F32) + emb_row
    center = hidden - jnp.mean(hidden, axis=-1, keepdims=True)
    inv_attn = lax.rsqrt(jnp.mean(center * center, axis=-1, keepdims=True) + EPS)
    normed = (center * inv_attn * gain_attn).astype(BF)
    projected = dot(w_qkv, normed, 0, 1).astype(BF).reshape(3, 2, GROUP, length)

    own = lax.dynamic_index_in_dim(projected, core_here, 1, keepdims=False)
    theirs = lax.dynamic_index_in_dim(projected, 1 - core_here, 1, keepdims=False)
    pair = jnp.stack([own, swap(theirs, core)])
    normed_partner = swap(normed, core)
    kv_late = lax.ppermute(pair[:, 1:, :HALF], "pass", to_late)
    q_early = lax.ppermute(pair[:, 0, HALF:], "pass", to_early)
    flat = pair.reshape(2, 3 * GROUP, length)
    out_local, lse_local = attend(flags, (flat, 0), (flat, 1), (flat, 2), False)
    q_cross = jnp.where(early, q_early, pair[:, 0, :HALF])
    kv_cross = jnp.where(early, pair[:, 1:, HALF:], kv_late).reshape(2, 2 * HALF, length)
    out_cross, lse_cross = attend(flags, (q_cross, 0), (kv_cross, 0), (kv_cross, 1), True)
    out_back = lax.ppermute(out_cross.astype(BF), "pass", to_late)
    lse_back = lax.ppermute(lse_cross, "pass", to_late)

    lse_other = jnp.concatenate([lse_cross, lse_back], 0)
    out_other = jnp.concatenate([out_cross, out_back.astype(F32)], 1)
    top = jnp.maximum(lse_local, lse_other)
    lse_both = top + jnp.log2(jnp.exp2(lse_local - top) + jnp.exp2(lse_other - top))
    lse = jnp.where(early, lse_local, lse_both)
    share_local = jnp.where(early, 1.0, jnp.exp2(lse_local - lse)).transpose(1, 0, 2)[:, :, None]
    share_other = jnp.where(early, 0.0, jnp.exp2(lse_other - lse_both)).transpose(1, 0, 2)[:, :, None]
    by_head = (2, HEADS // 2, HEAD_DIM, length)
    attended_f32 = (
        out_local.reshape(by_head) * share_local + out_other.reshape(by_head) * share_other
    )
    attended_pair = attended_f32.reshape(2, GROUP, length).astype(BF)
    attended = join(attended_pair[0], swap(attended_pair[1], core), core)

    residual = hidden + dot(attended, w_out, 0, 0)
    center2 = residual - jnp.mean(residual, axis=-1, keepdims=True)
    inv_mlp = lax.rsqrt(jnp.mean(center2 * center2, axis=-1, keepdims=True) + EPS)
    n2 = center2 * inv_mlp
    normed2 = (n2 * gain_mlp).astype(BF)
    up_proj = dot(normed2, w_up, 1, 0)
    activated_val, gelu_pull = jax.vjp(lambda u: jax.nn.gelu(u, approximate=True), up_proj)
    activated = activated_val.astype(BF)
    output = (residual + dot(activated, w_down, 1, 0)).astype(BF)

    grad_out = cotangent[0]
    ff_half = activated.shape[1] // 2

    def columns(array, which, width):
        return lax.dynamic_slice_in_dim(array, which * width, width, 1)

    down_sent = dot(columns(activated, 1 - core_here, ff_half), grad_out, 0, 0).astype(BF)
    down_recv = swap(down_sent, core)
    grad_up = gelu_pull(dot(grad_out, w_down, 1, 1))[0].astype(BF)
    down_half = dot(columns(activated, core_here, ff_half), grad_out, 0, 0) + down_recv.astype(F32)
    up_sent = dot(columns(normed2, 1 - core_here, GROUP), grad_up, 0, 0).astype(BF)
    up_recv = swap(up_sent, core)
    grad_normed2 = dot(grad_up, w_up, 1, 1)
    up_half = dot(columns(normed2, core_here, GROUP), grad_up, 0, 0) + up_recv.astype(F32)
    grad_gain_mlp = jnp.sum(grad_normed2 * n2, axis=0)
    scaled = grad_normed2 * gain_mlp
    grad_residual = grad_out.astype(F32) + inv_mlp * (
        scaled
        - jnp.mean(scaled, axis=-1, keepdims=True)
        - n2 * jnp.mean(scaled * n2, axis=-1, keepdims=True)
    )
    grad_attn = grad_residual.astype(BF)

    grad_attn_pair = jnp.stack([grad_attn, swap(grad_attn, core)])
    w_out_half = lax.dynamic_slice_in_dim(w_out, core_here * GROUP, GROUP, 0)
    grad_attended = jnp.stack(
        [dot(w_out_half, grad_attn_pair[i], 1, 1) for i in range(2)]
    ).astype(BF)
    delta = jnp.sum(grad_attended.astype(F32).reshape(by_head) * attended_f32, axis=2).transpose(
        1, 0, 2
    )
    half_heads = HEADS // 4
    grad_early = lax.ppermute(grad_attended[:, HALF:], "pass", to_early)
    rows_early = lax.ppermute(
        jnp.stack([lse[half_heads:], delta[half_heads:]]), "pass", to_early
    )
    out_half = dot(attended_pair[0], grad_attn_pair[0], 1, 0) + dot(
        attended_pair[1], grad_attn_pair[1], 1, 0
    )
    dq_local, dk_local, dv_local = attend_back(
        flags, (flat, 0), (flat, 1), (flat, 2), (grad_attended, 0), lse, delta, False, F32
    )
    grad_cross = jnp.where(early, grad_early, grad_attended[:, :HALF])
    lse_x = jnp.where(early, rows_early[0], lse[:half_heads])
    delta_x = jnp.where(early, rows_early[1], delta[:half_heads])
    dq_cross, dk_cross, dv_cross = attend_back(
        flags, (q_cross, 0), (kv_cross, 0), (kv_cross, 1), (grad_cross, 0), lse_x, delta_x, True, BF
    )
    dq_back = lax.ppermute(dq_cross, "pass", to_late)
    dkv_back = lax.ppermute(jnp.stack([dk_cross, dv_cross]), "pass", to_early)
    dq = dq_local + jnp.where(
        early, 0.0, jnp.concatenate([dq_cross, dq_back], 1).astype(F32)
    )
    dk = dk_local + jnp.where(
        early, jnp.concatenate([dkv_back[0], dk_cross], 1).astype(F32), 0.0
    )
    dv = dv_local + jnp.where(
        early, jnp.concatenate([dkv_back[1], dv_cross], 1).astype(F32), 0.0
    )
    grad_pair = jnp.stack([dq, dk, dv], 1).astype(BF)
    grad_other = swap(grad_pair[1], core)
    parts = [
        dot(normed, grad_pair[0, i], 0, 1) + dot(normed_partner, grad_pair[1, i], 0, 1)
        for i in range(3)
    ]

    grad_normed = jnp.zeros((length, D), F32)
    w_by_core = w_qkv.reshape(D, 3, 2, GROUP)
    w_own = lax.dynamic_index_in_dim(w_by_core, core_here, 2, keepdims=False).reshape(D, 3 * GROUP)
    w_other = lax.dynamic_index_in_dim(w_by_core, 1 - core_here, 2, keepdims=False).reshape(
        D, 3 * GROUP
    )
    grad_normed = dot(grad_pair[0].reshape(3 * GROUP, length), w_own, 0, 1) + dot(
        grad_other.reshape(3 * GROUP, length), w_other, 0, 1
    )
    n1 = center * inv_attn
    grad_gain_attn = jnp.sum(grad_normed * n1, axis=0)
    scaled1 = grad_normed * gain_attn
    grad_hidden = grad_residual + inv_attn * (
        scaled1
        - jnp.mean(scaled1, axis=-1, keepdims=True)
        - n1 * jnp.mean(scaled1 * n1, axis=-1, keepdims=True)
    )
    selector = (jnp.arange(passes) == pass_here).astype(F32)
    small = jnp.concatenate(
        [
            selector[:, None] * jnp.sum(grad_hidden, axis=0)[None],
            grad_gain_attn[None],
            grad_gain_mlp[None],
        ]
    )
    for step in [core, cross] + lanes:
        small = small + swap(small, step)

    def whole(half, steps, axis=0):
        half = sum_over(half, steps)
        return join(half, swap(half, core), core, axis).astype(F32)

    down_total = whole(down_half, order_a)
    up_total = whole(up_half, order_b)
    out_total = whole(out_half, order_c)
    qkv_total = jnp.concatenate(
        [
            whole(part, order, 1)
            for part, order in zip(parts, (order_a, order_b, order_c), strict=True)
        ],
        axis=1,
    )
    return (
        output[None],
        grad_hidden.astype(BF)[None],
        small[:passes],
        small[passes],
        qkv_total,
        out_total,
        small[passes + 1],
        up_total,
        down_total,
    )


def solution(mesh):
    sizes = (mesh.shape["pass"], mesh.shape["dp"])
    tokens = P("pass", "dp", None)
    in_specs = (tokens, P("dp")) + (P(),) * 7 + (tokens,)
    out_specs = (tokens, tokens) + (P(),) * 7
    return jax.shard_map(
        functools.partial(on_device, sizes),
        mesh=mesh,
        in_specs=in_specs,
        out_specs=out_specs,
        check_vma=False,
    )
```

```python
import functools
import math

import jax
import jax.numpy as jnp
from jax import lax
from jax.experimental import pallas as pl
from jax.experimental.pallas import tpu as pltpu
from jax.sharding import PartitionSpec as P

D = 768
HEADS = 12
HEAD_DIM = 64
SHORT = 256
FF_TILE = 512
GROUP = D // 2
HALF = GROUP // 2
HALF_HEADS = HEADS // 4
EPS = 1e-05
SCALE = HEAD_DIM**-0.5
SCALE2 = SCALE * math.log2(math.e)
BF = jnp.bfloat16
F32 = jnp.float32


def dot(a, b, ca, cb):
    return lax.dot_general(a, b, (((ca,), (cb,)), ((), ())), preferred_element_type=F32)


def cost(us):
    return pl.CostEstimate(flops=int(us * 1.1e9), bytes_accessed=1 << 20, transcendentals=0)


def params(mib):
    return pltpu.CompilerParams(vmem_limit_bytes=mib << 20)


def call(kernel, flags, grid, ins, outs, us, name, mib=48, scratch=()):
    return pl.pallas_call(
        kernel,
        grid_spec=pltpu.PrefetchScalarGridSpec(
            num_scalar_prefetch=1,
            grid=grid,
            in_specs=[pl.BlockSpec(block, index) for _, block, index in ins],
            out_specs=[pl.BlockSpec(block, index) for _, _, block, index in outs],
            scratch_shapes=list(scratch),
        ),
        out_shape=[jax.ShapeDtypeStruct(shape, dtype) for shape, dtype, _, _ in outs],
        cost_estimate=cost(us),
        compiler_params=params(mib),
        name=name,
    )(flags, *[array for array, _, _ in ins])


def fixed(array):
    return (array, array.shape, lambda i, f: (0,) * array.ndim)


def out_fixed(shape, dtype):
    return (shape, dtype, shape, lambda i, f: (0,) * len(shape))


def row(vector):
    return vector.reshape(1, -1)


def one_sequence(f):
    return f[0] == 1


def hidden_of(x_ref, emb_ref):
    return x_ref[...].astype(F32) + emb_ref[0]


def centered(values):
    center = values - jnp.mean(values, axis=-1, keepdims=True)
    return center, lax.rsqrt(jnp.mean(center * center, axis=-1, keepdims=True) + EPS)


def write_part(part, out_ref, low_ref, high_ref, value):
    out_ref[...] = value

    @pl.when(part == 0)
    def _():
        high_ref[...] = value[HALF:]

    @pl.when(part > 0)
    def _():
        low_ref[pl.ds(pl.multiple_of((part - 1) * HALF, HALF), HALF), :] = value[:HALF]


def norm_project_kernel(f, x_ref, emb_ref, gain_ref, w_ref, normed_ref, out_ref, low_ref, high_ref):
    part = pl.program_id(0)

    @pl.when(part == 0)
    def _():
        center, inv = centered(hidden_of(x_ref, emb_ref))
        normed_ref[...] = (center * inv * gain_ref[...]).T.astype(BF)

    value = dot(w_ref[...], normed_ref[...], 0, 0).astype(BF)
    write_part(part, out_ref, low_ref, high_ref, value)


def project_kernel(f, normed_ref, w_ref, out_ref, low_ref, high_ref):
    value = dot(w_ref[...], normed_ref[...], 0, 0).astype(BF)
    write_part(pl.program_id(0), out_ref, low_ref, high_ref, value)


def projection_outs(length):
    return [
        ((3 * GROUP, length), BF, (GROUP, length), lambda i, f: (i, 0)),
        out_fixed((2 * HALF, length), BF),
        out_fixed((HALF, length), BF),
    ]


def mask_tail(scores):
    n = scores.shape[0]
    key = lax.broadcasted_iota(jnp.int32, (SHORT, SHORT), 0)
    query = lax.broadcasted_iota(jnp.int32, (SHORT, SHORT), 1)
    diag = jnp.where(key <= query, scores[n - SHORT :], -1e30)
    return diag if n == SHORT else jnp.concatenate([scores[: n - SHORT], diag], 0)


def sweep(f, length, tile, variants):
    for condition, units in variants:
        for whole in (True, False):

            @pl.when(condition & (one_sequence(f) == whole))
            def _():
                for at in range(length // SHORT):
                    for unit in units:
                        tile(unit, at, 0 if whole else at)


def spans(at, first):
    return slice(at * SHORT, (at + 1) * SHORT), slice(first * SHORT, (at + 1) * SHORT)


def softmax_tile(q_refs, k_refs, v_refs, o_refs, lse_ref, unit, at, first):
    qp, keys = unit
    qs, ks = spans(at, first)
    q = q_refs[qp][:, qs]
    scores = [mask_tail(dot(k_refs[kp][:, ks], q, 0, 0) * SCALE2) for kp in keys]
    top = functools.reduce(jnp.maximum, [jnp.max(s, axis=0, keepdims=True) for s in scores])
    raw = [jnp.exp2(s - top) for s in scores]
    total = functools.reduce(jnp.add, [jnp.sum(p, axis=0, keepdims=True) for p in raw])
    out = functools.reduce(
        jnp.add, [dot(v_refs[kp][:, ks], p.astype(BF), 1, 0) for kp, p in zip(keys, raw)]
    )
    o_refs[qp][:, qs] = (out * (1.0 / total)).astype(o_refs[qp].dtype)
    lse_ref[0, qp : qp + 1, qs] = top + jnp.log2(total)


LOCAL_UNITS = (
    lambda f: (f[1] == 0, [(0, [0]), (1, [0, 1])]),
    lambda f: (f[1] == 1, [(1, [1]), (0, [0, 1])]),
)
CROSS_UNITS = [(0, [0, 1]), (1, [0, 1])]


def local_kernel(f, q0, q1, k0, k1, v0, v1, o0, o1, lse_ref):
    sweep(
        f,
        q0.shape[1],
        functools.partial(softmax_tile, (q0, q1), (k0, k1), (v0, v1), (o0, o1), lse_ref),
        [unit(f) for unit in LOCAL_UNITS],
    )


def cross_kernel(f, *refs):
    ins, (o_ref, lse_ref) = refs[:12], refs[12:]
    outs = (o_ref.at[0], o_ref.at[1])
    for early, at in ((1, 0), (0, 6)):
        q0, q1, k0, k1, v0, v1 = ins[at : at + 6]
        sweep(
            f,
            q0.shape[1],
            functools.partial(softmax_tile, (q0, q1), (k0, k1), (v0, v1), outs, lse_ref),
            [(f[2] == early, CROSS_UNITS)],
        )


def head(array, at):
    return (array, (HEAD_DIM, array.shape[-1]), lambda h, f: (at + h, 0))


def lse_spec(array):
    return (array, (1,) + array.shape[1:], lambda h, f: (h, 0, 0))


def lse_out(heads, length):
    return ((heads, 2, length), F32, (1, 2, length), lambda h, f: (h, 0, 0))


def cross_inputs(early_q, own, other, late_kv):
    return [
        head(early_q[0], 0),
        head(early_q[1], 0),
        head(own, 6 + HALF_HEADS),
        head(other, 6 + HALF_HEADS),
        head(own, 12 + HALF_HEADS),
        head(other, 12 + HALF_HEADS),
        head(own, 0),
        head(other, 0),
        head(late_kv[0], 0),
        head(late_kv[1], 0),
        head(late_kv[0], HALF_HEADS),
        head(late_kv[1], HALF_HEADS),
    ]


def merge_kernel(f, o0, o1, lse_ref, oc_ref, lsec_ref, ob_ref, lseb_ref, a0, a1, lse_out_ref, high_ref, lse_high_ref):
    half = pl.program_id(0)

    def finish(values, lse):
        for i, ref in ((0, a0), (1, a1)):
            ref[...] = values[i].astype(BF)
        lse_out_ref[...] = lse
        for i in (0, 1):
            high_ref[i] = values[i].astype(BF)
        lse_high_ref[...] = lse

    @pl.when(f[2] == 1)
    def _():
        finish((o0[...], o1[...]), lse_ref[...])

    @pl.when(f[2] == 0)
    def _():
        low = half == 0
        lse_c = jnp.where(low, lsec_ref[...], lseb_ref[...])
        lse_l = lse_ref[...]
        top = jnp.maximum(lse_l, lse_c)
        lse = top + jnp.log2(jnp.exp2(lse_l - top) + jnp.exp2(lse_c - top))
        share_l, share_c = jnp.exp2(lse_l - lse), jnp.exp2(lse_c - lse)
        values = []
        for i, ref in ((0, o0), (1, o1)):
            other = jnp.where(low, oc_ref[i], ob_ref[i]).astype(F32)
            rows = []
            for h in range(HALF_HEADS):
                at = slice(h * HEAD_DIM, (h + 1) * HEAD_DIM)
                rows.append(
                    ref[at, :] * share_l[h, i : i + 1] + other[at] * share_c[h, i : i + 1]
                )
            values.append(jnp.concatenate(rows, 0))
        finish(values, lse)


def gradient_tile(
    q_refs, k_refs, v_refs, g_refs, o_refs, lse_ref, dq_refs, dk_acc, dv_acc, unit, at, first
):
    qp, keys = unit
    qs, ks = spans(at, first)
    q, g = q_refs[qp][:, qs], g_refs[qp][:, qs]
    lse = lse_ref[0, qp : qp + 1, qs]
    delta = jnp.sum(g.astype(F32) * o_refs[qp][:, qs].astype(F32), axis=0, keepdims=True)
    dq = None
    for kp in keys:
        k, v = k_refs[kp][:, ks], v_refs[kp][:, ks]
        weights = jnp.exp2(mask_tail(dot(k, q, 0, 0) * SCALE2) - lse)
        ds = (weights * (dot(v, g, 0, 0) - delta)).astype(BF)
        term = dot(k, ds, 1, 0)
        dq = term if dq is None else dq + term
        dk_acc[kp, :, ks] += dot(q, ds, 1, 1)
        dv_acc[kp, :, ks] += dot(g, weights.astype(BF), 1, 1)
    dq_refs[qp][:, qs] = (dq * SCALE).astype(BF)


def local_back_kernel(
    f, q0, q1, k0, k1, v0, v1, g0, g1, o0, o1, lse_ref, d0, d1, dk_acc, dv_acc
):
    dk_acc[...] = jnp.zeros_like(dk_acc)
    dv_acc[...] = jnp.zeros_like(dv_acc)
    sweep(
        f,
        q0.shape[1],
        functools.partial(
            gradient_tile,
            (q0, q1),
            (k0, k1),
            (v0, v1),
            (g0, g1),
            (o0, o1),
            lse_ref,
            (d0.at[0], d1.at[0]),
            dk_acc,
            dv_acc,
        ),
        [unit(f) for unit in LOCAL_UNITS],
    )
    for i, ref in ((0, d0), (1, d1)):
        ref[1] = (dk_acc[i] * SCALE).astype(BF)
        ref[2] = dv_acc[i].astype(BF)


def cross_back_kernel(f, *refs):
    ins, more = refs[:12], refs[12:]
    (ga0, ga1, oa, lse_a, gb0, gb1, ob0, ob1, lse_b, dq_ref, dkv_ref, dk_acc, dv_acc) = more
    dk_acc[...] = jnp.zeros_like(dk_acc)
    dv_acc[...] = jnp.zeros_like(dv_acc)
    for early, at, grads, outs, lse_ref in (
        (1, 0, (ga0, ga1), (oa.at[0], oa.at[1]), lse_a),
        (0, 6, (gb0, gb1), (ob0, ob1), lse_b),
    ):
        q0, q1, k0, k1, v0, v1 = ins[at : at + 6]
        sweep(
            f,
            q0.shape[1],
            functools.partial(
                gradient_tile,
                (q0, q1),
                (k0, k1),
                (v0, v1),
                grads,
                outs,
                lse_ref,
                (dq_ref.at[0], dq_ref.at[1]),
                dk_acc,
                dv_acc,
            ),
            [(f[2] == early, CROSS_UNITS)],
        )
    for i in (0, 1):
        dkv_ref[0, i] = (dk_acc[i] * SCALE).astype(BF)
        dkv_ref[1, i] = dv_acc[i].astype(BF)


def gelu_pair(u):
    k = math.sqrt(2 / math.pi)
    square = u * u
    t = jnp.tanh(k * u * (1.0 + 0.044715 * square))
    half = 0.5 + 0.5 * t
    slope = half + 0.5 * u * (1.0 - t * t) * (k * (1.0 + 3 * 0.044715 * square))
    return u * half, slope


def ff_tile(normed2_ref, cot_ref, wu_ref, wd_ref):
    act, slope = gelu_pair(dot(normed2_ref[...], wu_ref[...], 1, 0))
    act = act.astype(BF)
    grad_up = (dot(cot_ref[...], wd_ref[...], 1, 1) * slope).astype(BF)
    return act, grad_up, dot(act, wd_ref[...], 1, 0), dot(grad_up, wu_ref[...], 1, 1)


def feed_first_kernel(
    f, x_ref, emb_ref, a_ref, b_ref, wa_ref, wb_ref, gain_ref, cot_ref, wu_ref, wd_ref,
    res_ref, n_ref, y_ref, c_ref, dd_ref, du_ref,
):
    step = pl.program_id(0)

    @pl.when(step == 0)
    def _():
        residual = (
            hidden_of(x_ref, emb_ref)
            + dot(a_ref[...], wa_ref[...], 0, 0)
            + dot(b_ref[...], wb_ref[...], 0, 0)
        )
        res_ref[...] = residual
        center, inv = centered(residual)
        n_ref[...] = (center * inv * gain_ref[...]).astype(BF)
        y_ref[...] = residual
        c_ref[...] = jnp.zeros_like(c_ref)

    act, grad_up, y, c = ff_tile(n_ref, cot_ref, wu_ref, wd_ref)
    y_ref[...] += y
    c_ref[...] += c
    dd_ref[...] = dot(act, cot_ref[...], 0, 0).astype(BF)
    du_ref[...] = dot(n_ref[...], grad_up, 0, 0).astype(BF)


def feed_second_kernel(
    f, res_ref, n_ref, y_ref, c_ref, gain_ref, cot_ref, wu_ref, wd_ref, wa_ref, wb_ref, b_ref,
    act_ref, gup_ref, out_ref, gres_ref, gattn_ref, ga_ref, gb_ref, gah_ref, gbh_ref, dgain_ref, dwo_ref,
    y_acc, c_acc,
):
    step = pl.program_id(0)

    @pl.when(step == 0)
    def _():
        y_acc[...] = y_ref[...]
        c_acc[...] = c_ref[...]

    act, grad_up, y, c = ff_tile(n_ref, cot_ref, wu_ref, wd_ref)
    act_ref[...] = act
    gup_ref[...] = grad_up
    y_acc[...] += y
    c_acc[...] += c

    @pl.when(step == pl.num_programs(0) - 1)
    def _():
        out_ref[...] = y_acc[...].astype(BF)
        center, inv = centered(res_ref[...])
        n2 = center * inv
        c_all = c_acc[...]
        dgain_ref[...] = jnp.sum(c_all * n2, axis=0, keepdims=True)
        e = c_all * gain_ref[...]
        grad_residual = cot_ref[...].astype(F32) + inv * (
            e - jnp.mean(e, axis=-1, keepdims=True) - n2 * jnp.mean(e * n2, axis=-1, keepdims=True)
        )
        gres_ref[...] = grad_residual
        grad_attn = grad_residual.astype(BF)
        gattn_ref[...] = grad_attn
        mine = dot(wa_ref[...], grad_attn, 1, 1).astype(BF)
        theirs = dot(wb_ref[...], grad_attn, 1, 1).astype(BF)
        ga_ref[...] = mine
        gb_ref[...] = theirs
        gah_ref[...] = mine[HALF:]
        gbh_ref[...] = theirs[HALF:]
        dwo_ref[...] = dot(b_ref[...], grad_attn, 1, 0).astype(BF)


def combine_kernel(
    f, d0, d1, dqc_ref, dqb_ref, dkvc_ref, dkvb_ref, n0_ref, n1_ref, g0, g1, dw_ref
):
    part = pl.program_id(0)
    late, early = f[2] == 0, f[2] == 1

    def put(low, high):
        for i, (d, g) in enumerate(((d0, g0), (d1, g1))):
            if low is None:
                g[...] = d[0]
            else:
                g[:HALF] = (d[0, :HALF].astype(F32) + low[0, i].astype(F32)).astype(BF)
                g[HALF:] = (d[0, HALF:].astype(F32) + high[0, i].astype(F32)).astype(BF)

    @pl.when(late & (part == 0))
    def _():
        put(dqc_ref, dqb_ref)

    @pl.when(early & (part > 0))
    def _():
        put(dkvb_ref, dkvc_ref)

    @pl.when((late & (part > 0)) | (early & (part == 0)))
    def _():
        put(None, None)

    dw_ref[0] = dot(n0_ref[...], g0[...], 1, 1) + dot(n1_ref[...], g1[...], 1, 1)


def input_grad_kernel(
    f, g_ref, h_ref, wg_ref, wh_ref, x_ref, emb_ref, gain_ref, gres_ref, gin_ref, sums_ref, acc
):
    part = pl.program_id(0)
    value = dot(wg_ref[...], g_ref[...], 1, 0) + dot(wh_ref[...], h_ref[...], 1, 0)

    @pl.when(part == 0)
    def _():
        acc[...] = value

    @pl.when(part > 0)
    def _():
        acc[...] += value

    @pl.when(part == pl.num_programs(0) - 1)
    def _():
        center, inv = centered(hidden_of(x_ref, emb_ref))
        n1 = center * inv
        grad = acc[...].T
        e = grad * gain_ref[...]
        total = gres_ref[...] + inv * (
            e - jnp.mean(e, axis=-1, keepdims=True) - n1 * jnp.mean(e * n1, axis=-1, keepdims=True)
        )
        gin_ref[...] = total.astype(BF)
        sums_ref[...] = jnp.concatenate(
            [jnp.sum(total, axis=0, keepdims=True), jnp.sum(grad * n1, axis=0, keepdims=True)], 0
        )


def swap(array, step):
    axis, mask, size = step
    return lax.ppermute(array, axis, [(i, i ^ mask) for i in range(size)])


def side(step):
    axis, mask, _ = step
    return (lax.axis_index(axis) // mask) % 2


def halve(total, step):
    here, half = side(step), total.shape[0] // 2
    sent = lax.dynamic_slice_in_dim(total, (1 - here) * half, half, 0).astype(BF)
    kept = lax.dynamic_slice_in_dim(total, here * half, half, 0)
    return kept.astype(F32) + swap(sent, step).astype(F32)


def join(own, other, step, axis=0):
    return jnp.where(
        side(step) == 0,
        jnp.concatenate([own, other], axis),
        jnp.concatenate([other, own], axis),
    )


def sum_over(total, steps):
    for step in steps:
        total = halve(total, step)
    total = total.astype(BF)
    for step in reversed(steps):
        total = join(total, swap(total, step), step)
    return total


def on_device(
    sizes, block_input, segments, pass_emb, gain_attn, w_qkv, w_out, gain_mlp, w_up, w_down, cotangent
):
    passes, n_dp = sizes
    core = ("pass", 1, passes)
    cross = ("pass", 2, passes)
    lanes = [("dp", 1 << i, n_dp) for i in range(n_dp.bit_length() - 1)]
    order_a = lanes[:1] + [cross] + lanes[1:]
    order_b = lanes[1:] + lanes[:1] + [cross]
    order_c = [cross] + lanes

    pass_here = lax.axis_index("pass")
    core_here = pass_here % 2
    length = segments.shape[0]
    flags = jnp.stack(
        [
            (segments[0] == segments[length - 1]).astype(jnp.int32),
            core_here.astype(jnp.int32),
            (pass_here < 2).astype(jnp.int32),
            pass_here.astype(jnp.int32),
        ]
    )

    def to_late(array, other=0):
        return lax.ppermute(array, "pass", [(0, 2 + other), (1, 3 - other)])

    def to_early(array, other=0):
        return lax.ppermute(array, "pass", [(2, other), (3, 1 - other)])

    x, cot = block_input[0], cotangent[0]
    emb = (pass_emb.reshape(passes, 1, D), (1, 1, D), lambda i, f: (f[3], 0, 0))

    normed, theirs, low_t, high_t = call(
        norm_project_kernel,
        flags,
        (3,),
        [
            fixed(x),
            emb,
            fixed(row(gain_attn)),
            (w_qkv, (D, GROUP), lambda i, f: (0, 2 * i + 1 - f[1])),
        ],
        [out_fixed((D, length), BF)] + projection_outs(length),
        5,
        "norm_project",
    )
    other = swap(theirs, core)
    own, low_o, high_o = call(
        project_kernel,
        flags,
        (3,),
        [fixed(normed), (w_qkv, (D, GROUP), lambda i, f: (0, 2 * i + f[1]))],
        projection_outs(length),
        3,
        "project_own",
    )
    late_kv = (to_late(low_o), to_late(low_t, 1))
    early_q = (to_early(high_o), to_early(high_t, 1))
    normed_other = swap(normed, core)

    local_inputs = [head(a, at) for at in (0, 6, 12) for a in (own, other)]
    o0, o1, lse_local = call(
        local_kernel,
        flags,
        (HEADS // 2,),
        local_inputs,
        [((GROUP, length), F32, (HEAD_DIM, length), lambda h, f: (h, 0))] * 2
        + [lse_out(HEADS // 2, length)],
        14,
        "attend_local",
    )
    cross_in = cross_inputs(early_q, own, other, late_kv)
    pair_out = ((2, HALF, length), BF, (2, HEAD_DIM, length), lambda h, f: (0, h, 0))
    o_cross, lse_cross = call(
        cross_kernel,
        flags,
        (HALF_HEADS,),
        cross_in,
        [pair_out, lse_out(HALF_HEADS, length)],
        11,
        "attend_cross",
    )
    o_back, lse_back = to_late(o_cross), to_late(lse_cross)
    half_rows = (HALF, length)
    att_own, att_pair, lse, att_high, lse_high = call(
        merge_kernel,
        flags,
        (2,),
        [
            (o0, half_rows, lambda i, f: (i, 0)),
            (o1, half_rows, lambda i, f: (i, 0)),
            (lse_local, (HALF_HEADS, 2, length), lambda i, f: (i, 0, 0)),
            fixed(o_cross),
            fixed(lse_cross),
            fixed(o_back),
            fixed(lse_back),
        ],
        [((GROUP, length), BF, half_rows, lambda i, f: (i, 0))] * 2
        + [
            ((HEADS // 2, 2, length), F32, (HALF_HEADS, 2, length), lambda i, f: (i, 0, 0)),
            out_fixed((2, HALF, length), BF),
            out_fixed((HALF_HEADS, 2, length), F32),
        ],
        3,
        "merge",
    )
    att_other = swap(att_pair, core)
    att_early, lse_early = to_early(att_high), to_early(lse_high)

    w_half = [(w_out, (GROUP, D), lambda i, f: (f[1], 0)), (w_out, (GROUP, D), lambda i, f: (1 - f[1], 0))]
    ff_half = w_up.shape[1] // 2
    steps = ff_half // FF_TILE

    def ff_weights(at):
        return [
            (w_up, (D, FF_TILE), lambda i, f: (0, at(f) * steps + i)),
            (w_down, (FF_TILE, D), lambda i, f: (at(f) * steps + i, 0)),
        ]

    tokens = (length, D)
    residual, normed2, y_part, c_part, down_sent, up_sent = call(
        feed_first_kernel,
        flags,
        (steps,),
        [fixed(x), emb, fixed(att_own), fixed(att_other)]
        + w_half
        + [fixed(row(gain_mlp)), fixed(cot)]
        + ff_weights(lambda f: 1 - f[1]),
        [
            out_fixed(tokens, F32),
            out_fixed(tokens, BF),
            out_fixed(tokens, F32),
            out_fixed(tokens, F32),
            ((ff_half, D), BF, (FF_TILE, D), lambda i, f: (i, 0)),
            ((D, ff_half), BF, (D, FF_TILE), lambda i, f: (0, i)),
        ],
        16,
        "feed_first",
        56,
    )
    down_recv, up_recv = swap(down_sent, core), swap(up_sent, core)
    (
        act, grad_up, output, grad_residual, grad_attn, g_own, g_theirs, g_own_high, g_theirs_high, dgain_mlp, out_sent
    ) = call(
        feed_second_kernel,
        flags,
        (steps,),
        [fixed(a) for a in (residual, normed2, y_part, c_part, row(gain_mlp), cot)]
        + ff_weights(lambda f: f[1])
        + w_half
        + [fixed(att_other)],
        [
            ((length, ff_half), BF, (length, FF_TILE), lambda i, f: (0, i)),
            ((length, ff_half), BF, (length, FF_TILE), lambda i, f: (0, i)),
            out_fixed(tokens, BF),
            out_fixed(tokens, F32),
            out_fixed(tokens, BF),
            out_fixed((GROUP, length), BF),
            out_fixed((GROUP, length), BF),
            out_fixed(half_rows, BF),
            out_fixed(half_rows, BF),
            out_fixed((1, D), F32),
            out_fixed((GROUP, D), BF),
        ],
        16,
        "feed_second",
        56,
        [pltpu.VMEM(tokens, F32)] * 2,
    )
    g_other = swap(g_theirs, core)
    early_g = (to_early(g_own_high), to_early(g_theirs_high, 1))
    down_half = dot(act, cot, 0, 0) + down_recv.astype(F32)
    up_half = dot(normed2, grad_up, 0, 0) + up_recv.astype(F32)
    out_half = dot(att_own, grad_attn, 1, 0) + swap(out_sent, core).astype(F32)

    accumulators = [pltpu.VMEM((2, HEAD_DIM, length), F32)] * 2
    dq_cross, dkv_cross = call(
        cross_back_kernel,
        flags,
        (HALF_HEADS,),
        cross_in
        + [
            head(early_g[0], 0),
            head(early_g[1], 0),
            (att_early, (2, HEAD_DIM, length), lambda h, f: (0, h, 0)),
            lse_spec(lse_early),
            head(g_own, 0),
            head(g_other, 0),
            head(att_own, 0),
            head(att_pair, 0),
            lse_spec(lse),
        ],
        [
            pair_out,
            (
                (2, 2, HALF, length),
                BF,
                (2, 2, HEAD_DIM, length),
                lambda h, f: (0, 0, h, 0),
            ),
        ],
        16,
        "attend_back_cross",
        48,
        accumulators,
    )
    dq_back, dkv_back = to_late(dq_cross), to_early(dkv_cross)
    d_own, d_pair = call(
        local_back_kernel,
        flags,
        (HEADS // 2,),
        local_inputs
        + [head(a, 0) for a in (g_own, g_other, att_own, att_pair)]
        + [lse_spec(lse)],
        [((3, GROUP, length), BF, (3, HEAD_DIM, length), lambda h, f: (0, h, 0))] * 2,
        25,
        "attend_back_local",
        48,
        accumulators,
    )
    part_block = (1, GROUP, length)
    one_q = (1, 2, HALF, length)
    gp_own, gp_pair, dw_parts = call(
        combine_kernel,
        flags,
        (3,),
        [
            (d_own, part_block, lambda i, f: (i, 0, 0)),
            (d_pair, part_block, lambda i, f: (i, 0, 0)),
            fixed(dq_cross.reshape(one_q)),
            fixed(dq_back.reshape(one_q)),
            (dkv_cross, one_q, lambda i, f: (jnp.maximum(i - 1, 0), 0, 0, 0)),
            (dkv_back, one_q, lambda i, f: (jnp.maximum(i - 1, 0), 0, 0, 0)),
            fixed(normed),
            fixed(normed_other),
        ],
        [((3 * GROUP, length), BF, (GROUP, length), lambda i, f: (i, 0))] * 2
        + [((3, D, GROUP), F32, (1, D, GROUP), lambda i, f: (i, 0, 0))],
        6,
        "combine",
    )
    gp_other = swap(gp_pair, core)
    grad_input, sums = call(
        input_grad_kernel,
        flags,
        (3,),
        [
            (gp_own, (GROUP, length), lambda i, f: (i, 0)),
            (gp_other, (GROUP, length), lambda i, f: (i, 0)),
            (w_qkv, (D, GROUP), lambda i, f: (0, 2 * i + f[1])),
            (w_qkv, (D, GROUP), lambda i, f: (0, 2 * i + 1 - f[1])),
            fixed(x),
            emb,
            fixed(row(gain_attn)),
            fixed(grad_residual),
        ],
        [out_fixed(tokens, BF), out_fixed((2, D), F32)],
        6,
        "input_grad",
        48,
        [pltpu.VMEM((D, length), F32)],
    )
    selector = (jnp.arange(passes) == pass_here).astype(F32)
    small = jnp.concatenate([selector[:, None] * sums[:1], sums[1:], dgain_mlp])
    for step in [core, cross] + lanes:
        small = small + swap(small, step)

    def whole(half, steps, axis=0):
        half = sum_over(half, steps)
        return join(half, swap(half, core), core, axis).astype(F32)

    down_total = whole(down_half, order_a)
    up_total = whole(up_half, order_b, 1)
    out_total = whole(out_half, order_c)
    qkv_total = jnp.concatenate(
        [whole(dw_parts[i], order, 1) for i, order in enumerate((order_a, order_b, order_c))],
        axis=1,
    )
    return (
        output[None],
        grad_input[None],
        small[:passes],
        small[passes],
        qkv_total,
        out_total,
        small[passes + 1],
        up_total,
        down_total,
    )


def solution(mesh):
    sizes = (mesh.shape["pass"], mesh.shape["dp"])
    tokens = P("pass", "dp", None)
    in_specs = (tokens, P("dp")) + (P(),) * 7 + (tokens,)
    out_specs = (tokens, tokens) + (P(),) * 7
    return jax.shard_map(
        functools.partial(on_device, sizes),
        mesh=mesh,
        in_specs=in_specs,
        out_specs=out_specs,
        check_vma=False,
    )
```

```python
import functools
import math

import jax
import jax.numpy as jnp
from jax import lax
from jax.experimental import pallas as pl
from jax.experimental.pallas import tpu as pltpu
from jax.sharding import PartitionSpec as P

D = 768
HEADS = 12
HEAD_DIM = 64
SHORT = 256
FF_TILE = 512
GROUP = D // 2
HALF = GROUP // 2
HALF_HEADS = HEADS // 4
EPS = 1e-05
SCALE = HEAD_DIM**-0.5
SCALE2 = SCALE * math.log2(math.e)
BF = jnp.bfloat16
F32 = jnp.float32


def dot(a, b, ca, cb):
    return lax.dot_general(a, b, (((ca,), (cb,)), ((), ())), preferred_element_type=F32)


def cost(us):
    return pl.CostEstimate(flops=int(us * 1.1e9), bytes_accessed=1 << 20, transcendentals=0)


def params(mib):
    return pltpu.CompilerParams(vmem_limit_bytes=mib << 20)


def call(kernel, flags, grid, ins, outs, us, name, mib=48, scratch=()):
    return pl.pallas_call(
        kernel,
        grid_spec=pltpu.PrefetchScalarGridSpec(
            num_scalar_prefetch=1,
            grid=grid,
            in_specs=[pl.BlockSpec(block, index) for _, block, index in ins],
            out_specs=[pl.BlockSpec(block, index) for _, _, block, index in outs],
            scratch_shapes=list(scratch),
        ),
        out_shape=[jax.ShapeDtypeStruct(shape, dtype) for shape, dtype, _, _ in outs],
        cost_estimate=cost(us),
        compiler_params=params(mib),
        name=name,
    )(flags, *[array for array, _, _ in ins])


def fixed(array):
    return (array, array.shape, lambda i, f: (0,) * array.ndim)


def out_fixed(shape, dtype):
    return (shape, dtype, shape, lambda i, f: (0,) * len(shape))


def row(vector):
    return vector.reshape(1, -1)


def one_sequence(f):
    return f[0] == 1


def hidden_of(x_ref, emb_ref):
    return x_ref[...].astype(F32) + emb_ref[0]


def centered(values):
    center = values - jnp.mean(values, axis=-1, keepdims=True)
    return center, lax.rsqrt(jnp.mean(center * center, axis=-1, keepdims=True) + EPS)


def write_part(part, out_ref, low_ref, high_ref, value):
    out_ref[...] = value

    @pl.when(part == 0)
    def _():
        high_ref[...] = value[HALF:]

    @pl.when(part > 0)
    def _():
        low_ref[pl.ds(pl.multiple_of((part - 1) * HALF, HALF), HALF), :] = value[:HALF]


def norm_project_kernel(f, x_ref, emb_ref, gain_ref, w_ref, normed_ref, out_ref, low_ref, high_ref):
    part = pl.program_id(0)

    @pl.when(part == 0)
    def _():
        center, inv = centered(hidden_of(x_ref, emb_ref))
        normed_ref[...] = (center * inv * gain_ref[...]).T.astype(BF)

    value = dot(w_ref[...], normed_ref[...], 0, 0).astype(BF)
    write_part(part, out_ref, low_ref, high_ref, value)


def project_kernel(f, normed_ref, w_ref, out_ref, low_ref, high_ref):
    value = dot(w_ref[...], normed_ref[...], 0, 0).astype(BF)
    write_part(pl.program_id(0), out_ref, low_ref, high_ref, value)


def projection_outs(length):
    return [
        ((3 * GROUP, length), BF, (GROUP, length), lambda i, f: (i, 0)),
        out_fixed((2 * HALF, length), BF),
        out_fixed((HALF, length), BF),
    ]


def mask_tail(scores):
    n = scores.shape[0]
    key = lax.broadcasted_iota(jnp.int32, (SHORT, SHORT), 0)
    query = lax.broadcasted_iota(jnp.int32, (SHORT, SHORT), 1)
    diag = jnp.where(key <= query, scores[n - SHORT :], -1e30)
    return diag if n == SHORT else jnp.concatenate([scores[: n - SHORT], diag], 0)


def sweep(f, length, tile, variants):
    for condition, units in variants:
        for whole in (True, False):

            @pl.when(condition & (one_sequence(f) == whole))
            def _():
                for at in range(length // SHORT):
                    for unit in units:
                        tile(unit, at, 0 if whole else at)


def spans(at, first):
    return slice(at * SHORT, (at + 1) * SHORT), slice(first * SHORT, (at + 1) * SHORT)


def softmax_tile(q_refs, k_refs, v_refs, o_refs, lse_ref, unit, at, first):
    qp, keys = unit
    qs, ks = spans(at, first)
    q = q_refs[qp][:, qs]
    scores = [mask_tail(dot(k_refs[kp][:, ks], q, 0, 0) * SCALE2) for kp in keys]
    top = functools.reduce(jnp.maximum, [jnp.max(s, axis=0, keepdims=True) for s in scores])
    raw = [jnp.exp2(s - top) for s in scores]
    total = functools.reduce(jnp.add, [jnp.sum(p, axis=0, keepdims=True) for p in raw])
    out = functools.reduce(
        jnp.add, [dot(v_refs[kp][:, ks], p.astype(BF), 1, 0) for kp, p in zip(keys, raw)]
    )
    o_refs[qp][:, qs] = (out * (1.0 / total)).astype(o_refs[qp].dtype)
    lse_ref[0, qp : qp + 1, qs] = top + jnp.log2(total)


LOCAL_UNITS = (
    lambda f: (f[1] == 0, [(0, [0]), (1, [0, 1])]),
    lambda f: (f[1] == 1, [(1, [1]), (0, [0, 1])]),
)
CROSS_UNITS = [(0, [0, 1]), (1, [0, 1])]


def local_kernel(f, q0, q1, k0, k1, v0, v1, o0, o1, lse_ref):
    sweep(
        f,
        q0.shape[1],
        functools.partial(softmax_tile, (q0, q1), (k0, k1), (v0, v1), (o0, o1), lse_ref),
        [unit(f) for unit in LOCAL_UNITS],
    )


def cross_kernel(f, *refs):
    ins, (o_ref, lse_ref) = refs[:12], refs[12:]
    outs = (o_ref.at[0], o_ref.at[1])
    for early, at in ((1, 0), (0, 6)):
        q0, q1, k0, k1, v0, v1 = ins[at : at + 6]
        sweep(
            f,
            q0.shape[1],
            functools.partial(softmax_tile, (q0, q1), (k0, k1), (v0, v1), outs, lse_ref),
            [(f[2] == early, CROSS_UNITS)],
        )


def head(array, at):
    return (array, (HEAD_DIM, array.shape[-1]), lambda h, f: (at + h, 0))


def lse_spec(array):
    return (array, (1,) + array.shape[1:], lambda h, f: (h, 0, 0))


def lse_out(heads, length):
    return ((heads, 2, length), F32, (1, 2, length), lambda h, f: (h, 0, 0))


def cross_inputs(early_q, own, other, late_kv):
    return [
        head(early_q[0], 0),
        head(early_q[1], 0),
        head(own, 6 + HALF_HEADS),
        head(other, 6 + HALF_HEADS),
        head(own, 12 + HALF_HEADS),
        head(other, 12 + HALF_HEADS),
        head(own, 0),
        head(other, 0),
        head(late_kv[0], 0),
        head(late_kv[1], 0),
        head(late_kv[0], HALF_HEADS),
        head(late_kv[1], HALF_HEADS),
    ]


def merge_kernel(f, o0, o1, lse_ref, oc_ref, lsec_ref, ob_ref, lseb_ref, a0, a1, lse_out_ref, high_ref, lse_high_ref):
    half = pl.program_id(0)

    def finish(values, lse):
        for i, ref in ((0, a0), (1, a1)):
            ref[...] = values[i].astype(BF)
        lse_out_ref[...] = lse
        for i in (0, 1):
            high_ref[i] = values[i].astype(BF)
        lse_high_ref[...] = lse

    @pl.when(f[2] == 1)
    def _():
        finish((o0[...], o1[...]), lse_ref[...])

    @pl.when(f[2] == 0)
    def _():
        low = half == 0
        lse_c = jnp.where(low, lsec_ref[...], lseb_ref[...])
        lse_l = lse_ref[...]
        top = jnp.maximum(lse_l, lse_c)
        lse = top + jnp.log2(jnp.exp2(lse_l - top) + jnp.exp2(lse_c - top))
        share_l, share_c = jnp.exp2(lse_l - lse), jnp.exp2(lse_c - lse)
        values = []
        for i, ref in ((0, o0), (1, o1)):
            other = jnp.where(low, oc_ref[i], ob_ref[i]).astype(F32)
            rows = []
            for h in range(HALF_HEADS):
                at = slice(h * HEAD_DIM, (h + 1) * HEAD_DIM)
                rows.append(
                    ref[at, :] * share_l[h, i : i + 1] + other[at] * share_c[h, i : i + 1]
                )
            values.append(jnp.concatenate(rows, 0))
        finish(values, lse)


def gradient_tile(
    q_refs, k_refs, v_refs, g_refs, o_refs, lse_ref, dq_refs, dk_acc, dv_acc, unit, at, first
):
    qp, keys = unit
    qs, ks = spans(at, first)
    q, g = q_refs[qp][:, qs], g_refs[qp][:, qs]
    lse = lse_ref[0, qp : qp + 1, qs]
    delta = jnp.sum(g.astype(F32) * o_refs[qp][:, qs].astype(F32), axis=0, keepdims=True)
    dq = None
    for kp in keys:
        k, v = k_refs[kp][:, ks], v_refs[kp][:, ks]
        weights = jnp.exp2(mask_tail(dot(k, q, 0, 0) * SCALE2) - lse)
        ds = (weights * (dot(v, g, 0, 0) - delta)).astype(BF)
        term = dot(k, ds, 1, 0)
        dq = term if dq is None else dq + term
        dk_acc[kp, :, ks] += dot(q, ds, 1, 1)
        dv_acc[kp, :, ks] += dot(g, weights.astype(BF), 1, 1)
    dq_refs[qp][:, qs] = (dq * SCALE).astype(BF)


def local_back_kernel(
    f, q0, q1, k0, k1, v0, v1, g0, g1, o0, o1, lse_ref, d0, d1, dk_acc, dv_acc
):
    dk_acc[...] = jnp.zeros_like(dk_acc)
    dv_acc[...] = jnp.zeros_like(dv_acc)
    sweep(
        f,
        q0.shape[1],
        functools.partial(
            gradient_tile,
            (q0, q1),
            (k0, k1),
            (v0, v1),
            (g0, g1),
            (o0, o1),
            lse_ref,
            (d0.at[0], d1.at[0]),
            dk_acc,
            dv_acc,
        ),
        [unit(f) for unit in LOCAL_UNITS],
    )
    for i, ref in ((0, d0), (1, d1)):
        ref[1] = (dk_acc[i] * SCALE).astype(BF)
        ref[2] = dv_acc[i].astype(BF)


def cross_back_kernel(f, *refs):
    ins, more = refs[:12], refs[12:]
    (ga0, ga1, oa, lse_a, gb0, gb1, ob0, ob1, lse_b, dq_ref, dkv_ref, dk_acc, dv_acc) = more
    dk_acc[...] = jnp.zeros_like(dk_acc)
    dv_acc[...] = jnp.zeros_like(dv_acc)
    for early, at, grads, outs, lse_ref in (
        (1, 0, (ga0, ga1), (oa.at[0], oa.at[1]), lse_a),
        (0, 6, (gb0, gb1), (ob0, ob1), lse_b),
    ):
        q0, q1, k0, k1, v0, v1 = ins[at : at + 6]
        sweep(
            f,
            q0.shape[1],
            functools.partial(
                gradient_tile,
                (q0, q1),
                (k0, k1),
                (v0, v1),
                grads,
                outs,
                lse_ref,
                (dq_ref.at[0], dq_ref.at[1]),
                dk_acc,
                dv_acc,
            ),
            [(f[2] == early, CROSS_UNITS)],
        )
    for i in (0, 1):
        dkv_ref[0, i] = (dk_acc[i] * SCALE).astype(BF)
        dkv_ref[1, i] = dv_acc[i].astype(BF)


def gelu_pair(u):
    k = math.sqrt(2 / math.pi)
    square = u * u
    t = jnp.tanh(k * u * (1.0 + 0.044715 * square))
    half = 0.5 + 0.5 * t
    slope = half + 0.5 * u * (1.0 - t * t) * (k * (1.0 + 3 * 0.044715 * square))
    return u * half, slope


def ff_tile(normed2_ref, cot_ref, wu_ref, wd_ref):
    act, slope = gelu_pair(dot(normed2_ref[...], wu_ref[...], 1, 0))
    act = act.astype(BF)
    grad_up = (dot(cot_ref[...], wd_ref[...], 1, 1) * slope).astype(BF)
    return act, grad_up, dot(act, wd_ref[...], 1, 0), dot(grad_up, wu_ref[...], 1, 1)


def feed_first_kernel(
    f, x_ref, emb_ref, a_ref, b_ref, wa_ref, wb_ref, gain_ref, cot_ref, wu_ref, wd_ref,
    res_ref, n_ref, y_ref, c_ref, dd_ref, du_ref,
):
    step = pl.program_id(0)

    @pl.when(step == 0)
    def _():
        residual = (
            hidden_of(x_ref, emb_ref)
            + dot(a_ref[...], wa_ref[...], 0, 0)
            + dot(b_ref[...], wb_ref[...], 0, 0)
        )
        res_ref[...] = residual
        center, inv = centered(residual)
        n_ref[...] = (center * inv * gain_ref[...]).astype(BF)
        y_ref[...] = residual
        c_ref[...] = jnp.zeros_like(c_ref)

    act, grad_up, y, c = ff_tile(n_ref, cot_ref, wu_ref, wd_ref)
    y_ref[...] += y
    c_ref[...] += c
    dd_ref[...] = dot(act, cot_ref[...], 0, 0).astype(BF)
    du_ref[...] = dot(n_ref[...], grad_up, 0, 0).astype(BF)


def feed_second_kernel(
    f, res_ref, n_ref, y_ref, c_ref, gain_ref, cot_ref, wu_ref, wd_ref, wa_ref, wb_ref, b_ref,
    act_ref, gup_ref, out_ref, gres_ref, gattn_ref, ga_ref, gb_ref, gah_ref, gbh_ref, dgain_ref, dwo_ref,
    y_acc, c_acc,
):
    step = pl.program_id(0)

    @pl.when(step == 0)
    def _():
        y_acc[...] = y_ref[...]
        c_acc[...] = c_ref[...]

    act, grad_up, y, c = ff_tile(n_ref, cot_ref, wu_ref, wd_ref)
    act_ref[...] = act
    gup_ref[...] = grad_up
    y_acc[...] += y
    c_acc[...] += c

    @pl.when(step == pl.num_programs(0) - 1)
    def _():
        out_ref[...] = y_acc[...].astype(BF)
        center, inv = centered(res_ref[...])
        n2 = center * inv
        c_all = c_acc[...]
        dgain_ref[...] = jnp.sum(c_all * n2, axis=0, keepdims=True)
        e = c_all * gain_ref[...]
        grad_residual = cot_ref[...].astype(F32) + inv * (
            e - jnp.mean(e, axis=-1, keepdims=True) - n2 * jnp.mean(e * n2, axis=-1, keepdims=True)
        )
        gres_ref[...] = grad_residual
        grad_attn = grad_residual.astype(BF)
        gattn_ref[...] = grad_attn
        mine = dot(wa_ref[...], grad_attn, 1, 1).astype(BF)
        theirs = dot(wb_ref[...], grad_attn, 1, 1).astype(BF)
        ga_ref[...] = mine
        gb_ref[...] = theirs
        gah_ref[...] = mine[HALF:]
        gbh_ref[...] = theirs[HALF:]
        dwo_ref[...] = dot(b_ref[...], grad_attn, 1, 0).astype(BF)


def combine_kernel(
    f, dl0, dl1, dh0, dh1, dqc_ref, dqb_ref, dkvc_ref, dkvb_ref, n0_ref, n1_ref, g0, g1, dw_ref
):
    part = pl.program_id(0)
    late, early = f[2] == 0, f[2] == 1

    def put(low, high):
        for i, (dl, dh, g) in enumerate(((dl0, dh0, g0), (dl1, dh1, g1))):
            if low is None:
                g[:HALF] = dl[0]
                g[HALF:] = dh[0]
            else:
                g[:HALF] = (dl[0].astype(F32) + low[0, i].astype(F32)).astype(BF)
                g[HALF:] = (dh[0].astype(F32) + high[0, i].astype(F32)).astype(BF)

    @pl.when(late & (part == 0))
    def _():
        put(dqc_ref, dqb_ref)

    @pl.when(early & (part > 0))
    def _():
        put(dkvb_ref, dkvc_ref)

    @pl.when((late & (part > 0)) | (early & (part == 0)))
    def _():
        put(None, None)

    dw_ref[0] = (dot(n0_ref[...], g0[...], 1, 1) + dot(n1_ref[...], g1[...], 1, 1)).astype(BF)


def input_grad_kernel(
    f, g_ref, h_ref, wg_ref, wh_ref, x_ref, emb_ref, gain_ref, gres_ref, gin_ref, sums_ref, acc
):
    part = pl.program_id(0)
    value = dot(wg_ref[...], g_ref[...], 1, 0) + dot(wh_ref[...], h_ref[...], 1, 0)

    @pl.when(part == 0)
    def _():
        acc[...] = value

    @pl.when(part > 0)
    def _():
        acc[...] += value

    @pl.when(part == pl.num_programs(0) - 1)
    def _():
        center, inv = centered(hidden_of(x_ref, emb_ref))
        n1 = center * inv
        grad = acc[...].T
        e = grad * gain_ref[...]
        total = gres_ref[...] + inv * (
            e - jnp.mean(e, axis=-1, keepdims=True) - n1 * jnp.mean(e * n1, axis=-1, keepdims=True)
        )
        gin_ref[...] = total.astype(BF)
        sums_ref[...] = jnp.concatenate(
            [jnp.sum(total, axis=0, keepdims=True), jnp.sum(grad * n1, axis=0, keepdims=True)], 0
        )


def swap(array, step):
    axis, mask, size = step
    return lax.ppermute(array, axis, [(i, i ^ mask) for i in range(size)])


def side(step):
    axis, mask, _ = step
    return (lax.axis_index(axis) // mask) % 2


def join(own, other, step, axis=0):
    return jnp.where(
        side(step) == 0,
        jnp.concatenate([own, other], axis),
        jnp.concatenate([other, own], axis),
    )


def tie(*groups):
    leaves, tree = jax.tree.flatten(groups)
    return jax.tree.unflatten(tree, lax.optimization_barrier(leaves))


class Chain:
    def __init__(self, total, steps):
        self.total, self.halving, self.joining = total, list(steps), list(reversed(steps))

    def load(self):
        if self.halving:
            step, half = self.halving[0], self.total.shape[0] // 2
            here = side(step)
            self.kept = lax.dynamic_slice_in_dim(self.total, here * half, half, 0)
            self.out = lax.dynamic_slice_in_dim(self.total, (1 - here) * half, half, 0).astype(BF)
        else:
            self.out = self.total
        return self.out

    def send(self, out):
        self.came = swap(out, (self.halving or self.joining)[0])

    def land(self):
        if self.halving:
            self.halving.pop(0)
            self.total = (self.kept.astype(F32) + self.came.astype(F32)).astype(BF)
        else:
            self.total = join(self.total, self.came, self.joining.pop(0))


def on_device(
    sizes, block_input, segments, pass_emb, gain_attn, w_qkv, w_out, gain_mlp, w_up, w_down, cotangent
):
    passes, n_dp = sizes
    core = ("pass", 1, passes)
    cross = ("pass", 2, passes)
    lanes = [("dp", 1 << i, n_dp) for i in range(n_dp.bit_length() - 1)]
    ring = [cross] + lanes
    orders = [ring, ring[1:] + ring[:1], ring[2:] + ring[:2]]

    pass_here = lax.axis_index("pass")
    core_here = pass_here % 2
    length = segments.shape[0]
    flags = jnp.stack(
        [
            (segments[0] == segments[length - 1]).astype(jnp.int32),
            core_here.astype(jnp.int32),
            (pass_here < 2).astype(jnp.int32),
            pass_here.astype(jnp.int32),
        ]
    )

    def to_late(array, other=0):
        return lax.ppermute(array, "pass", [(0, 2 + other), (1, 3 - other)])

    def to_early(array, other=0):
        return lax.ppermute(array, "pass", [(2, other), (3, 1 - other)])

    x, cot = block_input[0], cotangent[0]
    emb = (pass_emb.reshape(passes, 1, D), (1, 1, D), lambda i, f: (f[3], 0, 0))

    normed, theirs, low_t, high_t = call(
        norm_project_kernel,
        flags,
        (3,),
        [
            fixed(x),
            emb,
            fixed(row(gain_attn)),
            (w_qkv, (D, GROUP), lambda i, f: (0, 2 * i + 1 - f[1])),
        ],
        [out_fixed((D, length), BF)] + projection_outs(length),
        5,
        "norm_project",
    )
    other = swap(theirs, core)
    own, low_o, high_o = call(
        project_kernel,
        flags,
        (3,),
        [fixed(normed), (w_qkv, (D, GROUP), lambda i, f: (0, 2 * i + f[1]))],
        projection_outs(length),
        3,
        "project_own",
    )
    late_kv = (to_late(low_o), to_late(low_t, 1))
    early_q = (to_early(high_o), to_early(high_t, 1))
    normed_other = swap(normed, core)

    local_inputs = [head(a, at) for at in (0, 6, 12) for a in (own, other)]
    o0, o1, lse_local = call(
        local_kernel,
        flags,
        (HEADS // 2,),
        local_inputs,
        [((GROUP, length), F32, (HEAD_DIM, length), lambda h, f: (h, 0))] * 2
        + [lse_out(HEADS // 2, length)],
        14,
        "attend_local",
    )
    cross_in = cross_inputs(early_q, own, other, late_kv)
    pair_out = ((2, HALF, length), BF, (2, HEAD_DIM, length), lambda h, f: (0, h, 0))
    o_cross, lse_cross = call(
        cross_kernel,
        flags,
        (HALF_HEADS,),
        cross_in,
        [pair_out, lse_out(HALF_HEADS, length)],
        11,
        "attend_cross",
    )
    o_back, lse_back = to_late(o_cross), to_late(lse_cross)
    half_rows = (HALF, length)
    att_own, att_pair, lse, att_high, lse_high = call(
        merge_kernel,
        flags,
        (2,),
        [
            (o0, half_rows, lambda i, f: (i, 0)),
            (o1, half_rows, lambda i, f: (i, 0)),
            (lse_local, (HALF_HEADS, 2, length), lambda i, f: (i, 0, 0)),
            fixed(o_cross),
            fixed(lse_cross),
            fixed(o_back),
            fixed(lse_back),
        ],
        [((GROUP, length), BF, half_rows, lambda i, f: (i, 0))] * 2
        + [
            ((HEADS // 2, 2, length), F32, (HALF_HEADS, 2, length), lambda i, f: (i, 0, 0)),
            out_fixed((2, HALF, length), BF),
            out_fixed((HALF_HEADS, 2, length), F32),
        ],
        3,
        "merge",
    )
    att_other = swap(att_pair, core)
    att_early, lse_early = to_early(att_high), to_early(lse_high)

    w_half = [(w_out, (GROUP, D), lambda i, f: (f[1], 0)), (w_out, (GROUP, D), lambda i, f: (1 - f[1], 0))]
    ff_half = w_up.shape[1] // 2
    steps = ff_half // FF_TILE

    def ff_weights(at):
        return [
            (w_up, (D, FF_TILE), lambda i, f: (0, at(f) * steps + i)),
            (w_down, (FF_TILE, D), lambda i, f: (at(f) * steps + i, 0)),
        ]

    tokens = (length, D)
    residual, normed2, y_part, c_part, down_sent, up_sent = call(
        feed_first_kernel,
        flags,
        (steps,),
        [fixed(x), emb, fixed(att_own), fixed(att_other)]
        + w_half
        + [fixed(row(gain_mlp)), fixed(cot)]
        + ff_weights(lambda f: 1 - f[1]),
        [
            out_fixed(tokens, F32),
            out_fixed(tokens, BF),
            out_fixed(tokens, F32),
            out_fixed(tokens, F32),
            ((ff_half, D), BF, (FF_TILE, D), lambda i, f: (i, 0)),
            ((D, ff_half), BF, (D, FF_TILE), lambda i, f: (0, i)),
        ],
        16,
        "feed_first",
        56,
    )
    down_recv, up_recv = swap(down_sent, core), swap(up_sent, core)
    (
        act, grad_up, output, grad_residual, grad_attn, g_own, g_theirs, g_own_high, g_theirs_high, dgain_mlp, out_sent
    ) = call(
        feed_second_kernel,
        flags,
        (steps,),
        [fixed(a) for a in (residual, normed2, y_part, c_part, row(gain_mlp), cot)]
        + ff_weights(lambda f: f[1])
        + w_half
        + [fixed(att_other)],
        [
            ((length, ff_half), BF, (length, FF_TILE), lambda i, f: (0, i)),
            ((length, ff_half), BF, (length, FF_TILE), lambda i, f: (0, i)),
            out_fixed(tokens, BF),
            out_fixed(tokens, F32),
            out_fixed(tokens, BF),
            out_fixed((GROUP, length), BF),
            out_fixed((GROUP, length), BF),
            out_fixed(half_rows, BF),
            out_fixed(half_rows, BF),
            out_fixed((1, D), F32),
            out_fixed((GROUP, D), BF),
        ],
        16,
        "feed_second",
        56,
        [pltpu.VMEM(tokens, F32)] * 2,
    )
    g_other = swap(g_theirs, core)
    early_g = (to_early(g_own_high), to_early(g_theirs_high, 1))
    out_recv = swap(out_sent, core)
    down_half = (dot(act, cot, 0, 0) + down_recv.astype(F32)).astype(BF)
    up_half = (dot(normed2, grad_up, 0, 0) + up_recv.astype(F32)).astype(BF)
    out_half = (dot(att_own, grad_attn, 1, 0) + out_recv.astype(F32)).astype(BF)
    cut = ff_half - GROUP
    first = [
        Chain(down_half[:cut], orders[0]),
        Chain(up_half[:, :cut], orders[1]),
        Chain(
            jnp.concatenate(
                [
                    down_half[cut:],
                    out_half,
                    jnp.concatenate([up_half[:GROUP, cut:], up_half[GROUP:, cut:]], 1),
                ]
            ),
            orders[2],
        ),
    ]
    second = []

    def stage(chains, *more):
        loads, more = tie([c.load() for c in chains], more)
        for c, load in zip(chains, loads, strict=True):
            c.send(load)
        return more

    def land(chains):
        for c in chains:
            c.land()

    accumulators = [pltpu.VMEM((2, HEAD_DIM, length), F32)] * 2

    def local_back(at, g0, g1):
        return call(
            local_back_kernel,
            flags,
            (HALF_HEADS,),
            [head(a, base + at) for base in (0, 6, 12) for a in (own, other)]
            + [head(a, at) for a in (g0, g1, att_own, att_pair)]
            + [(lse, (1, 2, length), lambda h, f: (at + h, 0, 0))],
            [((3, HALF, length), BF, (3, HEAD_DIM, length), lambda h, f: (0, h, 0))] * 2,
            12,
            "attend_back_local",
            48,
            accumulators,
        )

    (g_own_1, g_other_1) = stage(first, g_own, g_other)
    d_low = local_back(0, g_own_1, g_other_1)
    d_low, early_g = tie(d_low, early_g)
    dq_cross, dkv_cross = call(
        cross_back_kernel,
        flags,
        (HALF_HEADS,),
        cross_in
        + [
            head(early_g[0], 0),
            head(early_g[1], 0),
            (att_early, (2, HEAD_DIM, length), lambda h, f: (0, h, 0)),
            lse_spec(lse_early),
            head(g_own_1, 0),
            head(g_other_1, 0),
            head(att_own, 0),
            head(att_pair, 0),
            lse_spec(lse),
        ],
        [
            pair_out,
            (
                (2, 2, HALF, length),
                BF,
                (2, 2, HEAD_DIM, length),
                lambda h, f: (0, 0, h, 0),
            ),
        ],
        16,
        "attend_back_cross",
        48,
        accumulators,
    )
    land(first)
    (dq_cross, dkv_cross, g_own_2, g_other_2) = stage(
        first, dq_cross, dkv_cross, g_own_1, g_other_1
    )
    dq_back, dkv_back = to_late(dq_cross), to_early(dkv_cross)
    d_high = local_back(HALF_HEADS, g_own_2, g_other_2)
    land(first)
    (d_high, dq_back, dkv_back) = stage(first, d_high, dq_back, dkv_back)
    part_block = (1, HALF, length)
    one_q = (1, 2, HALF, length)
    gp_own, gp_pair, dw_parts = call(
        combine_kernel,
        flags,
        (3,),
        [(d, part_block, lambda i, f: (i, 0, 0)) for d in (*d_low, *d_high)]
        + [
            fixed(dq_cross.reshape(one_q)),
            fixed(dq_back.reshape(one_q)),
            (dkv_cross, one_q, lambda i, f: (jnp.maximum(i - 1, 0), 0, 0, 0)),
            (dkv_back, one_q, lambda i, f: (jnp.maximum(i - 1, 0), 0, 0, 0)),
            fixed(normed),
            fixed(normed_other),
        ],
        [((3 * GROUP, length), BF, (GROUP, length), lambda i, f: (i, 0))] * 2
        + [((3, D, GROUP), BF, (1, D, GROUP), lambda i, f: (i, 0, 0))],
        6,
        "combine",
    )
    second = [Chain(dw_parts[i], order) for i, order in enumerate(orders)]
    land(first)
    (gp_pair,) = stage(first + second, gp_pair)
    gp_other = swap(gp_pair, core)
    land(first + second)
    (gp_own, gp_other) = stage(first + second, gp_own, gp_other)
    grad_input, sums = call(
        input_grad_kernel,
        flags,
        (3,),
        [
            (gp_own, (GROUP, length), lambda i, f: (i, 0)),
            (gp_other, (GROUP, length), lambda i, f: (i, 0)),
            (w_qkv, (D, GROUP), lambda i, f: (0, 2 * i + f[1])),
            (w_qkv, (D, GROUP), lambda i, f: (0, 2 * i + 1 - f[1])),
            fixed(x),
            emb,
            fixed(row(gain_attn)),
            fixed(grad_residual),
        ],
        [out_fixed(tokens, BF), out_fixed((2, D), F32)],
        6,
        "input_grad",
        48,
        [pltpu.VMEM((D, length), F32)],
    )
    selector = (jnp.arange(passes) == pass_here).astype(F32)
    small = jnp.concatenate([selector[:, None] * sums[:1], sums[1:], dgain_mlp])
    rounds = [core, cross] + lanes
    while first[0].joining or second[0].joining:
        active = [c for c in first + second if c.halving or c.joining]
        land(active)
        active = [c for c in first + second if c.halving or c.joining]
        (small,) = stage(active, small)
        if rounds:
            small = small + swap(small, rounds.pop(0))
    for step in rounds:
        small = small + swap(small, step)

    def both(half, axis=0):
        return join(half, swap(half, core), core, axis).astype(F32)

    down_1, up_1, mixed = [c.total for c in first]
    up_2 = jnp.concatenate([mixed[2 * GROUP :, :GROUP], mixed[2 * GROUP :, GROUP:]])
    down_total = both(jnp.concatenate([down_1, mixed[:GROUP]]))
    out_total = both(mixed[GROUP : 2 * GROUP])
    up_total = both(jnp.concatenate([up_1, up_2], 1), 1)
    qkv_total = jnp.concatenate([both(c.total, 1) for c in second], axis=1)
    return (
        output[None],
        grad_input[None],
        small[:passes],
        small[passes],
        qkv_total,
        out_total,
        small[passes + 1],
        up_total,
        down_total,
    )


def solution(mesh):
    sizes = (mesh.shape["pass"], mesh.shape["dp"])
    tokens = P("pass", "dp", None)
    in_specs = (tokens, P("dp")) + (P(),) * 7 + (tokens,)
    out_specs = (tokens, tokens) + (P(),) * 7
    return jax.shard_map(
        functools.partial(on_device, sizes),
        mesh=mesh,
        in_specs=in_specs,
        out_specs=out_specs,
        check_vma=False,
    )
```

```python
import functools
import math

import jax
import jax.numpy as jnp
from jax import lax
from jax.experimental import pallas as pl
from jax.experimental.pallas import tpu as pltpu
from jax.sharding import PartitionSpec as P

D = 768
HEADS = 12
HEAD_DIM = 64
SHORT = 256
FF_TILE = 512
GROUP = D // 2
HALF = GROUP // 2
HALF_HEADS = HEADS // 4
EPS = 1e-05
SCALE = HEAD_DIM**-0.5
SCALE2 = SCALE * math.log2(math.e)
BF = jnp.bfloat16
F32 = jnp.float32
BRIEF = 0.2


def dot(a, b, ca, cb):
    return lax.dot_general(a, b, (((ca,), (cb,)), ((), ())), preferred_element_type=F32)


def cost(us):
    return pl.CostEstimate(flops=int(us * 1.1e9), bytes_accessed=1 << 20, transcendentals=0)


def call(kernel, flags, grid, ins, outs, us, name, scratch=(), temporaries=8):
    blocks = [(math.prod(block), array.dtype) for array, block, _ in ins]
    blocks += [(math.prod(block), dtype) for _, dtype, block, _ in outs]
    blocks += [(math.prod(buffer.shape) // 2, buffer.dtype) for buffer in scratch]
    limit = sum(2 * n * jnp.dtype(dtype).itemsize for n, dtype in blocks) + (temporaries << 20)
    return pl.pallas_call(
        kernel,
        grid_spec=pltpu.PrefetchScalarGridSpec(
            num_scalar_prefetch=1,
            grid=grid,
            in_specs=[pl.BlockSpec(block, index) for _, block, index in ins],
            out_specs=[pl.BlockSpec(block, index) for _, _, block, index in outs],
            scratch_shapes=list(scratch),
        ),
        out_shape=[jax.ShapeDtypeStruct(shape, dtype) for shape, dtype, _, _ in outs],
        cost_estimate=cost(us),
        compiler_params=pltpu.CompilerParams(vmem_limit_bytes=min(limit, 60 << 20)),
        name=name,
    )(flags, *[array for array, _, _ in ins])


def fixed(array):
    return (array, array.shape, lambda i, f: (0,) * array.ndim)


def out_fixed(shape, dtype):
    return (shape, dtype, shape, lambda i, f: (0,) * len(shape))


def row(vector):
    return vector.reshape(1, -1)


def one_sequence(f):
    return f[0] == 1


def hidden_of(x_ref, emb_ref):
    return x_ref[...].astype(F32) + emb_ref[0]


def centered(values):
    center = values - jnp.mean(values, axis=-1, keepdims=True)
    return center, lax.rsqrt(jnp.mean(center * center, axis=-1, keepdims=True) + EPS)


def write_part(part, out_ref, low_ref, high_ref, value):
    out_ref[...] = value

    @pl.when(part == 0)
    def _():
        high_ref[...] = value[HALF:]

    @pl.when(part > 0)
    def _():
        low_ref[pl.ds(pl.multiple_of((part - 1) * HALF, HALF), HALF), :] = value[:HALF]


def norm_project_kernel(f, x_ref, emb_ref, gain_ref, w_ref, normed_ref, out_ref, low_ref, high_ref):
    part = pl.program_id(0)

    @pl.when(part == 0)
    def _():
        center, inv = centered(hidden_of(x_ref, emb_ref))
        normed_ref[...] = (center * inv * gain_ref[...]).T.astype(BF)

    value = dot(w_ref[...], normed_ref[...], 0, 0).astype(BF)
    write_part(part, out_ref, low_ref, high_ref, value)


def project_kernel(f, normed_ref, w_ref, out_ref, low_ref, high_ref):
    value = dot(w_ref[...], normed_ref[...], 0, 0).astype(BF)
    write_part(pl.program_id(0), out_ref, low_ref, high_ref, value)


def projection_outs(length):
    return [
        ((3 * GROUP, length), BF, (GROUP, length), lambda i, f: (i, 0)),
        out_fixed((2 * HALF, length), BF),
        out_fixed((HALF, length), BF),
    ]


def mask_tail(scores):
    n = scores.shape[0]
    key = lax.broadcasted_iota(jnp.int32, (SHORT, SHORT), 0)
    query = lax.broadcasted_iota(jnp.int32, (SHORT, SHORT), 1)
    diag = jnp.where(key <= query, scores[n - SHORT :], -1e30)
    return diag if n == SHORT else jnp.concatenate([scores[: n - SHORT], diag], 0)


def sweep(f, length, tile, variants):
    for condition, units in variants:
        for whole in (True, False):

            @pl.when(condition & (one_sequence(f) == whole))
            def _():
                for at in range(length // SHORT):
                    for unit in units:
                        tile(unit, at, 0 if whole else at)


def spans(at, first):
    return slice(at * SHORT, (at + 1) * SHORT), slice(first * SHORT, (at + 1) * SHORT)


def softmax_tile(q_refs, k_refs, v_refs, o_refs, lse_ref, unit, at, first):
    qp, keys = unit
    qs, ks = spans(at, first)
    q = q_refs[qp][:, qs]
    scores = [mask_tail(dot(k_refs[kp][:, ks], q, 0, 0) * SCALE2) for kp in keys]
    top = functools.reduce(jnp.maximum, [jnp.max(s, axis=0, keepdims=True) for s in scores])
    raw = [jnp.exp2(s - top) for s in scores]
    total = functools.reduce(jnp.add, [jnp.sum(p, axis=0, keepdims=True) for p in raw])
    out = functools.reduce(
        jnp.add, [dot(v_refs[kp][:, ks], p.astype(BF), 1, 0) for kp, p in zip(keys, raw)]
    )
    o_refs[qp][:, qs] = (out * (1.0 / total)).astype(o_refs[qp].dtype)
    lse_ref[0, qp : qp + 1, qs] = top + jnp.log2(total)


LOCAL_UNITS = (
    lambda f: (f[1] == 0, [(0, [0]), (1, [0, 1])]),
    lambda f: (f[1] == 1, [(1, [1]), (0, [0, 1])]),
)
CROSS_UNITS = [(0, [0, 1]), (1, [0, 1])]


def local_kernel(f, q0, q1, k0, k1, v0, v1, o0, o1, lse_ref):
    sweep(
        f,
        q0.shape[1],
        functools.partial(softmax_tile, (q0, q1), (k0, k1), (v0, v1), (o0, o1), lse_ref),
        [unit(f) for unit in LOCAL_UNITS],
    )


def cross_kernel(f, *refs):
    ins, (o_ref, lse_ref) = refs[:12], refs[12:]
    outs = (o_ref.at[0], o_ref.at[1])
    for early, at in ((1, 0), (0, 6)):
        q0, q1, k0, k1, v0, v1 = ins[at : at + 6]
        sweep(
            f,
            q0.shape[1],
            functools.partial(softmax_tile, (q0, q1), (k0, k1), (v0, v1), outs, lse_ref),
            [(f[2] == early, CROSS_UNITS)],
        )


def head(array, at):
    return (array, (HEAD_DIM, array.shape[-1]), lambda h, f: (at + h, 0))


def lse_spec(array):
    return (array, (1,) + array.shape[1:], lambda h, f: (h, 0, 0))


def lse_out(heads, length):
    return ((heads, 2, length), F32, (1, 2, length), lambda h, f: (h, 0, 0))


def cross_inputs(early_q, own, other, late_kv):
    return [
        head(early_q[0], 0),
        head(early_q[1], 0),
        head(own, 6 + HALF_HEADS),
        head(other, 6 + HALF_HEADS),
        head(own, 12 + HALF_HEADS),
        head(other, 12 + HALF_HEADS),
        head(own, 0),
        head(other, 0),
        head(late_kv[0], 0),
        head(late_kv[1], 0),
        head(late_kv[0], HALF_HEADS),
        head(late_kv[1], HALF_HEADS),
    ]


def merge_kernel(f, o0, o1, lse_ref, oc_ref, lsec_ref, ob_ref, lseb_ref, a0, a1, lse_out_ref, high_ref, lse_high_ref):
    half = pl.program_id(0)

    def finish(values, lse):
        for i, ref in ((0, a0), (1, a1)):
            ref[...] = values[i].astype(BF)
        lse_out_ref[...] = lse
        for i in (0, 1):
            high_ref[i] = values[i].astype(BF)
        lse_high_ref[...] = lse

    @pl.when(f[2] == 1)
    def _():
        finish((o0[...], o1[...]), lse_ref[...])

    @pl.when(f[2] == 0)
    def _():
        low = half == 0
        lse_c = jnp.where(low, lsec_ref[...], lseb_ref[...])
        lse_l = lse_ref[...]
        top = jnp.maximum(lse_l, lse_c)
        lse = top + jnp.log2(jnp.exp2(lse_l - top) + jnp.exp2(lse_c - top))
        share_l, share_c = jnp.exp2(lse_l - lse), jnp.exp2(lse_c - lse)
        values = []
        for i, ref in ((0, o0), (1, o1)):
            other = jnp.where(low, oc_ref[i], ob_ref[i]).astype(F32)
            rows = []
            for h in range(HALF_HEADS):
                at = slice(h * HEAD_DIM, (h + 1) * HEAD_DIM)
                rows.append(
                    ref[at, :] * share_l[h, i : i + 1] + other[at] * share_c[h, i : i + 1]
                )
            values.append(jnp.concatenate(rows, 0))
        finish(values, lse)


def gradient_tile(
    q_refs, k_refs, v_refs, g_refs, o_refs, lse_ref, dq_refs, dk_acc, dv_acc, unit, at, first
):
    qp, keys = unit
    qs, ks = spans(at, first)
    q, g = q_refs[qp][:, qs], g_refs[qp][:, qs]
    lse = lse_ref[0, qp : qp + 1, qs]
    delta = jnp.sum(g.astype(F32) * o_refs[qp][:, qs].astype(F32), axis=0, keepdims=True)
    dq = None
    for kp in keys:
        k, v = k_refs[kp][:, ks], v_refs[kp][:, ks]
        weights = jnp.exp2(mask_tail(dot(k, q, 0, 0) * SCALE2) - lse)
        ds = (weights * (dot(v, g, 0, 0) - delta)).astype(BF)
        term = dot(k, ds, 1, 0)
        dq = term if dq is None else dq + term
        dk_acc[kp, :, ks] += dot(q, ds, 1, 1)
        dv_acc[kp, :, ks] += dot(g, weights.astype(BF), 1, 1)
    dq_refs[qp][:, qs] = (dq * SCALE).astype(BF)


def local_back_kernel(
    f, q0, q1, k0, k1, v0, v1, g0, g1, o0, o1, lse_ref, d0, d1, dk_acc, dv_acc
):
    dk_acc[...] = jnp.zeros_like(dk_acc)
    dv_acc[...] = jnp.zeros_like(dv_acc)
    sweep(
        f,
        q0.shape[1],
        functools.partial(
            gradient_tile,
            (q0, q1),
            (k0, k1),
            (v0, v1),
            (g0, g1),
            (o0, o1),
            lse_ref,
            (d0.at[0], d1.at[0]),
            dk_acc,
            dv_acc,
        ),
        [unit(f) for unit in LOCAL_UNITS],
    )
    for i, ref in ((0, d0), (1, d1)):
        ref[1] = (dk_acc[i] * SCALE).astype(BF)
        ref[2] = dv_acc[i].astype(BF)


def cross_back_kernel(f, *refs):
    ins, more = refs[:12], refs[12:]
    (ga0, ga1, oa, lse_a, gb0, gb1, ob0, ob1, lse_b, dq_ref, dkv_ref, dk_acc, dv_acc) = more
    dk_acc[...] = jnp.zeros_like(dk_acc)
    dv_acc[...] = jnp.zeros_like(dv_acc)
    for early, at, grads, outs, lse_ref in (
        (1, 0, (ga0, ga1), (oa.at[0], oa.at[1]), lse_a),
        (0, 6, (gb0, gb1), (ob0, ob1), lse_b),
    ):
        q0, q1, k0, k1, v0, v1 = ins[at : at + 6]
        sweep(
            f,
            q0.shape[1],
            functools.partial(
                gradient_tile,
                (q0, q1),
                (k0, k1),
                (v0, v1),
                grads,
                outs,
                lse_ref,
                (dq_ref.at[0], dq_ref.at[1]),
                dk_acc,
                dv_acc,
            ),
            [(f[2] == early, CROSS_UNITS)],
        )
    for i in (0, 1):
        dkv_ref[0, i] = (dk_acc[i] * SCALE).astype(BF)
        dkv_ref[1, i] = dv_acc[i].astype(BF)


def gelu_pair(u):
    k = math.sqrt(2 / math.pi)
    square = u * u
    t = jnp.tanh(k * u * (1.0 + 0.044715 * square))
    half = 0.5 + 0.5 * t
    slope = half + 0.5 * u * (1.0 - t * t) * (k * (1.0 + 3 * 0.044715 * square))
    return u * half, slope


def ff_tile(normed2_ref, cot_ref, wu_ref, wd_ref):
    act, slope = gelu_pair(dot(normed2_ref[...], wu_ref[...], 1, 0))
    act = act.astype(BF)
    grad_up = (dot(cot_ref[...], wd_ref[...], 1, 1) * slope).astype(BF)
    return act, grad_up, dot(act, wd_ref[...], 1, 0), dot(grad_up, wu_ref[...], 1, 1)


def feed_first_kernel(
    f, x_ref, emb_ref, a_ref, b_ref, wa_ref, wb_ref, gain_ref, cot_ref, wu_ref, wd_ref,
    res_ref, n_ref, y_ref, c_ref, dd_ref, du_ref,
):
    step = pl.program_id(0)

    @pl.when(step == 0)
    def _():
        residual = (
            hidden_of(x_ref, emb_ref)
            + dot(a_ref[...], wa_ref[...], 0, 0)
            + dot(b_ref[...], wb_ref[...], 0, 0)
        )
        res_ref[...] = residual
        center, inv = centered(residual)
        n_ref[...] = (center * inv * gain_ref[...]).astype(BF)
        y_ref[...] = residual
        c_ref[...] = jnp.zeros_like(c_ref)

    act, grad_up, y, c = ff_tile(n_ref, cot_ref, wu_ref, wd_ref)
    y_ref[...] += y
    c_ref[...] += c
    dd_ref[...] = dot(act, cot_ref[...], 0, 0).astype(BF)
    du_ref[...] = dot(n_ref[...], grad_up, 0, 0).astype(BF)


def feed_second_kernel(
    f, res_ref, n_ref, y_ref, c_ref, gain_ref, cot_ref, wu_ref, wd_ref, wa_ref, wb_ref, a_ref, b_ref,
    dd_ref, du_ref, out_ref, gres_ref, ga_ref, gb_ref, gah_ref, gbh_ref, dgain_ref, dwa_ref, dwb_ref,
    y_acc, c_acc,
):
    step = pl.program_id(0)

    @pl.when(step == 0)
    def _():
        y_acc[...] = y_ref[...]
        c_acc[...] = c_ref[...]

    act, grad_up, y, c = ff_tile(n_ref, cot_ref, wu_ref, wd_ref)
    dd_ref[...] = dot(act, cot_ref[...], 0, 0).astype(BF)
    du_ref[...] = dot(n_ref[...], grad_up, 0, 0).astype(BF)
    y_acc[...] += y
    c_acc[...] += c

    @pl.when(step == pl.num_programs(0) - 1)
    def _():
        out_ref[...] = y_acc[...].astype(BF)
        center, inv = centered(res_ref[...])
        n2 = center * inv
        c_all = c_acc[...]
        dgain_ref[...] = jnp.sum(c_all * n2, axis=0, keepdims=True)
        e = c_all * gain_ref[...]
        grad_residual = cot_ref[...].astype(F32) + inv * (
            e - jnp.mean(e, axis=-1, keepdims=True) - n2 * jnp.mean(e * n2, axis=-1, keepdims=True)
        )
        gres_ref[...] = grad_residual
        grad_attn = grad_residual.astype(BF)
        mine = dot(wa_ref[...], grad_attn, 1, 1).astype(BF)
        theirs = dot(wb_ref[...], grad_attn, 1, 1).astype(BF)
        ga_ref[...] = mine
        gb_ref[...] = theirs
        gah_ref[...] = mine[HALF:]
        gbh_ref[...] = theirs[HALF:]
        dwa_ref[...] = dot(a_ref[...], grad_attn, 1, 0).astype(BF)
        dwb_ref[...] = dot(b_ref[...], grad_attn, 1, 0).astype(BF)


def combine_kernel(
    f, da0, da1, db0, db1, dqc_ref, dqb_ref, dkvc_ref, dkvb_ref, n0_ref, n1_ref,
    g0, g1, s0_ref, k0_ref, s1_ref, k1_ref, *, at,
):
    part = pl.program_id(0)
    late, early = f[2] == 0, f[2] == 1

    def put(low, high):
        for i, (refs, g) in enumerate((((da0, db0), g0), ((da1, db1), g1))):
            local = jnp.concatenate([d[0] for d in refs], 0)
            if low is None:
                g[...] = local
            else:
                more = jnp.concatenate([low[0, i], high[0, i]], 0)
                g[...] = (local.astype(F32) + more.astype(F32)).astype(BF)

    @pl.when(late & (part == 0))
    def _():
        put(dqc_ref, dqb_ref)

    @pl.when(early & (part > 0))
    def _():
        put(dkvb_ref, dkvc_ref)

    @pl.when((late & (part > 0)) | (early & (part == 0)))
    def _():
        put(None, None)

    value = dot(n0_ref[...], g0[...], 1, 1) + dot(n1_ref[...], g1[...], 1, 1)
    for i, (sent_ref, kept_ref) in enumerate(((s0_ref, k0_ref), (s1_ref, k1_ref))):
        sent, kept = pick(f[at[i]], value[i * (D // 2) : (i + 1) * (D // 2)])
        sent_ref[...] = sent.astype(BF)
        kept_ref[...] = kept.astype(BF)


def input_grad_kernel(
    f, g_ref, h_ref, wg_ref, wh_ref, x_ref, emb_ref, gain_ref, gres_ref, gin_ref, sums_ref, acc
):
    part = pl.program_id(0)
    value = dot(wg_ref[...], g_ref[...], 1, 0) + dot(wh_ref[...], h_ref[...], 1, 0)

    @pl.when(part == 0)
    def _():
        acc[...] = value

    @pl.when(part > 0)
    def _():
        acc[...] += value

    @pl.when(part == pl.num_programs(0) - 1)
    def _():
        center, inv = centered(hidden_of(x_ref, emb_ref))
        n1 = center * inv
        grad = acc[...].T
        e = grad * gain_ref[...]
        total = gres_ref[...] + inv * (
            e - jnp.mean(e, axis=-1, keepdims=True) - n1 * jnp.mean(e * n1, axis=-1, keepdims=True)
        )
        gin_ref[...] = total.astype(BF)
        sums_ref[...] = jnp.concatenate(
            [jnp.sum(total, axis=0, keepdims=True), jnp.sum(grad * n1, axis=0, keepdims=True)], 0
        )


def assemble_first_kernel(f, d_own, d_oth, u_own, u_oth, m_own, m_oth, down_ref, up_ref, out_ref):
    step = pl.program_id(0)
    half, at = step // 4, step % 4
    for mine, d, u, m in ((True, d_own, u_own, m_own), (False, d_oth, u_oth, m_oth)):
        here = (half == f[1]) == mine

        @pl.when(here & (at < 3))
        def _():
            down_ref[...] = d[...].astype(F32)
            up_ref[...] = u[...].astype(F32)

        @pl.when(here & (at == 3))
        def _():
            down_ref[...] = m[:GROUP].astype(F32)
            up_ref[:GROUP] = m[2 * GROUP :, :GROUP].astype(F32)
            up_ref[GROUP:] = m[2 * GROUP :, GROUP:].astype(F32)
            out_ref[...] = m[GROUP : 2 * GROUP].astype(F32)


def assemble_second_kernel(f, a_own, a_oth, b_own, b_oth, out_ref):
    for mine, a, b in ((True, a_own, b_own), (False, a_oth, b_oth)):

        @pl.when((pl.program_id(0) % 2 == f[1]) == mine)
        def _():
            out_ref[:GROUP] = a[...].astype(F32)
            out_ref[GROUP:] = b[...].astype(F32)


def swap(array, step):
    axis, mask, size, _ = step
    return lax.ppermute(array, axis, [(i, i ^ mask) for i in range(size)])


def tie(*groups):
    leaves, tree = jax.tree.flatten(groups)
    return jax.tree.unflatten(tree, lax.optimization_barrier(leaves))


def pick(here, total):
    half = total.shape[0] // 2
    low, high = total[:half], total[half:]
    return jnp.where(here == 0, high, low), jnp.where(here == 0, low, high)


def joined(here, own, other):
    return jnp.where(
        here == 0, jnp.concatenate([own, other], 0), jnp.concatenate([other, own], 0)
    )


def round_work(here, own, came, mode):
    if mode == "join":
        return (joined(here, own, came),)
    total = own + came
    return (total,) if mode == "sum" else pick(here, total)


def round_kernel(f, *refs, modes, at):
    refs = list(refs)
    outs = refs[2 * len(modes) :]
    for i, mode in enumerate(modes):
        own, came = refs[2 * i][...].astype(F32), refs[2 * i + 1][...].astype(F32)
        for value in round_work(f[at[i]], own, came, mode):
            outs.pop(0)[...] = value.astype(BF)


def whole_call(kernel, flags, ins, outs, name):
    vmem = pl.BlockSpec(memory_space=pltpu.VMEM)
    size = sum(math.prod(shape) for shape in [a.shape for a in ins] + outs)
    return pl.pallas_call(
        kernel,
        in_specs=[pl.BlockSpec(memory_space=pltpu.SMEM)] + [vmem] * len(ins),
        out_specs=[vmem] * len(outs),
        out_shape=[jax.ShapeDtypeStruct(shape, BF) for shape in outs],
        cost_estimate=cost(BRIEF),
        compiler_params=pltpu.CompilerParams(vmem_limit_bytes=2 * size + (8 << 20)),
        name=name,
    )(flags, *ins)


HALVE, FULL, JOIN = 0, 1, 2


class Chain:
    def __init__(self, steps, whole_steps, sent, kept):
        cut = len(steps) - whole_steps
        self.plan = (
            [(HALVE, step) for step in steps[:cut]]
            + [(FULL, step) for step in steps[cut:]]
            + [(JOIN, step) for step in reversed(steps[:cut])]
        )
        self.sent, self.kept, self.came = sent, kept, None

    def done(self):
        return not self.plan


def land(flags, chains):
    chains = [c for c in chains if c.came is not None]
    modes, at, ins, outs = [], [], [], []
    for c in chains:
        what, step = c.plan.pop(0)
        own = c.kept if what == HALVE else c.sent
        rows, columns = own.shape
        if what == JOIN:
            modes.append("join")
            at.append(step[3])
            outs += [(2 * rows, columns)]
        elif c.plan and c.plan[0][0] == HALVE:
            modes.append("split")
            at.append(c.plan[0][1][3])
            outs += [(rows // 2, columns)] * 2
        else:
            modes.append("sum")
            at.append(0)
            outs += [(rows, columns)]
        ins += [own, c.came]
    if all(shape[0] % 8 == 0 for shape in outs):
        kernel = functools.partial(round_kernel, modes=modes, at=at)
        results = list(whole_call(kernel, flags, ins, outs, "round"))
    else:
        results = []
        for i, mode in enumerate(modes):
            own, came = (a.astype(F32) for a in ins[2 * i : 2 * i + 2])
            results += [v.astype(BF) for v in round_work(flags[at[i]], own, came, mode)]
    for c, mode in zip(chains, modes, strict=True):
        c.came, c.sent = None, results.pop(0)
        if mode == "split":
            c.kept = results.pop(0)


def open_kernel(f, dd, ddr, du, dur, dw, dwr, *outs, at):
    def add(left, right):
        return left[...].astype(F32) + right[...].astype(F32)

    down, up, out = add(dd, ddr), add(du, dur), add(dw, dwr)
    cut = down.shape[0] - GROUP
    mixed = jnp.concatenate(
        [down[cut:], out, jnp.concatenate([up[:GROUP, cut:], up[GROUP:, cut:]], 1)], 0
    )
    for i, value in enumerate((down[:cut], up[:, :cut], mixed)):
        sent, kept = pick(f[at[i]], value)
        outs[2 * i][...] = sent.astype(BF)
        outs[2 * i + 1][...] = kept.astype(BF)


def send(chains, *more):
    chains = [c for c in chains if not c.done()]
    loads, more = tie([c.sent for c in chains], more)
    for c, load in zip(chains, loads, strict=True):
        c.sent, c.came = load, swap(load, c.plan[0][1])
    return more


def on_device(
    sizes, block_input, segments, pass_emb, gain_attn, w_qkv, w_out, gain_mlp, w_up, w_down, cotangent
):
    passes, n_dp = sizes
    core = ("pass", 1, passes, 1)
    cross = ("pass", 2, passes, 4)
    lanes = [("dp", 1 << i, n_dp, 5 + i) for i in range(n_dp.bit_length() - 1)]
    ring = [cross] + lanes
    orders = [ring, ring[1:] + ring[:1], ring[2:] + ring[:2]]

    pass_here = lax.axis_index("pass")
    core_here = pass_here % 2
    length = segments.shape[0]
    flags = jnp.stack(
        [
            (segments[0] == segments[length - 1]).astype(jnp.int32),
            core_here.astype(jnp.int32),
            (pass_here < 2).astype(jnp.int32),
            pass_here.astype(jnp.int32),
        ]
        + [((lax.axis_index(axis) // mask) % 2).astype(jnp.int32) for axis, mask, _, _ in ring]
    )

    def to_late(array, other=0):
        return lax.ppermute(array, "pass", [(0, 2 + other), (1, 3 - other)])

    def to_early(array, other=0):
        return lax.ppermute(array, "pass", [(2, other), (3, 1 - other)])

    x, cot = block_input[0], cotangent[0]
    emb = (pass_emb.reshape(passes, 1, D), (1, 1, D), lambda i, f: (f[3], 0, 0))

    normed, theirs, low_t, high_t = call(
        norm_project_kernel,
        flags,
        (3,),
        [
            fixed(x),
            emb,
            fixed(row(gain_attn)),
            (w_qkv, (D, GROUP), lambda i, f: (0, 2 * i + 1 - f[1])),
        ],
        [out_fixed((D, length), BF)] + projection_outs(length),
        BRIEF,
        "norm_project",
    )
    other = swap(theirs, core)
    own, low_o, high_o = call(
        project_kernel,
        flags,
        (3,),
        [fixed(normed), (w_qkv, (D, GROUP), lambda i, f: (0, 2 * i + f[1]))],
        projection_outs(length),
        BRIEF,
        "project_own",
    )
    late_kv = (to_late(low_o), to_late(low_t, 1))
    early_q = (to_early(high_o), to_early(high_t, 1))
    normed_other = swap(normed, core)

    cross_in = cross_inputs(early_q, own, other, late_kv)
    pair_out = ((2, HALF, length), BF, (2, HEAD_DIM, length), lambda h, f: (0, h, 0))
    o_cross, lse_cross = call(
        cross_kernel,
        flags,
        (HALF_HEADS,),
        cross_in,
        [pair_out, lse_out(HALF_HEADS, length)],
        BRIEF,
        "attend_cross",
    )
    o_cross, lse_cross, own, other = tie(o_cross, lse_cross, own, other)
    o_back, lse_back = to_late(o_cross), to_late(lse_cross)
    local_inputs = [head(a, at) for at in (0, 6, 12) for a in (own, other)]
    o0, o1, lse_local = call(
        local_kernel,
        flags,
        (HEADS // 2,),
        local_inputs,
        [((GROUP, length), F32, (HEAD_DIM, length), lambda h, f: (h, 0))] * 2
        + [lse_out(HEADS // 2, length)],
        BRIEF,
        "attend_local",
    )
    half_rows = (HALF, length)
    att_own, att_pair, lse, att_high, lse_high = call(
        merge_kernel,
        flags,
        (2,),
        [
            (o0, half_rows, lambda i, f: (i, 0)),
            (o1, half_rows, lambda i, f: (i, 0)),
            (lse_local, (HALF_HEADS, 2, length), lambda i, f: (i, 0, 0)),
            fixed(o_cross),
            fixed(lse_cross),
            fixed(o_back),
            fixed(lse_back),
        ],
        [((GROUP, length), BF, half_rows, lambda i, f: (i, 0))] * 2
        + [
            ((HEADS // 2, 2, length), F32, (HALF_HEADS, 2, length), lambda i, f: (i, 0, 0)),
            out_fixed((2, HALF, length), BF),
            out_fixed((HALF_HEADS, 2, length), F32),
        ],
        BRIEF,
        "merge",
    )
    att_other = swap(att_pair, core)
    att_early, lse_early = to_early(att_high), to_early(lse_high)
    att_own, att_other, normed_other = tie(att_own, att_other, normed_other)

    w_half = [(w_out, (GROUP, D), lambda i, f: (f[1], 0)), (w_out, (GROUP, D), lambda i, f: (1 - f[1], 0))]
    ff_half = w_up.shape[1] // 2
    steps = ff_half // FF_TILE

    def ff_weights(at):
        return [
            (w_up, (D, FF_TILE), lambda i, f: (0, at(f) * steps + i)),
            (w_down, (FF_TILE, D), lambda i, f: (at(f) * steps + i, 0)),
        ]

    tokens = (length, D)
    residual, normed2, y_part, c_part, down_sent, up_sent = call(
        feed_first_kernel,
        flags,
        (steps,),
        [fixed(x), emb, fixed(att_own), fixed(att_other)]
        + w_half
        + [fixed(row(gain_mlp)), fixed(cot)]
        + ff_weights(lambda f: 1 - f[1]),
        [
            out_fixed(tokens, F32),
            out_fixed(tokens, BF),
            out_fixed(tokens, F32),
            out_fixed(tokens, F32),
            ((ff_half, D), BF, (FF_TILE, D), lambda i, f: (i, 0)),
            ((D, ff_half), BF, (D, FF_TILE), lambda i, f: (0, i)),
        ],
        BRIEF,
        "feed_first",
        temporaries=14,
    )
    down_sent, up_sent, att_early, lse_early = tie(down_sent, up_sent, att_early, lse_early)
    down_recv, up_recv = swap(down_sent, core), swap(up_sent, core)
    (
        down_own, up_own, output, grad_residual, g_own, g_theirs, g_own_high, g_theirs_high, dgain_mlp, out_own, out_sent
    ) = call(
        feed_second_kernel,
        flags,
        (steps,),
        [fixed(a) for a in (residual, normed2, y_part, c_part, row(gain_mlp), cot)]
        + ff_weights(lambda f: f[1])
        + w_half
        + [fixed(att_own), fixed(att_other)],
        [
            ((ff_half, D), BF, (FF_TILE, D), lambda i, f: (i, 0)),
            ((D, ff_half), BF, (D, FF_TILE), lambda i, f: (0, i)),
            out_fixed(tokens, BF),
            out_fixed(tokens, F32),
            out_fixed((GROUP, length), BF),
            out_fixed((GROUP, length), BF),
            out_fixed(half_rows, BF),
            out_fixed(half_rows, BF),
            out_fixed((1, D), F32),
            out_fixed((GROUP, D), BF),
            out_fixed((GROUP, D), BF),
        ],
        BRIEF,
        "feed_second",
        [pltpu.VMEM(tokens, F32)] * 2,
        14,
    )
    g_other = swap(g_theirs, core)
    early_g = (to_early(g_own_high), to_early(g_theirs_high, 1))
    out_recv = swap(out_sent, core)

    accumulators = [pltpu.VMEM((2, HEAD_DIM, length), F32)] * 2

    def local_back(at, heads, g0, g1):
        return call(
            local_back_kernel,
            flags,
            (heads,),
            [head(a, base + at) for base in (0, 6, 12) for a in (own, other)]
            + [head(a, at) for a in (g0, g1, att_own, att_pair)]
            + [(lse, (1, 2, length), lambda h, f: (at + h, 0, 0))],
            [((3, heads * HEAD_DIM, length), BF, (3, HEAD_DIM, length), lambda h, f: (0, h, 0))] * 2,
            BRIEF,
            "attend_back_local",
            accumulators,
        )

    d_0 = local_back(0, 2, g_own, g_other)
    d_0, early_g, out_own = tie(d_0, early_g, out_own)
    opened = whole_call(
        functools.partial(open_kernel, at=[steps_[0][3] for steps_ in orders]),
        flags,
        [down_own, down_recv, up_own, up_recv, out_own, out_recv],
        [shape for shape in ((576, D), (GROUP, 3 * GROUP), (576, D)) for _ in (0, 1)],
        "open",
    )
    first = [Chain(orders[i], 1, *opened[2 * i : 2 * i + 2]) for i in range(3)]
    (early_g,) = send(first, early_g)
    dq_cross, dkv_cross = call(
        cross_back_kernel,
        flags,
        (HALF_HEADS,),
        cross_in
        + [
            head(early_g[0], 0),
            head(early_g[1], 0),
            (att_early, (2, HEAD_DIM, length), lambda h, f: (0, h, 0)),
            lse_spec(lse_early),
            head(g_own, 0),
            head(g_other, 0),
            head(att_own, 0),
            head(att_pair, 0),
            lse_spec(lse),
        ],
        [
            pair_out,
            (
                (2, 2, HALF, length),
                BF,
                (2, 2, HEAD_DIM, length),
                lambda h, f: (0, 0, h, 0),
            ),
        ],
        BRIEF,
        "attend_back_cross",
        accumulators,
    )
    land(flags, first)
    dq_cross, dkv_cross, g_own, g_other = send(first, dq_cross, dkv_cross, g_own, g_other)
    dq_back, dkv_back = to_late(dq_cross), to_early(dkv_cross)
    d_1 = local_back(2, 4, g_own, g_other)
    land(flags, first)
    d_1, dq_back, dkv_back = send(first, d_1, dq_back, dkv_back)
    few, many = (1, 2 * HEAD_DIM, length), (1, 4 * HEAD_DIM, length)
    one_q = (1, 2, HALF, length)
    by_y = lanes[:1] + [cross] + lanes[1:]
    gp_own, gp_pair, *opened = call(
        functools.partial(combine_kernel, at=[ring[0][3], by_y[0][3]]),
        flags,
        (3,),
        [(d, few, lambda i, f: (i, 0, 0)) for d in d_0]
        + [(d, many, lambda i, f: (i, 0, 0)) for d in d_1]
        + [
            fixed(dq_cross.reshape(one_q)),
            fixed(dq_back.reshape(one_q)),
            (dkv_cross, one_q, lambda i, f: (jnp.maximum(i - 1, 0), 0, 0, 0)),
            (dkv_back, one_q, lambda i, f: (jnp.maximum(i - 1, 0), 0, 0, 0)),
            fixed(normed),
            fixed(normed_other),
        ],
        [((3 * GROUP, length), BF, (GROUP, length), lambda i, f: (i, 0))] * 2
        + [((D // 4, 3 * GROUP), BF, (D // 4, GROUP), lambda i, f: (0, i))] * 4,
        BRIEF,
        "combine",
    )
    second = [Chain(order, 2, *opened[2 * i : 2 * i + 2]) for i, order in enumerate((ring, by_y))]
    send(second)
    gp_other = swap(gp_pair, core)
    land(flags, first)
    (gp_other,) = send(first, gp_other)
    land(flags, first + second)
    (gp_other,) = send(first + second, gp_other)
    land(flags, first + second)
    gp_own, gp_other = send(first + second, gp_own, gp_other)
    grad_input, sums = call(
        input_grad_kernel,
        flags,
        (3,),
        [
            (gp_own, (GROUP, length), lambda i, f: (i, 0)),
            (gp_other, (GROUP, length), lambda i, f: (i, 0)),
            (w_qkv, (D, GROUP), lambda i, f: (0, 2 * i + f[1])),
            (w_qkv, (D, GROUP), lambda i, f: (0, 2 * i + 1 - f[1])),
            fixed(x),
            emb,
            fixed(row(gain_attn)),
            fixed(grad_residual),
        ],
        [out_fixed(tokens, BF), out_fixed((2, D), F32)],
        BRIEF,
        "input_grad",
        [pltpu.VMEM((D, length), F32)],
    )
    selector = (jnp.arange(passes) == pass_here).astype(F32)
    small = jnp.concatenate([selector[:, None] * sums[:1], sums[1:], dgain_mlp])
    rounds = [core, cross] + lanes
    land(flags, first + second)
    while not first[0].done():
        (small,) = send(first + second, small)
        if rounds:
            small = small + swap(small, rounds.pop(0))
        land(flags, first + second)
    pairs = [(c.sent, swap(c.sent, core)) for c in first]
    third = [a for pair in pairs for a in pair]
    at_most = [
        (third[i], (GROUP, D), lambda j, f: (jnp.minimum(j % 4, 2), 0)) for i in (0, 1)
    ] + [(third[i], (D, GROUP), lambda j, f: (0, jnp.minimum(j % 4, 2))) for i in (2, 3)]
    down_total, up_total, out_total = call(
        assemble_first_kernel,
        flags,
        (8,),
        at_most + [fixed(third[4]), fixed(third[5])],
        [
            ((4 * D, D), F32, (GROUP, D), lambda j, f: (j, 0)),
            ((D, 4 * D), F32, (D, GROUP), lambda j, f: (0, j)),
            ((D, D), F32, (GROUP, D), lambda j, f: (j // 4, 0)),
        ],
        BRIEF,
        "assemble_first",
    )
    while not second[0].done():
        (small,) = send(second, small)
        if rounds:
            small = small + swap(small, rounds.pop(0))
        came = [c.came for c in second]
        came, down_total, up_total, out_total = tie(came, down_total, up_total, out_total)
        for c, array in zip(second, came, strict=True):
            c.came = array
        land(flags, second)
    for step in rounds:
        small = small + swap(small, step)
    qkv_total = call(
        assemble_second_kernel,
        flags,
        (6,),
        [
            (a, (GROUP, GROUP), lambda j, f: (0, j // 2))
            for c in second
            for a in (c.sent, swap(c.sent, core))
        ],
        [((D, 3 * D), F32, (D, GROUP), lambda j, f: (0, j))],
        BRIEF,
        "assemble_second",
    )[0]
    return (
        output[None],
        grad_input[None],
        small[:passes],
        small[passes],
        qkv_total,
        out_total,
        small[passes + 1],
        up_total,
        down_total,
    )


def solution(mesh):
    sizes = (mesh.shape["pass"], mesh.shape["dp"])
    tokens = P("pass", "dp", None)
    in_specs = (tokens, P("dp")) + (P(),) * 7 + (tokens,)
    out_specs = (tokens, tokens) + (P(),) * 7
    return jax.shard_map(
        functools.partial(on_device, sizes),
        mesh=mesh,
        in_specs=in_specs,
        out_specs=out_specs,
        check_vma=False,
    )
```

```python
import functools
import math

import jax
import jax.numpy as jnp
from jax import lax
from jax.experimental import pallas as pl
from jax.experimental.pallas import tpu as pltpu
from jax.sharding import PartitionSpec as P

D = 768
HEADS = 12
HEAD_DIM = 64
SHORT = 256
FF_TILE = 512
GROUP = D // 2
HALF = GROUP // 2
HALF_HEADS = HEADS // 4
EPS = 1e-05
SCALE = HEAD_DIM**-0.5
SCALE2 = SCALE * math.log2(math.e)
BF = jnp.bfloat16
F32 = jnp.float32
BRIEF = 0.2


def dot(a, b, ca, cb):
    return lax.dot_general(a, b, (((ca,), (cb,)), ((), ())), preferred_element_type=F32)


def cost(us):
    return pl.CostEstimate(flops=int(us * 1.1e9), bytes_accessed=1 << 20, transcendentals=0)


def call(kernel, flags, grid, ins, outs, us, name, scratch=(), temporaries=8):
    blocks = [(math.prod(block), array.dtype) for array, block, _ in ins]
    blocks += [(math.prod(block), dtype) for _, dtype, block, _ in outs]
    blocks += [(math.prod(buffer.shape) // 2, buffer.dtype) for buffer in scratch]
    limit = sum(2 * n * jnp.dtype(dtype).itemsize for n, dtype in blocks) + (temporaries << 20)
    return pl.pallas_call(
        kernel,
        grid_spec=pltpu.PrefetchScalarGridSpec(
            num_scalar_prefetch=1,
            grid=grid,
            in_specs=[pl.BlockSpec(block, index) for _, block, index in ins],
            out_specs=[pl.BlockSpec(block, index) for _, _, block, index in outs],
            scratch_shapes=list(scratch),
        ),
        out_shape=[jax.ShapeDtypeStruct(shape, dtype) for shape, dtype, _, _ in outs],
        cost_estimate=cost(us),
        compiler_params=pltpu.CompilerParams(vmem_limit_bytes=min(limit, 60 << 20)),
        name=name,
    )(flags, *[array for array, _, _ in ins])


def fixed(array):
    return (array, array.shape, lambda i, f: (0,) * array.ndim)


def out_fixed(shape, dtype):
    return (shape, dtype, shape, lambda i, f: (0,) * len(shape))


def row(vector):
    return vector.reshape(1, -1)


def one_sequence(f):
    return f[0] == 1


def hidden_of(x_ref, emb_ref):
    return x_ref[...].astype(F32) + emb_ref[0]


def centered(values):
    center = values - jnp.mean(values, axis=-1, keepdims=True)
    return center, lax.rsqrt(jnp.mean(center * center, axis=-1, keepdims=True) + EPS)


def write_part(part, out_ref, low_ref, high_ref, value):
    out_ref[...] = value

    @pl.when(part == 0)
    def _():
        high_ref[...] = value[HALF:]

    @pl.when(part > 0)
    def _():
        low_ref[pl.ds(pl.multiple_of((part - 1) * HALF, HALF), HALF), :] = value[:HALF]


def norm_project_kernel(f, x_ref, emb_ref, gain_ref, w_ref, normed_ref, out_ref, low_ref, high_ref):
    part = pl.program_id(0)

    @pl.when(part == 0)
    def _():
        center, inv = centered(hidden_of(x_ref, emb_ref))
        normed_ref[...] = (center * inv * gain_ref[...]).T.astype(BF)

    value = dot(w_ref[...], normed_ref[...], 0, 0).astype(BF)
    write_part(part, out_ref, low_ref, high_ref, value)


def project_kernel(f, normed_ref, w_ref, out_ref, low_ref, high_ref):
    value = dot(w_ref[...], normed_ref[...], 0, 0).astype(BF)
    write_part(pl.program_id(0), out_ref, low_ref, high_ref, value)


def projection_outs(length):
    return [
        ((3 * GROUP, length), BF, (GROUP, length), lambda i, f: (i, 0)),
        out_fixed((2 * HALF, length), BF),
        out_fixed((HALF, length), BF),
    ]


def mask_tail(scores):
    n = scores.shape[0]
    key = lax.broadcasted_iota(jnp.int32, (SHORT, SHORT), 0)
    query = lax.broadcasted_iota(jnp.int32, (SHORT, SHORT), 1)
    diag = jnp.where(key <= query, scores[n - SHORT :], -1e30)
    return diag if n == SHORT else jnp.concatenate([scores[: n - SHORT], diag], 0)


def sweep(f, length, tile, variants):
    for condition, units in variants:
        for whole in (True, False):

            @pl.when(condition & (one_sequence(f) == whole))
            def _():
                for at in range(length // SHORT):
                    for unit in units:
                        tile(unit, at, 0 if whole else at)


def spans(at, first):
    return slice(at * SHORT, (at + 1) * SHORT), slice(first * SHORT, (at + 1) * SHORT)


def softmax_tile(q_refs, k_refs, v_refs, o_refs, lse_ref, unit, at, first):
    qp, keys = unit
    qs, ks = spans(at, first)
    q = q_refs[qp][:, qs]
    scores = [mask_tail(dot(k_refs[kp][:, ks], q, 0, 0) * SCALE2) for kp in keys]
    top = functools.reduce(jnp.maximum, [jnp.max(s, axis=0, keepdims=True) for s in scores])
    raw = [jnp.exp2(s - top) for s in scores]
    total = functools.reduce(jnp.add, [jnp.sum(p, axis=0, keepdims=True) for p in raw])
    out = functools.reduce(
        jnp.add, [dot(v_refs[kp][:, ks], p.astype(BF), 1, 0) for kp, p in zip(keys, raw)]
    )
    o_refs[qp][:, qs] = (out * (1.0 / total)).astype(o_refs[qp].dtype)
    lse_ref[0, qp : qp + 1, qs] = top + jnp.log2(total)


LOCAL_UNITS = (
    lambda f: (f[1] == 0, [(0, [0]), (1, [0, 1])]),
    lambda f: (f[1] == 1, [(1, [1]), (0, [0, 1])]),
)
CROSS_UNITS = [(0, [0, 1]), (1, [0, 1])]


def local_kernel(f, q0, q1, k0, k1, v0, v1, o0, o1, lse_ref):
    sweep(
        f,
        q0.shape[1],
        functools.partial(softmax_tile, (q0, q1), (k0, k1), (v0, v1), (o0, o1), lse_ref),
        [unit(f) for unit in LOCAL_UNITS],
    )


def cross_kernel(f, *refs):
    ins, (o_ref, lse_ref) = refs[:12], refs[12:]
    outs = (o_ref.at[0], o_ref.at[1])
    for early, at in ((1, 0), (0, 6)):
        q0, q1, k0, k1, v0, v1 = ins[at : at + 6]
        sweep(
            f,
            q0.shape[1],
            functools.partial(softmax_tile, (q0, q1), (k0, k1), (v0, v1), outs, lse_ref),
            [(f[2] == early, CROSS_UNITS)],
        )


def head(array, at):
    return (array, (HEAD_DIM, array.shape[-1]), lambda h, f: (at + h, 0))


def lse_spec(array):
    return (array, (1,) + array.shape[1:], lambda h, f: (h, 0, 0))


def lse_out(heads, length):
    return ((heads, 2, length), F32, (1, 2, length), lambda h, f: (h, 0, 0))


def cross_inputs(early_q, own, other, late_kv):
    return [
        head(early_q[0], 0),
        head(early_q[1], 0),
        head(own, 6 + HALF_HEADS),
        head(other, 6 + HALF_HEADS),
        head(own, 12 + HALF_HEADS),
        head(other, 12 + HALF_HEADS),
        head(own, 0),
        head(other, 0),
        head(late_kv[0], 0),
        head(late_kv[1], 0),
        head(late_kv[0], HALF_HEADS),
        head(late_kv[1], HALF_HEADS),
    ]


def merge_kernel(f, o0, o1, lse_ref, oc_ref, lsec_ref, ob_ref, lseb_ref, a0, a1, lse_out_ref, high_ref, lse_high_ref):
    half = pl.program_id(0)

    def finish(values, lse):
        for i, ref in ((0, a0), (1, a1)):
            ref[...] = values[i].astype(BF)
        lse_out_ref[...] = lse
        for i in (0, 1):
            high_ref[i] = values[i].astype(BF)
        lse_high_ref[...] = lse

    @pl.when(f[2] == 1)
    def _():
        finish((o0[...], o1[...]), lse_ref[...])

    @pl.when(f[2] == 0)
    def _():
        low = half == 0
        lse_c = jnp.where(low, lsec_ref[...], lseb_ref[...])
        lse_l = lse_ref[...]
        top = jnp.maximum(lse_l, lse_c)
        lse = top + jnp.log2(jnp.exp2(lse_l - top) + jnp.exp2(lse_c - top))
        share_l, share_c = jnp.exp2(lse_l - lse), jnp.exp2(lse_c - lse)
        values = []
        for i, ref in ((0, o0), (1, o1)):
            other = jnp.where(low, oc_ref[i], ob_ref[i]).astype(F32)
            rows = []
            for h in range(HALF_HEADS):
                at = slice(h * HEAD_DIM, (h + 1) * HEAD_DIM)
                rows.append(
                    ref[at, :] * share_l[h, i : i + 1] + other[at] * share_c[h, i : i + 1]
                )
            values.append(jnp.concatenate(rows, 0))
        finish(values, lse)


def gradient_tile(
    q_refs, k_refs, v_refs, g_refs, o_refs, lse_ref, dq_refs, dk_acc, dv_acc, unit, at, first
):
    qp, keys = unit
    qs, ks = spans(at, first)
    q, g = q_refs[qp][:, qs], g_refs[qp][:, qs]
    lse = lse_ref[0, qp : qp + 1, qs]
    delta = jnp.sum(g.astype(F32) * o_refs[qp][:, qs].astype(F32), axis=0, keepdims=True)
    dq = None
    for kp in keys:
        k, v = k_refs[kp][:, ks], v_refs[kp][:, ks]
        weights = jnp.exp2(mask_tail(dot(k, q, 0, 0) * SCALE2) - lse)
        ds = (weights * (dot(v, g, 0, 0) - delta)).astype(BF)
        term = dot(k, ds, 1, 0)
        dq = term if dq is None else dq + term
        dk_acc[kp, :, ks] += dot(q, ds, 1, 1)
        dv_acc[kp, :, ks] += dot(g, weights.astype(BF), 1, 1)
    dq_refs[qp][:, qs] = (dq * SCALE).astype(BF)


def local_back_kernel(
    f, q0, q1, k0, k1, v0, v1, g0, g1, o0, o1, lse_ref, d0, d1, dk_acc, dv_acc
):
    dk_acc[...] = jnp.zeros_like(dk_acc)
    dv_acc[...] = jnp.zeros_like(dv_acc)
    sweep(
        f,
        q0.shape[1],
        functools.partial(
            gradient_tile,
            (q0, q1),
            (k0, k1),
            (v0, v1),
            (g0, g1),
            (o0, o1),
            lse_ref,
            (d0.at[0], d1.at[0]),
            dk_acc,
            dv_acc,
        ),
        [unit(f) for unit in LOCAL_UNITS],
    )
    for i, ref in ((0, d0), (1, d1)):
        ref[1] = (dk_acc[i] * SCALE).astype(BF)
        ref[2] = dv_acc[i].astype(BF)


def cross_back_kernel(f, *refs):
    ins, more = refs[:12], refs[12:]
    (ga0, ga1, oa, lse_a, gb0, gb1, ob0, ob1, lse_b, dq_ref, dkv_ref, dk_acc, dv_acc) = more
    dk_acc[...] = jnp.zeros_like(dk_acc)
    dv_acc[...] = jnp.zeros_like(dv_acc)
    for early, at, grads, outs, lse_ref in (
        (1, 0, (ga0, ga1), (oa.at[0], oa.at[1]), lse_a),
        (0, 6, (gb0, gb1), (ob0, ob1), lse_b),
    ):
        q0, q1, k0, k1, v0, v1 = ins[at : at + 6]
        sweep(
            f,
            q0.shape[1],
            functools.partial(
                gradient_tile,
                (q0, q1),
                (k0, k1),
                (v0, v1),
                grads,
                outs,
                lse_ref,
                (dq_ref.at[0], dq_ref.at[1]),
                dk_acc,
                dv_acc,
            ),
            [(f[2] == early, CROSS_UNITS)],
        )
    for i in (0, 1):
        dkv_ref[0, i] = (dk_acc[i] * SCALE).astype(BF)
        dkv_ref[1, i] = dv_acc[i].astype(BF)


def gelu_pair(u):
    k = math.sqrt(2 / math.pi)
    square = u * u
    t = jnp.tanh(k * u * (1.0 + 0.044715 * square))
    half = 0.5 + 0.5 * t
    slope = half + 0.5 * u * (1.0 - t * t) * (k * (1.0 + 3 * 0.044715 * square))
    return u * half, slope


def ff_tile(normed2_ref, cot_ref, wu_ref, wd_ref):
    act, slope = gelu_pair(dot(normed2_ref[...], wu_ref[...], 1, 0))
    act = act.astype(BF)
    grad_up = (dot(cot_ref[...], wd_ref[...], 1, 1) * slope).astype(BF)
    return act, grad_up, dot(act, wd_ref[...], 1, 0), dot(grad_up, wu_ref[...], 1, 1)


def feed_first_kernel(
    f, x_ref, emb_ref, a_ref, b_ref, wa_ref, wb_ref, gain_ref, cot_ref, wu_ref, wd_ref,
    res_ref, n_ref, y_ref, c_ref, dd_ref, du_ref,
):
    step = pl.program_id(0)

    @pl.when(step == 0)
    def _():
        residual = (
            hidden_of(x_ref, emb_ref)
            + dot(a_ref[...], wa_ref[...], 0, 0)
            + dot(b_ref[...], wb_ref[...], 0, 0)
        )
        res_ref[...] = residual
        center, inv = centered(residual)
        n_ref[...] = (center * inv * gain_ref[...]).astype(BF)
        y_ref[...] = residual
        c_ref[...] = jnp.zeros_like(c_ref)

    act, grad_up, y, c = ff_tile(n_ref, cot_ref, wu_ref, wd_ref)
    y_ref[...] += y
    c_ref[...] += c
    dd_ref[...] = dot(act, cot_ref[...], 0, 0).astype(BF)
    du_ref[...] = dot(n_ref[...], grad_up, 0, 0).astype(BF)


def feed_second_kernel(
    f, res_ref, n_ref, y_ref, c_ref, gain_ref, cot_ref, wu_ref, wd_ref, wa_ref, wb_ref, a_ref, b_ref,
    dd_ref, du_ref, out_ref, gres_ref, ga_ref, gb_ref, gah_ref, gbh_ref, dgain_ref, dwa_ref, dwb_ref,
    y_acc, c_acc,
):
    step = pl.program_id(0)

    @pl.when(step == 0)
    def _():
        y_acc[...] = y_ref[...]
        c_acc[...] = c_ref[...]

    act, grad_up, y, c = ff_tile(n_ref, cot_ref, wu_ref, wd_ref)
    dd_ref[...] = dot(act, cot_ref[...], 0, 0).astype(BF)
    du_ref[...] = dot(n_ref[...], grad_up, 0, 0).astype(BF)
    y_acc[...] += y
    c_acc[...] += c

    @pl.when(step == pl.num_programs(0) - 1)
    def _():
        out_ref[...] = y_acc[...].astype(BF)
        center, inv = centered(res_ref[...])
        n2 = center * inv
        c_all = c_acc[...]
        dgain_ref[...] = jnp.sum(c_all * n2, axis=0, keepdims=True)
        e = c_all * gain_ref[...]
        grad_residual = cot_ref[...].astype(F32) + inv * (
            e - jnp.mean(e, axis=-1, keepdims=True) - n2 * jnp.mean(e * n2, axis=-1, keepdims=True)
        )
        gres_ref[...] = grad_residual
        grad_attn = grad_residual.astype(BF)
        mine = dot(wa_ref[...], grad_attn, 1, 1).astype(BF)
        theirs = dot(wb_ref[...], grad_attn, 1, 1).astype(BF)
        ga_ref[...] = mine
        gb_ref[...] = theirs
        gah_ref[...] = mine[HALF:]
        gbh_ref[...] = theirs[HALF:]
        dwa_ref[...] = dot(a_ref[...], grad_attn, 1, 0).astype(BF)
        dwb_ref[...] = dot(b_ref[...], grad_attn, 1, 0).astype(BF)


def combine_kernel(f, da0, da1, db0, db1, dc0, dc1, dqc_ref, dqb_ref, dkvc_ref, dkvb_ref, g0, g1):
    part = pl.program_id(0)
    late, early = f[2] == 0, f[2] == 1

    def put(low, high):
        for i, (refs, g) in enumerate((((da0, db0, dc0), g0), ((da1, db1, dc1), g1))):
            local = jnp.concatenate([d[0] for d in refs], 0)
            if low is None:
                g[...] = local
            else:
                more = jnp.concatenate([low[0, i], high[0, i]], 0)
                g[...] = (local.astype(F32) + more.astype(F32)).astype(BF)

    @pl.when(late & (part == 0))
    def _():
        put(dqc_ref, dqb_ref)

    @pl.when(early & (part > 0))
    def _():
        put(dkvb_ref, dkvc_ref)

    @pl.when((late & (part > 0)) | (early & (part == 0)))
    def _():
        put(None, None)


def project_grad_kernel(f, g0, g1, n0_ref, n1_ref, s0_ref, k0_ref, s1_ref, k1_ref, *, at):
    value = dot(n0_ref[...], g0[...], 1, 1) + dot(n1_ref[...], g1[...], 1, 1)
    for i, (sent_ref, kept_ref) in enumerate(((s0_ref, k0_ref), (s1_ref, k1_ref))):
        sent, kept = pick(f[at[i]], value[i * (D // 2) : (i + 1) * (D // 2)])
        sent_ref[...] = sent.astype(BF)
        kept_ref[...] = kept.astype(BF)


def input_grad_kernel(
    f, g_ref, h_ref, wg_ref, wh_ref, x_ref, emb_ref, gain_ref, gres_ref, dgain_ref, gin_ref, sums_ref, acc
):
    part = pl.program_id(0)
    value = dot(wg_ref[...], g_ref[...], 1, 0) + dot(wh_ref[...], h_ref[...], 1, 0)

    @pl.when(part == 0)
    def _():
        acc[...] = value

    @pl.when(part > 0)
    def _():
        acc[...] += value

    @pl.when(part == pl.num_programs(0) - 1)
    def _():
        center, inv = centered(hidden_of(x_ref, emb_ref))
        n1 = center * inv
        grad = acc[...].T
        e = grad * gain_ref[...]
        total = gres_ref[...] + inv * (
            e - jnp.mean(e, axis=-1, keepdims=True) - n1 * jnp.mean(e * n1, axis=-1, keepdims=True)
        )
        gin_ref[...] = total.astype(BF)
        sums = jnp.sum(total, axis=0, keepdims=True)
        passes = sums_ref.shape[0] - 2
        for i in range(passes):
            sums_ref[i : i + 1] = jnp.where(f[3] == i, sums, 0.0)
        sums_ref[passes : passes + 1] = jnp.sum(grad * n1, axis=0, keepdims=True)
        sums_ref[passes + 1 :] = dgain_ref[...]


def assemble_first_kernel(f, d_own, d_oth, u_own, u_oth, m_own, m_oth, down_ref, up_ref, out_ref):
    step = pl.program_id(0)
    half, at = step // 4, step % 4
    for mine, d, u, m in ((True, d_own, u_own, m_own), (False, d_oth, u_oth, m_oth)):
        here = (half == f[1]) == mine

        @pl.when(here)
        def _():
            up_ref[...] = u[...].astype(F32)

        @pl.when(here & (at < 3))
        def _():
            down_ref[...] = d[...].astype(F32)

        @pl.when(here & (at == 3))
        def _():
            down_ref[...] = m[:GROUP].astype(F32)
            out_ref[...] = m[GROUP:].astype(F32)


def assemble_second_kernel(f, a_own, a_oth, b_own, b_oth, out_ref):
    for mine, a, b in ((True, a_own, b_own), (False, a_oth, b_oth)):

        @pl.when((pl.program_id(0) % 2 == f[1]) == mine)
        def _():
            out_ref[:GROUP] = a[...].astype(F32)
            out_ref[GROUP:] = b[...].astype(F32)


def swap(array, step):
    axis, mask, size, _ = step
    return lax.ppermute(array, axis, [(i, i ^ mask) for i in range(size)])


def tie(*groups):
    leaves, tree = jax.tree.flatten(groups)
    return jax.tree.unflatten(tree, lax.optimization_barrier(leaves))


def pick(here, total):
    half = total.shape[0] // 2
    low, high = total[:half], total[half:]
    return jnp.where(here == 0, high, low), jnp.where(here == 0, low, high)


def joined(here, own, other):
    return jnp.where(
        here == 0, jnp.concatenate([own, other], 0), jnp.concatenate([other, own], 0)
    )


def round_work(here, own, came, mode, riders):
    if mode == "join":
        cut = own.shape[0] - riders
        value = joined(here, own[:cut], came[:cut])
        return (jnp.concatenate([value, own[cut:] + came[cut:]], 0) if riders else value,)
    total = own + came
    return (total,) if mode == "sum" else pick(here, total)


def round_kernel(f, *refs, modes, at, riders):
    refs = list(refs)
    ins, outs = refs[: 2 * len(modes)], refs[2 * len(modes) :]
    for i, mode in enumerate(modes):
        own, came = ins[2 * i][...].astype(F32), ins[2 * i + 1][...].astype(F32)
        for value in round_work(f[at[i]], own, came, mode, riders[i]):
            outs.pop(0)[...] = value.astype(BF)


def whole_call(kernel, flags, ins, outs, name):
    vmem = pl.BlockSpec(memory_space=pltpu.VMEM)
    size = sum(math.prod(shape) for shape in [a.shape for a in ins] + outs)
    return pl.pallas_call(
        kernel,
        in_specs=[pl.BlockSpec(memory_space=pltpu.SMEM)] + [vmem] * len(ins),
        out_specs=[vmem] * len(outs),
        out_shape=[jax.ShapeDtypeStruct(shape, BF) for shape in outs],
        cost_estimate=cost(BRIEF),
        compiler_params=pltpu.CompilerParams(vmem_limit_bytes=2 * size + (8 << 20)),
        name=name,
    )(flags, *ins)


HALVE, FULL, JOIN = 0, 1, 2


class Chain:
    def __init__(self, steps, whole_steps, sent, kept):
        cut = len(steps) - whole_steps
        self.plan = (
            [(HALVE, step) for step in steps[:cut]]
            + [(FULL, step) for step in steps[cut:]]
            + [(JOIN, step) for step in reversed(steps[:cut])]
        )
        self.sent, self.kept, self.came, self.riders = sent, kept, None, 0

    def done(self):
        return not self.plan


def land(flags, chains):
    chains = [c for c in chains if c.came is not None]
    modes, at, ins, outs, riders = [], [], [], [], [c.riders for c in chains]
    for c in chains:
        what, step = c.plan.pop(0)
        own = c.kept if what == HALVE else c.sent
        rows, columns = own.shape
        if what == JOIN:
            modes.append("join")
            at.append(step[3])
            outs += [(2 * rows - c.riders, columns)]
        elif c.plan and c.plan[0][0] == HALVE:
            modes.append("split")
            at.append(c.plan[0][1][3])
            outs += [(rows // 2, columns)] * 2
        else:
            modes.append("sum")
            at.append(0)
            outs += [(rows, columns)]
        ins += [own, c.came]
    if all(shape[0] % 8 == 0 for shape in outs):
        kernel = functools.partial(round_kernel, modes=modes, at=at, riders=riders)
        results = list(whole_call(kernel, flags, ins, outs, "round"))
    else:
        results = []
        for i, mode in enumerate(modes):
            own, came = (a.astype(F32) for a in ins[2 * i : 2 * i + 2])
            results += [
                v.astype(BF) for v in round_work(flags[at[i]], own, came, mode, riders[i])
            ]
    for c, mode in zip(chains, modes, strict=True):
        c.came, c.sent = None, results.pop(0)
        if mode == "split":
            c.kept = results.pop(0)


def open_kernel(f, dd, ddr, du, dur, dw, dwr, *outs, at):
    def add(left, right):
        return left[...].astype(F32) + right[...].astype(F32)

    down, up, out = add(dd, ddr), add(du, dur), add(dw, dwr)
    cut = down.shape[0] - GROUP
    for i, value in enumerate((down[:cut], up, jnp.concatenate([down[cut:], out], 0))):
        sent, kept = pick(f[at[i]], value)
        outs[2 * i][...] = sent.astype(BF)
        outs[2 * i + 1][...] = kept.astype(BF)


def beside(chains, *more):
    chains = [c for c in chains if c.came is not None]
    arrays, more = tie([c.came for c in chains], more)
    for c, array in zip(chains, arrays, strict=True):
        c.came = array
    return more


def send(chains, *more):
    chains = [c for c in chains if not c.done()]
    loads, more = tie([c.sent for c in chains], more)
    for c, load in zip(chains, loads, strict=True):
        c.sent, c.came = load, swap(load, c.plan[0][1])
    return more


def on_device(
    sizes, block_input, segments, pass_emb, gain_attn, w_qkv, w_out, gain_mlp, w_up, w_down, cotangent
):
    passes, n_dp = sizes
    core = ("pass", 1, passes, 1)
    cross = ("pass", 2, passes, 4)
    lanes = [("dp", 1 << i, n_dp, 5 + i) for i in range(n_dp.bit_length() - 1)]
    ring = [cross] + lanes
    by_y = lanes[:1] + [cross] + lanes[:0:-1]
    orders = [ring, by_y, ring[2:] + ring[:2]]

    pass_here = lax.axis_index("pass")
    core_here = pass_here % 2
    length = segments.shape[0]
    flags = jnp.stack(
        [
            (segments[0] == segments[length - 1]).astype(jnp.int32),
            core_here.astype(jnp.int32),
            (pass_here < 2).astype(jnp.int32),
            pass_here.astype(jnp.int32),
        ]
        + [((lax.axis_index(axis) // mask) % 2).astype(jnp.int32) for axis, mask, _, _ in ring]
    )

    def to_late(array, other=0):
        return lax.ppermute(array, "pass", [(0, 2 + other), (1, 3 - other)])

    def to_early(array, other=0):
        return lax.ppermute(array, "pass", [(2, other), (3, 1 - other)])

    x, cot = block_input[0], cotangent[0]
    emb = (pass_emb.reshape(passes, 1, D), (1, 1, D), lambda i, f: (f[3], 0, 0))

    normed, theirs, low_t, high_t = call(
        norm_project_kernel,
        flags,
        (3,),
        [
            fixed(x),
            emb,
            fixed(row(gain_attn)),
            (w_qkv, (D, GROUP), lambda i, f: (0, 2 * i + 1 - f[1])),
        ],
        [out_fixed((D, length), BF)] + projection_outs(length),
        BRIEF,
        "norm_project",
    )
    other = swap(theirs, core)
    own, low_o, high_o = call(
        project_kernel,
        flags,
        (3,),
        [fixed(normed), (w_qkv, (D, GROUP), lambda i, f: (0, 2 * i + f[1]))],
        projection_outs(length),
        BRIEF,
        "project_own",
    )
    late_kv = (to_late(low_o), to_late(low_t, 1))
    early_q = (to_early(high_o), to_early(high_t, 1))
    normed_other = swap(normed, core)

    cross_in = cross_inputs(early_q, own, other, late_kv)
    pair_out = ((2, HALF, length), BF, (2, HEAD_DIM, length), lambda h, f: (0, h, 0))
    o_cross, lse_cross = call(
        cross_kernel,
        flags,
        (HALF_HEADS,),
        cross_in,
        [pair_out, lse_out(HALF_HEADS, length)],
        BRIEF,
        "attend_cross",
    )
    o_cross, lse_cross, own, other = tie(o_cross, lse_cross, own, other)
    o_back, lse_back = to_late(o_cross), to_late(lse_cross)
    local_inputs = [head(a, at) for at in (0, 6, 12) for a in (own, other)]
    o0, o1, lse_local = call(
        local_kernel,
        flags,
        (HEADS // 2,),
        local_inputs,
        [((GROUP, length), F32, (HEAD_DIM, length), lambda h, f: (h, 0))] * 2
        + [lse_out(HEADS // 2, length)],
        BRIEF,
        "attend_local",
    )
    half_rows = (HALF, length)
    att_own, att_pair, lse, att_high, lse_high = call(
        merge_kernel,
        flags,
        (2,),
        [
            (o0, half_rows, lambda i, f: (i, 0)),
            (o1, half_rows, lambda i, f: (i, 0)),
            (lse_local, (HALF_HEADS, 2, length), lambda i, f: (i, 0, 0)),
            fixed(o_cross),
            fixed(lse_cross),
            fixed(o_back),
            fixed(lse_back),
        ],
        [((GROUP, length), BF, half_rows, lambda i, f: (i, 0))] * 2
        + [
            ((HEADS // 2, 2, length), F32, (HALF_HEADS, 2, length), lambda i, f: (i, 0, 0)),
            out_fixed((2, HALF, length), BF),
            out_fixed((HALF_HEADS, 2, length), F32),
        ],
        BRIEF,
        "merge",
    )
    att_other = swap(att_pair, core)
    att_early, lse_early = to_early(att_high), to_early(lse_high)
    att_own, att_other, normed_other = tie(att_own, att_other, normed_other)

    w_half = [(w_out, (GROUP, D), lambda i, f: (f[1], 0)), (w_out, (GROUP, D), lambda i, f: (1 - f[1], 0))]
    ff_half = w_up.shape[1] // 2
    steps = ff_half // FF_TILE

    def ff_weights(at):
        return [
            (w_up, (D, FF_TILE), lambda i, f: (0, at(f) * steps + i)),
            (w_down, (FF_TILE, D), lambda i, f: (at(f) * steps + i, 0)),
        ]

    tokens = (length, D)
    residual, normed2, y_part, c_part, down_sent, up_sent = call(
        feed_first_kernel,
        flags,
        (steps,),
        [fixed(x), emb, fixed(att_own), fixed(att_other)]
        + w_half
        + [fixed(row(gain_mlp)), fixed(cot)]
        + ff_weights(lambda f: 1 - f[1]),
        [
            out_fixed(tokens, F32),
            out_fixed(tokens, BF),
            out_fixed(tokens, F32),
            out_fixed(tokens, F32),
            ((ff_half, D), BF, (FF_TILE, D), lambda i, f: (i, 0)),
            ((D, ff_half), BF, (D, FF_TILE), lambda i, f: (0, i)),
        ],
        BRIEF,
        "feed_first",
        temporaries=14,
    )
    down_sent, up_sent, att_early, lse_early = tie(down_sent, up_sent, att_early, lse_early)
    down_recv, up_recv = swap(down_sent, core), swap(up_sent, core)
    (
        down_own, up_own, output, grad_residual, g_own, g_theirs, g_own_high, g_theirs_high, dgain_mlp, out_own, out_sent
    ) = call(
        feed_second_kernel,
        flags,
        (steps,),
        [fixed(a) for a in (residual, normed2, y_part, c_part, row(gain_mlp), cot)]
        + ff_weights(lambda f: f[1])
        + w_half
        + [fixed(att_own), fixed(att_other)],
        [
            ((ff_half, D), BF, (FF_TILE, D), lambda i, f: (i, 0)),
            ((D, ff_half), BF, (D, FF_TILE), lambda i, f: (0, i)),
            out_fixed(tokens, BF),
            out_fixed(tokens, F32),
            out_fixed((GROUP, length), BF),
            out_fixed((GROUP, length), BF),
            out_fixed(half_rows, BF),
            out_fixed(half_rows, BF),
            out_fixed((1, D), F32),
            out_fixed((GROUP, D), BF),
            out_fixed((GROUP, D), BF),
        ],
        BRIEF,
        "feed_second",
        [pltpu.VMEM(tokens, F32)] * 2,
        14,
    )
    g_other = swap(g_theirs, core)
    early_g = (to_early(g_own_high), to_early(g_theirs_high, 1))
    out_recv = swap(out_sent, core)

    accumulators = [pltpu.VMEM((2, HEAD_DIM, length), F32)] * 2

    def local_back(at, heads, g0, g1):
        return call(
            local_back_kernel,
            flags,
            (heads,),
            [head(a, base + at) for base in (0, 6, 12) for a in (own, other)]
            + [head(a, at) for a in (g0, g1, att_own, att_pair)]
            + [(lse, (1, 2, length), lambda h, f: (at + h, 0, 0))],
            [((3, heads * HEAD_DIM, length), BF, (3, HEAD_DIM, length), lambda h, f: (0, h, 0))] * 2,
            BRIEF,
            "attend_back_local",
            accumulators,
        )

    d_0 = local_back(0, 2, g_own, g_other)
    d_0, early_g, out_own = tie(d_0, early_g, out_own)
    opened = whole_call(
        functools.partial(open_kernel, at=[steps_[0][3] for steps_ in orders]),
        flags,
        [down_own, down_recv, up_own, up_recv, out_own, out_recv],
        [shape for shape in (((ff_half - GROUP) // 2, D), (GROUP, ff_half), (GROUP, D)) for _ in (0, 1)],
        "open",
    )
    first = [Chain(orders[i], 1, *opened[2 * i : 2 * i + 2]) for i in range(3)]
    (early_g,) = send(first, early_g)
    dq_cross, dkv_cross = call(
        cross_back_kernel,
        flags,
        (HALF_HEADS,),
        cross_in
        + [
            head(early_g[0], 0),
            head(early_g[1], 0),
            (att_early, (2, HEAD_DIM, length), lambda h, f: (0, h, 0)),
            lse_spec(lse_early),
            head(g_own, 0),
            head(g_other, 0),
            head(att_own, 0),
            head(att_pair, 0),
            lse_spec(lse),
        ],
        [
            pair_out,
            (
                (2, 2, HALF, length),
                BF,
                (2, 2, HEAD_DIM, length),
                lambda h, f: (0, 0, h, 0),
            ),
        ],
        BRIEF,
        "attend_back_cross",
        accumulators,
    )
    dq_cross, dkv_cross, g_own, g_other = tie(dq_cross, dkv_cross, g_own, g_other)
    dq_back, dkv_back = to_late(dq_cross), to_early(dkv_cross)
    d_1 = local_back(2, 2, g_own, g_other)
    (d_1,) = beside(first, d_1)
    land(flags, first)
    g_own, g_other = send(first, g_own, g_other)
    d_2 = local_back(4, 2, g_own, g_other)
    d_2, dq_back, dkv_back = beside(first, d_2, dq_back, dkv_back)
    land(flags, first)
    d_2, dq_back, dkv_back = send(first, d_2, dq_back, dkv_back)
    few = (1, 2 * HEAD_DIM, length)
    one_q = (1, 2, HALF, length)
    gp_own, gp_pair = call(
        combine_kernel,
        flags,
        (3,),
        [(d, few, lambda i, f: (i, 0, 0)) for d in (*d_0, *d_1, *d_2)]
        + [
            fixed(dq_cross.reshape(one_q)),
            fixed(dq_back.reshape(one_q)),
            (dkv_cross, one_q, lambda i, f: (jnp.maximum(i - 1, 0), 0, 0, 0)),
            (dkv_back, one_q, lambda i, f: (jnp.maximum(i - 1, 0), 0, 0, 0)),
        ],
        [((3 * GROUP, length), BF, (GROUP, length), lambda i, f: (i, 0))] * 2,
        BRIEF,
        "combine",
    )
    gp_other = swap(gp_pair, core)
    opened = call(
        functools.partial(project_grad_kernel, at=[ring[0][3], by_y[0][3]]),
        flags,
        (3,),
        [(g, (GROUP, length), lambda i, f: (i, 0)) for g in (gp_own, gp_pair)]
        + [fixed(normed), fixed(normed_other)],
        [((D // 4, 3 * GROUP), BF, (D // 4, GROUP), lambda i, f: (0, i))] * 4,
        BRIEF,
        "project_grad",
    )
    gp_own, gp_other, opened = beside(first, gp_own, gp_other, opened)
    second = [Chain(order, 2, *opened[2 * i : 2 * i + 2]) for i, order in enumerate((ring, lanes[:1] + [cross] + lanes[1:]))]
    land(flags, first)
    send(first + second)
    land(flags, first + second)
    gp_own, gp_other = send(first + second, gp_own, gp_other)
    grad_input, sums = call(
        input_grad_kernel,
        flags,
        (3,),
        [
            (gp_own, (GROUP, length), lambda i, f: (i, 0)),
            (gp_other, (GROUP, length), lambda i, f: (i, 0)),
            (w_qkv, (D, GROUP), lambda i, f: (0, 2 * i + f[1])),
            (w_qkv, (D, GROUP), lambda i, f: (0, 2 * i + 1 - f[1])),
            fixed(x),
            emb,
            fixed(row(gain_attn)),
            fixed(grad_residual),
            fixed(dgain_mlp),
        ],
        [out_fixed(tokens, BF), out_fixed((passes + 2, D), F32)],
        BRIEF,
        "input_grad",
        [pltpu.VMEM((D, length), F32)],
    )
    grad_input, sums = beside(first + second, grad_input, sums)
    land(flags, first + second)
    while second[1].plan[0][0] == HALVE:
        send(first + second)
        land(flags, first + second)
    rider = jnp.pad(sums, ((0, 8 - passes - 2), (0, 3 * GROUP - D))).astype(BF)
    second[1].sent, second[1].riders = jnp.concatenate([second[1].sent, rider]), 8
    while not first[0].done():
        send(first + second)
        land(flags, first + second)
    send(second)
    pairs = [(c.sent, swap(c.sent, core)) for c in first]
    (pairs,) = beside(second, pairs)
    land(flags, second)
    third = [a for pair in pairs for a in pair]
    at_most = [
        (third[i], (GROUP, D), lambda j, f: (jnp.minimum(j % 4, 2), 0)) for i in (0, 1)
    ] + [(third[i], (D, GROUP), lambda j, f: (0, j % 4)) for i in (2, 3)]
    down_total, up_total, out_total = call(
        assemble_first_kernel,
        flags,
        (8,),
        at_most + [fixed(third[4]), fixed(third[5])],
        [
            ((4 * D, D), F32, (GROUP, D), lambda j, f: (j, 0)),
            ((D, 4 * D), F32, (D, GROUP), lambda j, f: (0, j)),
            ((D, D), F32, (GROUP, D), lambda j, f: (j // 4, 0)),
        ],
        BRIEF,
        "assemble_first",
    )
    while not second[0].done():
        send(second)
        down_total, up_total, out_total = beside(second, down_total, up_total, out_total)
        land(flags, second)
    lasts = [(c.sent, swap(c.sent, core)) for c in second]
    small = sum(a[D // 2 :, :D].astype(F32) for a in lasts[1])
    qkv_total = call(
        assemble_second_kernel,
        flags,
        (6,),
        [
            (a, (GROUP, GROUP), lambda j, f: (0, j // 2))
            for pair in lasts
            for a in pair
        ],
        [((D, 3 * D), F32, (D, GROUP), lambda j, f: (0, j))],
        BRIEF,
        "assemble_second",
    )[0]
    return (
        output[None],
        grad_input[None],
        small[:passes],
        small[passes],
        qkv_total,
        out_total,
        small[passes + 1],
        up_total,
        down_total,
    )


def solution(mesh):
    sizes = (mesh.shape["pass"], mesh.shape["dp"])
    tokens = P("pass", "dp", None)
    in_specs = (tokens, P("dp")) + (P(),) * 7 + (tokens,)
    out_specs = (tokens, tokens) + (P(),) * 7
    return jax.shard_map(
        functools.partial(on_device, sizes),
        mesh=mesh,
        in_specs=in_specs,
        out_specs=out_specs,
        check_vma=False,
    )
```

```python
import functools
import math

import jax
import jax.numpy as jnp
from jax import lax
from jax.experimental import pallas as pl
from jax.experimental.pallas import tpu as pltpu
from jax.sharding import PartitionSpec as P

D = 768
HEADS = 12
HEAD_DIM = 64
SHORT = 256
FF_TILE = 512
GROUP = D // 2
HALF = GROUP // 2
HALF_HEADS = HEADS // 4
EPS = 1e-05
SCALE = HEAD_DIM**-0.5
SCALE2 = SCALE * math.log2(math.e)
BF = jnp.bfloat16
F32 = jnp.float32
BRIEF = 0.2


def dot(a, b, ca, cb):
    return lax.dot_general(a, b, (((ca,), (cb,)), ((), ())), preferred_element_type=F32)


def cost(us):
    return pl.CostEstimate(flops=int(us * 1.1e9), bytes_accessed=1 << 20, transcendentals=0)


def call(kernel, flags, grid, ins, outs, us, name, scratch=(), temporaries=8):
    blocks = [(math.prod(block), array.dtype) for array, block, index in ins if index]
    blocks += [(math.prod(block), dtype) for _, dtype, block, index in outs if index]
    blocks += [(math.prod(buffer.shape) // 2, buffer.dtype) for buffer in scratch]
    limit = sum(2 * n * jnp.dtype(dtype).itemsize for n, dtype in blocks) + (temporaries << 20)
    return pl.pallas_call(
        kernel,
        grid_spec=pltpu.PrefetchScalarGridSpec(
            num_scalar_prefetch=1,
            grid=grid,
            in_specs=[spec(block, index) for _, block, index in ins],
            out_specs=[spec(block, index) for _, _, block, index in outs],
            scratch_shapes=list(scratch),
        ),
        out_shape=[jax.ShapeDtypeStruct(shape, dtype) for shape, dtype, _, _ in outs],
        cost_estimate=cost(us),
        compiler_params=pltpu.CompilerParams(vmem_limit_bytes=min(limit, 60 << 20)),
        name=name,
    )(flags, *[array for array, _, _ in ins])


def fixed(array):
    return (array, array.shape, lambda i, f: (0,) * array.ndim)


def out_fixed(shape, dtype):
    return (shape, dtype, shape, lambda i, f: (0,) * len(shape))


def held(array):
    return (array, array.shape, None)


def out_held(shape, dtype):
    return (shape, dtype, shape, None)


def spec(block, index):
    return pl.BlockSpec(block, index) if index else pl.BlockSpec(memory_space=pltpu.VMEM)


def row(vector):
    return vector.reshape(1, -1)


def one_sequence(f):
    return f[0] == 1


def hidden_of(x_ref, emb_ref):
    return x_ref[...].astype(F32) + emb_ref[0]


def centered(values):
    center = values - jnp.mean(values, axis=-1, keepdims=True)
    return center, lax.rsqrt(jnp.mean(center * center, axis=-1, keepdims=True) + EPS)


def write_part(part, out_ref, low_ref, high_ref, value):
    out_ref[...] = value

    @pl.when(part == 0)
    def _():
        high_ref[...] = value[HALF:]

    @pl.when(part > 0)
    def _():
        low_ref[pl.ds(pl.multiple_of((part - 1) * HALF, HALF), HALF), :] = value[:HALF]


def norm_project_kernel(f, x_ref, emb_ref, gain_ref, w_ref, normed_ref, out_ref, low_ref, high_ref):
    part = pl.program_id(0)

    @pl.when(part == 0)
    def _():
        center, inv = centered(hidden_of(x_ref, emb_ref))
        normed_ref[...] = (center * inv * gain_ref[...]).T.astype(BF)

    value = dot(w_ref[...], normed_ref[...], 0, 0).astype(BF)
    write_part(part, out_ref, low_ref, high_ref, value)


def project_kernel(f, normed_ref, w_ref, out_ref, low_ref, high_ref):
    value = dot(w_ref[...], normed_ref[...], 0, 0).astype(BF)
    write_part(pl.program_id(0), out_ref, low_ref, high_ref, value)


def projection_outs(length):
    return [
        ((3 * GROUP, length), BF, (GROUP, length), lambda i, f: (i, 0)),
        out_fixed((2 * HALF, length), BF),
        out_fixed((HALF, length), BF),
    ]


def mask_tail(scores):
    n = scores.shape[0]
    key = lax.broadcasted_iota(jnp.int32, (SHORT, SHORT), 0)
    query = lax.broadcasted_iota(jnp.int32, (SHORT, SHORT), 1)
    diag = jnp.where(key <= query, scores[n - SHORT :], -1e30)
    return diag if n == SHORT else jnp.concatenate([scores[: n - SHORT], diag], 0)


def sweep(f, length, tile, variants):
    for condition, units in variants:
        for whole in (True, False):

            @pl.when(condition & (one_sequence(f) == whole))
            def _():
                for at in range(length // SHORT):
                    for unit in units:
                        tile(unit, at, 0 if whole else at)


def spans(at, first):
    return slice(at * SHORT, (at + 1) * SHORT), slice(first * SHORT, (at + 1) * SHORT)


def softmax_tile(q_refs, k_refs, v_refs, o_refs, lse_ref, unit, at, first):
    qp, keys = unit
    qs, ks = spans(at, first)
    q = q_refs[qp][:, qs]
    scores = [mask_tail(dot(k_refs[kp][:, ks], q, 0, 0) * SCALE2) for kp in keys]
    top = functools.reduce(jnp.maximum, [jnp.max(s, axis=0, keepdims=True) for s in scores])
    raw = [jnp.exp2(s - top) for s in scores]
    total = functools.reduce(jnp.add, [jnp.sum(p, axis=0, keepdims=True) for p in raw])
    out = functools.reduce(
        jnp.add, [dot(v_refs[kp][:, ks], p.astype(BF), 1, 0) for kp, p in zip(keys, raw)]
    )
    o_refs[qp][:, qs] = (out * (1.0 / total)).astype(o_refs[qp].dtype)
    lse_ref[0, qp : qp + 1, qs] = top + jnp.log2(total)


LOCAL_UNITS = (
    lambda f: (f[1] == 0, [(0, [0]), (1, [0, 1])]),
    lambda f: (f[1] == 1, [(1, [1]), (0, [0, 1])]),
)
CROSS_UNITS = [(0, [0, 1]), (1, [0, 1])]


def local_kernel(f, q0, q1, k0, k1, v0, v1, o0, o1, lse_ref):
    sweep(
        f,
        q0.shape[1],
        functools.partial(softmax_tile, (q0, q1), (k0, k1), (v0, v1), (o0, o1), lse_ref),
        [unit(f) for unit in LOCAL_UNITS],
    )


def cross_kernel(f, *refs):
    ins, (o_ref, lse_ref) = refs[:12], refs[12:]
    outs = (o_ref.at[0], o_ref.at[1])
    for early, at in ((1, 0), (0, 6)):
        q0, q1, k0, k1, v0, v1 = ins[at : at + 6]
        sweep(
            f,
            q0.shape[1],
            functools.partial(softmax_tile, (q0, q1), (k0, k1), (v0, v1), outs, lse_ref),
            [(f[2] == early, CROSS_UNITS)],
        )


def head(array, at):
    return (array, (HEAD_DIM, array.shape[-1]), lambda h, f: (at + h, 0))


def lse_spec(array):
    return (array, (1,) + array.shape[1:], lambda h, f: (h, 0, 0))


def lse_out(heads, length):
    return ((heads, 2, length), F32, (1, 2, length), lambda h, f: (h, 0, 0))


def cross_inputs(early_q, own, other, late_kv):
    return [
        head(early_q[0], 0),
        head(early_q[1], 0),
        head(own, 6 + HALF_HEADS),
        head(other, 6 + HALF_HEADS),
        head(own, 12 + HALF_HEADS),
        head(other, 12 + HALF_HEADS),
        head(own, 0),
        head(other, 0),
        head(late_kv[0], 0),
        head(late_kv[1], 0),
        head(late_kv[0], HALF_HEADS),
        head(late_kv[1], HALF_HEADS),
    ]


def merge_kernel(f, o0, o1, lse_ref, oc_ref, lsec_ref, ob_ref, lseb_ref, a0, a1, lse_out_ref, high_ref, lse_high_ref):
    half = pl.program_id(0)

    def finish(values, lse):
        for i, ref in ((0, a0), (1, a1)):
            ref[...] = values[i].astype(BF)
        lse_out_ref[...] = lse
        for i in (0, 1):
            high_ref[i] = values[i].astype(BF)
        lse_high_ref[...] = lse

    @pl.when(f[2] == 1)
    def _():
        finish((o0[...], o1[...]), lse_ref[...])

    @pl.when(f[2] == 0)
    def _():
        low = half == 0
        lse_c = jnp.where(low, lsec_ref[...], lseb_ref[...])
        lse_l = lse_ref[...]
        top = jnp.maximum(lse_l, lse_c)
        lse = top + jnp.log2(jnp.exp2(lse_l - top) + jnp.exp2(lse_c - top))
        share_l, share_c = jnp.exp2(lse_l - lse), jnp.exp2(lse_c - lse)
        values = []
        for i, ref in ((0, o0), (1, o1)):
            other = jnp.where(low, oc_ref[i], ob_ref[i]).astype(F32)
            rows = []
            for h in range(HALF_HEADS):
                at = slice(h * HEAD_DIM, (h + 1) * HEAD_DIM)
                rows.append(
                    ref[at, :] * share_l[h, i : i + 1] + other[at] * share_c[h, i : i + 1]
                )
            values.append(jnp.concatenate(rows, 0))
        finish(values, lse)


def gradient_tile(
    q_refs, k_refs, v_refs, g_refs, o_refs, lse_ref, dq_refs, dk_acc, dv_acc, unit, at, first
):
    qp, keys = unit
    qs, ks = spans(at, first)
    q, g = q_refs[qp][:, qs], g_refs[qp][:, qs]
    lse = lse_ref[0, qp : qp + 1, qs]
    delta = jnp.sum(g.astype(F32) * o_refs[qp][:, qs].astype(F32), axis=0, keepdims=True)
    dq = None
    for kp in keys:
        k, v = k_refs[kp][:, ks], v_refs[kp][:, ks]
        weights = jnp.exp2(mask_tail(dot(k, q, 0, 0) * SCALE2) - lse)
        ds = (weights * (dot(v, g, 0, 0) - delta)).astype(BF)
        term = dot(k, ds, 1, 0)
        dq = term if dq is None else dq + term
        dk_acc[kp, :, ks] += dot(q, ds, 1, 1)
        dv_acc[kp, :, ks] += dot(g, weights.astype(BF), 1, 1)
    dq_refs[qp][:, qs] = (dq * SCALE).astype(BF)


def local_back_kernel(
    f, q0, q1, k0, k1, v0, v1, g0, g1, o0, o1, lse_ref, d0, d1, dk_acc, dv_acc
):
    dk_acc[...] = jnp.zeros_like(dk_acc)
    dv_acc[...] = jnp.zeros_like(dv_acc)
    sweep(
        f,
        q0.shape[1],
        functools.partial(
            gradient_tile,
            (q0, q1),
            (k0, k1),
            (v0, v1),
            (g0, g1),
            (o0, o1),
            lse_ref,
            (d0.at[0], d1.at[0]),
            dk_acc,
            dv_acc,
        ),
        [unit(f) for unit in LOCAL_UNITS],
    )
    for i, ref in ((0, d0), (1, d1)):
        ref[1] = (dk_acc[i] * SCALE).astype(BF)
        ref[2] = dv_acc[i].astype(BF)


def cross_back_kernel(f, *refs):
    ins, more = refs[:12], refs[12:]
    (ga0, ga1, oa, lse_a, gb0, gb1, ob0, ob1, lse_b, dq_ref, dkv_ref, dk_acc, dv_acc) = more
    dk_acc[...] = jnp.zeros_like(dk_acc)
    dv_acc[...] = jnp.zeros_like(dv_acc)
    for early, at, grads, outs, lse_ref in (
        (1, 0, (ga0, ga1), (oa.at[0], oa.at[1]), lse_a),
        (0, 6, (gb0, gb1), (ob0, ob1), lse_b),
    ):
        q0, q1, k0, k1, v0, v1 = ins[at : at + 6]
        sweep(
            f,
            q0.shape[1],
            functools.partial(
                gradient_tile,
                (q0, q1),
                (k0, k1),
                (v0, v1),
                grads,
                outs,
                lse_ref,
                (dq_ref.at[0], dq_ref.at[1]),
                dk_acc,
                dv_acc,
            ),
            [(f[2] == early, CROSS_UNITS)],
        )
    for i in (0, 1):
        dkv_ref[0, i] = (dk_acc[i] * SCALE).astype(BF)
        dkv_ref[1, i] = dv_acc[i].astype(BF)


def gelu_pair(u):
    k = math.sqrt(2 / math.pi)
    square = u * u
    t = jnp.tanh(k * u * (1.0 + 0.044715 * square))
    half = 0.5 + 0.5 * t
    slope = half + 0.5 * u * (1.0 - t * t) * (k * (1.0 + 3 * 0.044715 * square))
    return u * half, slope


def chunks(length):
    return [slice(at, at + SHORT) for at in range(0, length, SHORT)]


def ff_tile(n_ref, cot_ref, wu_ref, wd_ref, y_ref, c_ref, act_ref, gup_ref):
    for at in chunks(n_ref.shape[0]):
        act, slope = gelu_pair(dot(n_ref[at], wu_ref[...], 1, 0))
        act = act.astype(BF)
        grad_up = (dot(cot_ref[at], wd_ref[...], 1, 1) * slope).astype(BF)
        act_ref[at], gup_ref[at] = act, grad_up
        y_ref[at] += dot(act, wd_ref[...], 1, 0)
        c_ref[at] += dot(grad_up, wu_ref[...], 1, 1)


def feed_kernel(
    f, x_ref, emb_ref, a_ref, b_ref, wa_ref, wb_ref, gain_ref, cot_ref, wu_ref, wd_ref,
    dds_ref, dus_ref, ddo_ref, duo_ref, out_ref, gres_ref, ga_ref, gb_ref, gah_ref, gbh_ref, dgain_ref, dwa_ref, dwb_ref,
    res_ref, n_ref, y_ref, c_ref, act_ref, gup_ref,
):
    step, steps = pl.program_id(0), pl.num_programs(0)

    @pl.when(step == 0)
    def _():
        for at in chunks(n_ref.shape[0]):
            residual = (
                x_ref[at].astype(F32)
                + emb_ref[0]
                + dot(a_ref[:, at], wa_ref[...], 0, 0)
                + dot(b_ref[:, at], wb_ref[...], 0, 0)
            )
            res_ref[at] = residual
            center, inv = centered(residual)
            n_ref[at] = (center * inv * gain_ref[...]).astype(BF)
            y_ref[at] = residual
            c_ref[at] = jnp.zeros_like(residual)

    ff_tile(n_ref, cot_ref, wu_ref, wd_ref, y_ref, c_ref, act_ref, gup_ref)
    down = dot(act_ref[...], cot_ref[...], 0, 0).astype(BF)
    up = dot(n_ref[...], gup_ref[...], 0, 0).astype(BF)

    @pl.when(step < steps // 2)
    def _():
        dds_ref[...], dus_ref[...] = down, up

    @pl.when(step >= steps // 2)
    def _():
        ddo_ref[...], duo_ref[...] = down, up

    @pl.when(step == steps - 1)
    def _():
        dgain = None
        grads = []
        for at in chunks(n_ref.shape[0]):
            out_ref[at] = y_ref[at].astype(BF)
            center, inv = centered(res_ref[at])
            n2 = center * inv
            c = c_ref[at]
            part = jnp.sum(c * n2, axis=0, keepdims=True)
            dgain = part if dgain is None else dgain + part
            e = c * gain_ref[...]
            grad = cot_ref[at].astype(F32) + inv * (
                e
                - jnp.mean(e, axis=-1, keepdims=True)
                - n2 * jnp.mean(e * n2, axis=-1, keepdims=True)
            )
            gres_ref[at] = grad
            grad = grad.astype(BF)
            grads.append(grad)
            mine = dot(wa_ref[...], grad, 1, 1).astype(BF)
            theirs = dot(wb_ref[...], grad, 1, 1).astype(BF)
            ga_ref[:, at], gb_ref[:, at] = mine, theirs
            gah_ref[:, at], gbh_ref[:, at] = mine[HALF:], theirs[HALF:]
        dgain_ref[...] = dgain
        grad = jnp.concatenate(grads, 0)
        dwa_ref[...] = dot(a_ref[...], grad, 1, 0).astype(BF)
        dwb_ref[...] = dot(b_ref[...], grad, 1, 0).astype(BF)


def combine_kernel(f, da0, da1, db0, db1, dc0, dc1, dqc_ref, dqb_ref, dkvc_ref, dkvb_ref, g0, g1):
    part = pl.program_id(0)
    late, early = f[2] == 0, f[2] == 1

    def put(low, high):
        for i, (refs, g) in enumerate((((da0, db0, dc0), g0), ((da1, db1, dc1), g1))):
            local = jnp.concatenate([d[0] for d in refs], 0)
            if low is None:
                g[...] = local
            else:
                more = jnp.concatenate([low[0, i], high[0, i]], 0)
                g[...] = (local.astype(F32) + more.astype(F32)).astype(BF)

    @pl.when(late & (part == 0))
    def _():
        put(dqc_ref, dqb_ref)

    @pl.when(early & (part > 0))
    def _():
        put(dkvb_ref, dkvc_ref)

    @pl.when((late & (part > 0)) | (early & (part == 0)))
    def _():
        put(None, None)


def project_grad_kernel(f, g0, g1, n0_ref, n1_ref, s0_ref, k0_ref, s1_ref, k1_ref, *, at):
    value = dot(n0_ref[...], g0[...], 1, 1) + dot(n1_ref[...], g1[...], 1, 1)
    for i, (sent_ref, kept_ref) in enumerate(((s0_ref, k0_ref), (s1_ref, k1_ref))):
        sent, kept = pick(f[at[i]], value[i * (D // 2) : (i + 1) * (D // 2)])
        sent_ref[...] = sent.astype(BF)
        kept_ref[...] = kept.astype(BF)


def input_grad_kernel(
    f, g_ref, h_ref, wg_ref, wh_ref, x_ref, emb_ref, gain_ref, gres_ref, dgain_ref, gin_ref, sums_ref, acc
):
    part = pl.program_id(0)
    value = dot(wg_ref[...], g_ref[...], 1, 0) + dot(wh_ref[...], h_ref[...], 1, 0)

    @pl.when(part == 0)
    def _():
        acc[...] = value

    @pl.when(part > 0)
    def _():
        acc[...] += value

    @pl.when(part == pl.num_programs(0) - 1)
    def _():
        center, inv = centered(hidden_of(x_ref, emb_ref))
        n1 = center * inv
        grad = acc[...].T
        e = grad * gain_ref[...]
        total = gres_ref[...] + inv * (
            e - jnp.mean(e, axis=-1, keepdims=True) - n1 * jnp.mean(e * n1, axis=-1, keepdims=True)
        )
        gin_ref[...] = total.astype(BF)
        sums = jnp.sum(total, axis=0, keepdims=True)
        passes = sums_ref.shape[0] - 2
        for i in range(passes):
            sums_ref[i : i + 1] = jnp.where(f[3] == i, sums, 0.0)
        sums_ref[passes : passes + 1] = jnp.sum(grad * n1, axis=0, keepdims=True)
        sums_ref[passes + 1 :] = dgain_ref[...]


def assemble_first_kernel(f, d_own, d_oth, u_own, u_oth, m_own, m_oth, down_ref, up_ref, out_ref):
    step = pl.program_id(0)
    half, at = step // 4, step % 4
    for mine, d, u, m in ((True, d_own, u_own, m_own), (False, d_oth, u_oth, m_oth)):
        here = (half == f[1]) == mine

        @pl.when(here)
        def _():
            up_ref[...] = u[...].astype(F32)

        @pl.when(here & (at < 3))
        def _():
            down_ref[...] = d[...].astype(F32)

        @pl.when(here & (at == 3))
        def _():
            down_ref[...] = m[:GROUP].astype(F32)
            out_ref[...] = m[GROUP:].astype(F32)


def assemble_second_kernel(f, a_own, a_oth, b_own, b_oth, out_ref):
    for mine, a, b in ((True, a_own, b_own), (False, a_oth, b_oth)):

        @pl.when((pl.program_id(0) % 2 == f[1]) == mine)
        def _():
            out_ref[:GROUP] = a[...].astype(F32)
            out_ref[GROUP:] = b[...].astype(F32)


def swap(array, step):
    axis, mask, size, _ = step
    return lax.ppermute(array, axis, [(i, i ^ mask) for i in range(size)])


def tie(*groups):
    leaves, tree = jax.tree.flatten(groups)
    return jax.tree.unflatten(tree, lax.optimization_barrier(leaves))


def pick(here, total):
    half = total.shape[0] // 2
    low, high = total[:half], total[half:]
    return jnp.where(here == 0, high, low), jnp.where(here == 0, low, high)


def joined(here, own, other):
    return jnp.where(
        here == 0, jnp.concatenate([own, other], 0), jnp.concatenate([other, own], 0)
    )


def round_work(here, own, came, mode, riders):
    if mode == "join":
        cut = own.shape[0] - riders
        value = joined(here, own[:cut], came[:cut])
        return (jnp.concatenate([value, own[cut:] + came[cut:]], 0) if riders else value,)
    total = own + came
    return (total,) if mode == "sum" else pick(here, total)


def round_kernel(f, *refs, modes, at, riders):
    refs = list(refs)
    ins, outs = refs[: 2 * len(modes)], refs[2 * len(modes) :]
    for i, mode in enumerate(modes):
        own, came = ins[2 * i][...].astype(F32), ins[2 * i + 1][...].astype(F32)
        for value in round_work(f[at[i]], own, came, mode, riders[i]):
            outs.pop(0)[...] = value.astype(BF)


def whole_call(kernel, flags, ins, outs, name):
    vmem = pl.BlockSpec(memory_space=pltpu.VMEM)
    size = sum(math.prod(shape) for shape in [a.shape for a in ins] + outs)
    return pl.pallas_call(
        kernel,
        in_specs=[pl.BlockSpec(memory_space=pltpu.SMEM)] + [vmem] * len(ins),
        out_specs=[vmem] * len(outs),
        out_shape=[jax.ShapeDtypeStruct(shape, BF) for shape in outs],
        cost_estimate=cost(BRIEF),
        compiler_params=pltpu.CompilerParams(vmem_limit_bytes=2 * size + (8 << 20)),
        name=name,
    )(flags, *ins)


HALVE, FULL, JOIN = 0, 1, 2


class Chain:
    def __init__(self, steps, whole_steps, sent, kept):
        cut = len(steps) - whole_steps
        self.plan = (
            [(HALVE, step) for step in steps[:cut]]
            + [(FULL, step) for step in steps[cut:]]
            + [(JOIN, step) for step in reversed(steps[:cut])]
        )
        self.sent, self.kept, self.came, self.riders = sent, kept, None, 0

    def done(self):
        return not self.plan


def land(flags, chains):
    chains = [c for c in chains if c.came is not None]
    modes, at, ins, outs, riders = [], [], [], [], [c.riders for c in chains]
    for c in chains:
        what, step = c.plan.pop(0)
        own = c.kept if what == HALVE else c.sent
        rows, columns = own.shape
        if what == JOIN:
            modes.append("join")
            at.append(step[3])
            outs += [(2 * rows - c.riders, columns)]
        elif c.plan and c.plan[0][0] == HALVE:
            modes.append("split")
            at.append(c.plan[0][1][3])
            outs += [(rows // 2, columns)] * 2
        else:
            modes.append("sum")
            at.append(0)
            outs += [(rows, columns)]
        ins += [own, c.came]
    if all(shape[0] % 8 == 0 for shape in outs):
        kernel = functools.partial(round_kernel, modes=modes, at=at, riders=riders)
        results = list(whole_call(kernel, flags, ins, outs, "round"))
    else:
        results = []
        for i, mode in enumerate(modes):
            own, came = (a.astype(F32) for a in ins[2 * i : 2 * i + 2])
            results += [
                v.astype(BF) for v in round_work(flags[at[i]], own, came, mode, riders[i])
            ]
    for c, mode in zip(chains, modes, strict=True):
        c.came, c.sent = None, results.pop(0)
        if mode == "split":
            c.kept = results.pop(0)


def open_kernel(f, dd, ddr, du, dur, dw, dwr, *outs, at):
    def add(left, right):
        return left[...].astype(F32) + right[...].astype(F32)

    down, up, out = add(dd, ddr), add(du, dur), add(dw, dwr)
    cut = down.shape[0] - GROUP
    for i, value in enumerate((down[:cut], up, jnp.concatenate([down[cut:], out], 0))):
        sent, kept = pick(f[at[i]], value)
        outs[2 * i][...] = sent.astype(BF)
        outs[2 * i + 1][...] = kept.astype(BF)


def beside(chains, *more):
    chains = [c for c in chains if c.came is not None]
    arrays, more = tie([c.came for c in chains], more)
    for c, array in zip(chains, arrays, strict=True):
        c.came = array
    return more


def send(chains, *more):
    chains = [c for c in chains if not c.done()]
    loads, more = tie([c.sent for c in chains], more)
    for c, load in zip(chains, loads, strict=True):
        c.sent, c.came = load, swap(load, c.plan[0][1])
    return more


def on_device(
    sizes, block_input, segments, pass_emb, gain_attn, w_qkv, w_out, gain_mlp, w_up, w_down, cotangent
):
    passes, n_dp = sizes
    core = ("pass", 1, passes, 1)
    cross = ("pass", 2, passes, 4)
    lanes = [("dp", 1 << i, n_dp, 5 + i) for i in range(n_dp.bit_length() - 1)]
    ring = [cross] + lanes
    by_y = lanes[:1] + [cross] + lanes[:0:-1]
    orders = [ring, by_y, ring[2:] + ring[:2]]

    pass_here = lax.axis_index("pass")
    core_here = pass_here % 2
    length = segments.shape[0]
    flags = jnp.stack(
        [
            (segments[0] == segments[length - 1]).astype(jnp.int32),
            core_here.astype(jnp.int32),
            (pass_here < 2).astype(jnp.int32),
            pass_here.astype(jnp.int32),
        ]
        + [((lax.axis_index(axis) // mask) % 2).astype(jnp.int32) for axis, mask, _, _ in ring]
    )

    def to_late(array, other=0):
        return lax.ppermute(array, "pass", [(0, 2 + other), (1, 3 - other)])

    def to_early(array, other=0):
        return lax.ppermute(array, "pass", [(2, other), (3, 1 - other)])

    x, cot = block_input[0], cotangent[0]
    emb = (pass_emb.reshape(passes, 1, D), (1, 1, D), lambda i, f: (f[3], 0, 0))

    normed, theirs, low_t, high_t = call(
        norm_project_kernel,
        flags,
        (3,),
        [
            fixed(x),
            emb,
            fixed(row(gain_attn)),
            (w_qkv, (D, GROUP), lambda i, f: (0, 2 * i + 1 - f[1])),
        ],
        [out_fixed((D, length), BF)] + projection_outs(length),
        BRIEF,
        "norm_project",
    )
    other = swap(theirs, core)
    own, low_o, high_o = call(
        project_kernel,
        flags,
        (3,),
        [fixed(normed), (w_qkv, (D, GROUP), lambda i, f: (0, 2 * i + f[1]))],
        projection_outs(length),
        BRIEF,
        "project_own",
    )
    late_kv = (to_late(low_o), to_late(low_t, 1))
    early_q = (to_early(high_o), to_early(high_t, 1))
    normed_other = swap(normed, core)

    cross_in = cross_inputs(early_q, own, other, late_kv)
    pair_out = ((2, HALF, length), BF, (2, HEAD_DIM, length), lambda h, f: (0, h, 0))
    o_cross, lse_cross = call(
        cross_kernel,
        flags,
        (HALF_HEADS,),
        cross_in,
        [pair_out, lse_out(HALF_HEADS, length)],
        BRIEF,
        "attend_cross",
    )
    o_cross, lse_cross, own, other = tie(o_cross, lse_cross, own, other)
    o_back, lse_back = to_late(o_cross), to_late(lse_cross)
    local_inputs = [head(a, at) for at in (0, 6, 12) for a in (own, other)]
    o0, o1, lse_local = call(
        local_kernel,
        flags,
        (HEADS // 2,),
        local_inputs,
        [((GROUP, length), F32, (HEAD_DIM, length), lambda h, f: (h, 0))] * 2
        + [lse_out(HEADS // 2, length)],
        BRIEF,
        "attend_local",
    )
    half_rows = (HALF, length)
    att_own, att_pair, lse, att_high, lse_high = call(
        merge_kernel,
        flags,
        (2,),
        [
            (o0, half_rows, lambda i, f: (i, 0)),
            (o1, half_rows, lambda i, f: (i, 0)),
            (lse_local, (HALF_HEADS, 2, length), lambda i, f: (i, 0, 0)),
            fixed(o_cross),
            fixed(lse_cross),
            fixed(o_back),
            fixed(lse_back),
        ],
        [((GROUP, length), BF, half_rows, lambda i, f: (i, 0))] * 2
        + [
            ((HEADS // 2, 2, length), F32, (HALF_HEADS, 2, length), lambda i, f: (i, 0, 0)),
            out_fixed((2, HALF, length), BF),
            out_fixed((HALF_HEADS, 2, length), F32),
        ],
        BRIEF,
        "merge",
    )
    att_other = swap(att_pair, core)
    att_early, lse_early = to_early(att_high), to_early(lse_high)
    att_own, att_other, normed_other = tie(att_own, att_other, normed_other)

    w_half = [(w_out, (GROUP, D), lambda i, f: (f[1], 0)), (w_out, (GROUP, D), lambda i, f: (1 - f[1], 0))]
    ff_half = w_up.shape[1] // 2
    steps = ff_half // FF_TILE

    def tile_at(i, f):
        return jnp.where(i < steps, 1 - f[1], f[1]) * steps + i % steps

    sent_at, own_at = lambda i: jnp.minimum(i, steps - 1), lambda i: jnp.maximum(i - steps, 0)
    tokens = (length, D)
    (
        down_sent, up_sent, down_own, up_own, output, grad_residual, g_own, g_theirs, g_own_high, g_theirs_high,
        dgain_mlp, out_own, out_sent,
    ) = call(
        feed_kernel,
        flags,
        (2 * steps,),
        [held(x), emb, held(att_own), held(att_other)]
        + w_half
        + [held(row(gain_mlp)), held(cot)]
        + [
            (w_up, (D, FF_TILE), lambda i, f: (0, tile_at(i, f))),
            (w_down, (FF_TILE, D), lambda i, f: (tile_at(i, f), 0)),
        ],
        [
            ((ff_half, D), BF, (FF_TILE, D), lambda i, f: (sent_at(i), 0)),
            ((D, ff_half), BF, (D, FF_TILE), lambda i, f: (0, sent_at(i))),
            ((ff_half, D), BF, (FF_TILE, D), lambda i, f: (own_at(i), 0)),
            ((D, ff_half), BF, (D, FF_TILE), lambda i, f: (0, own_at(i))),
            (tokens, BF, tokens, lambda i, f: (0, 0)),
            (tokens, F32, tokens, lambda i, f: (0, 0)),
            out_held((GROUP, length), BF),
            out_held((GROUP, length), BF),
            out_held(half_rows, BF),
            out_held(half_rows, BF),
            out_held((1, D), F32),
            out_held((GROUP, D), BF),
            out_held((GROUP, D), BF),
        ],
        BRIEF,
        "feed",
        [pltpu.VMEM(tokens, F32), pltpu.VMEM(tokens, BF)]
        + [pltpu.VMEM(tokens, F32)] * 2
        + [pltpu.VMEM((length, FF_TILE), BF)] * 2,
        6,
    )
    (
        down_sent, up_sent, down_own, up_own, output, grad_residual, g_own, g_theirs, g_own_high, g_theirs_high,
        dgain_mlp, out_own, out_sent, att_early, lse_early,
    ) = tie(
        down_sent, up_sent, down_own, up_own, output, grad_residual, g_own, g_theirs, g_own_high, g_theirs_high,
        dgain_mlp, out_own, out_sent, att_early, lse_early,
    )
    down_recv, up_recv = swap(down_sent, core), swap(up_sent, core)
    g_other = swap(g_theirs, core)
    early_g = (to_early(g_own_high), to_early(g_theirs_high, 1))
    out_recv = swap(out_sent, core)

    accumulators = [pltpu.VMEM((2, HEAD_DIM, length), F32)] * 2

    def local_back(at, heads, g0, g1):
        return call(
            local_back_kernel,
            flags,
            (heads,),
            [head(a, base + at) for base in (0, 6, 12) for a in (own, other)]
            + [head(a, at) for a in (g0, g1, att_own, att_pair)]
            + [(lse, (1, 2, length), lambda h, f: (at + h, 0, 0))],
            [((3, heads * HEAD_DIM, length), BF, (3, HEAD_DIM, length), lambda h, f: (0, h, 0))] * 2,
            BRIEF,
            "attend_back_local",
            accumulators,
        )

    d_0 = local_back(0, 2, g_own, g_other)
    d_0, early_g, out_own = tie(d_0, early_g, out_own)
    opened = whole_call(
        functools.partial(open_kernel, at=[steps_[0][3] for steps_ in orders]),
        flags,
        [down_own, down_recv, up_own, up_recv, out_own, out_recv],
        [shape for shape in (((ff_half - GROUP) // 2, D), (GROUP, ff_half), (GROUP, D)) for _ in (0, 1)],
        "open",
    )
    first = [Chain(orders[i], 1, *opened[2 * i : 2 * i + 2]) for i in range(3)]
    (early_g,) = send(first, early_g)
    dq_cross, dkv_cross = call(
        cross_back_kernel,
        flags,
        (HALF_HEADS,),
        cross_in
        + [
            head(early_g[0], 0),
            head(early_g[1], 0),
            (att_early, (2, HEAD_DIM, length), lambda h, f: (0, h, 0)),
            lse_spec(lse_early),
            head(g_own, 0),
            head(g_other, 0),
            head(att_own, 0),
            head(att_pair, 0),
            lse_spec(lse),
        ],
        [
            pair_out,
            (
                (2, 2, HALF, length),
                BF,
                (2, 2, HEAD_DIM, length),
                lambda h, f: (0, 0, h, 0),
            ),
        ],
        BRIEF,
        "attend_back_cross",
        accumulators,
    )
    dq_cross, dkv_cross, g_own, g_other = tie(dq_cross, dkv_cross, g_own, g_other)
    dq_back, dkv_back = to_late(dq_cross), to_early(dkv_cross)
    d_1 = local_back(2, 2, g_own, g_other)
    (d_1,) = beside(first, d_1)
    land(flags, first)
    g_own, g_other = send(first, g_own, g_other)
    d_2 = local_back(4, 2, g_own, g_other)
    d_2, dq_back, dkv_back = beside(first, d_2, dq_back, dkv_back)
    land(flags, first)
    d_2, dq_back, dkv_back = send(first, d_2, dq_back, dkv_back)
    few = (1, 2 * HEAD_DIM, length)
    one_q = (1, 2, HALF, length)
    gp_own, gp_pair = call(
        combine_kernel,
        flags,
        (3,),
        [(d, few, lambda i, f: (i, 0, 0)) for d in (*d_0, *d_1, *d_2)]
        + [
            fixed(dq_cross.reshape(one_q)),
            fixed(dq_back.reshape(one_q)),
            (dkv_cross, one_q, lambda i, f: (jnp.maximum(i - 1, 0), 0, 0, 0)),
            (dkv_back, one_q, lambda i, f: (jnp.maximum(i - 1, 0), 0, 0, 0)),
        ],
        [((3 * GROUP, length), BF, (GROUP, length), lambda i, f: (i, 0))] * 2,
        BRIEF,
        "combine",
    )
    gp_other = swap(gp_pair, core)
    opened = call(
        functools.partial(project_grad_kernel, at=[ring[0][3], by_y[0][3]]),
        flags,
        (3,),
        [(g, (GROUP, length), lambda i, f: (i, 0)) for g in (gp_own, gp_pair)]
        + [fixed(normed), fixed(normed_other)],
        [((D // 4, 3 * GROUP), BF, (D // 4, GROUP), lambda i, f: (0, i))] * 4,
        BRIEF,
        "project_grad",
    )
    gp_own, gp_other, opened = beside(first, gp_own, gp_other, opened)
    second = [Chain(order, 2, *opened[2 * i : 2 * i + 2]) for i, order in enumerate((ring, lanes[:1] + [cross] + lanes[1:]))]
    land(flags, first)
    send(first + second)
    land(flags, first + second)
    gp_own, gp_other = send(first + second, gp_own, gp_other)
    grad_input, sums = call(
        input_grad_kernel,
        flags,
        (3,),
        [
            (gp_own, (GROUP, length), lambda i, f: (i, 0)),
            (gp_other, (GROUP, length), lambda i, f: (i, 0)),
            (w_qkv, (D, GROUP), lambda i, f: (0, 2 * i + f[1])),
            (w_qkv, (D, GROUP), lambda i, f: (0, 2 * i + 1 - f[1])),
            fixed(x),
            emb,
            fixed(row(gain_attn)),
            fixed(grad_residual),
            fixed(dgain_mlp),
        ],
        [out_fixed(tokens, BF), out_fixed((passes + 2, D), F32)],
        BRIEF,
        "input_grad",
        [pltpu.VMEM((D, length), F32)],
    )
    grad_input, sums = beside(first + second, grad_input, sums)
    land(flags, first + second)
    while second[1].plan[0][0] == HALVE:
        send(first + second)
        land(flags, first + second)
    rider = jnp.pad(sums, ((0, 8 - passes - 2), (0, 3 * GROUP - D))).astype(BF)
    second[1].sent, second[1].riders = jnp.concatenate([second[1].sent, rider]), 8
    while not first[0].done():
        send(first + second)
        land(flags, first + second)
    send(second)
    pairs = [(c.sent, swap(c.sent, core)) for c in first]
    (pairs,) = beside(second, pairs)
    land(flags, second)
    third = [a for pair in pairs for a in pair]
    at_most = [
        (third[i], (GROUP, D), lambda j, f: (jnp.minimum(j % 4, 2), 0)) for i in (0, 1)
    ] + [(third[i], (D, GROUP), lambda j, f: (0, j % 4)) for i in (2, 3)]
    down_total, up_total, out_total = call(
        assemble_first_kernel,
        flags,
        (8,),
        at_most + [fixed(third[4]), fixed(third[5])],
        [
            ((4 * D, D), F32, (GROUP, D), lambda j, f: (j, 0)),
            ((D, 4 * D), F32, (D, GROUP), lambda j, f: (0, j)),
            ((D, D), F32, (GROUP, D), lambda j, f: (j // 4, 0)),
        ],
        BRIEF,
        "assemble_first",
    )
    while not second[0].done():
        send(second)
        down_total, up_total, out_total = beside(second, down_total, up_total, out_total)
        land(flags, second)
    lasts = [(c.sent, swap(c.sent, core)) for c in second]
    small = sum(a[D // 2 :, :D].astype(F32) for a in lasts[1])
    qkv_total = call(
        assemble_second_kernel,
        flags,
        (6,),
        [
            (a, (GROUP, GROUP), lambda j, f: (0, j // 2))
            for pair in lasts
            for a in pair
        ],
        [((D, 3 * D), F32, (D, GROUP), lambda j, f: (0, j))],
        BRIEF,
        "assemble_second",
    )[0]
    return (
        output[None],
        grad_input[None],
        small[:passes],
        small[passes],
        qkv_total,
        out_total,
        small[passes + 1],
        up_total,
        down_total,
    )


def solution(mesh):
    sizes = (mesh.shape["pass"], mesh.shape["dp"])
    tokens = P("pass", "dp", None)
    in_specs = (tokens, P("dp")) + (P(),) * 7 + (tokens,)
    out_specs = (tokens, tokens) + (P(),) * 7
    return jax.shard_map(
        functools.partial(on_device, sizes),
        mesh=mesh,
        in_specs=in_specs,
        out_specs=out_specs,
        check_vma=False,
    )
```

```python
import functools
import math

import jax
import jax.numpy as jnp
from jax import lax
from jax.experimental import pallas as pl
from jax.experimental.pallas import tpu as pltpu
from jax.sharding import PartitionSpec as P

D = 768
HEADS = 12
HEAD_DIM = 64
SHORT = 256
FF_TILE = 512
GROUP = D // 2
HALF = GROUP // 2
HALF_HEADS = HEADS // 4
EPS = 1e-05
SCALE = HEAD_DIM**-0.5
SCALE2 = SCALE * math.log2(math.e)
BF = jnp.bfloat16
F32 = jnp.float32
PIECES, FIRST_HEADS = (2, 1), (0, 2)
BRIEF = 0.2


def dot(a, b, ca, cb):
    return lax.dot_general(a, b, (((ca,), (cb,)), ((), ())), preferred_element_type=F32)


def cost(us):
    return pl.CostEstimate(flops=int(us * 1.1e9), bytes_accessed=1 << 20, transcendentals=0)


def call(kernel, flags, grid, ins, outs, us, name, scratch=(), temporaries=8):
    blocks = [(math.prod(block), array.dtype) for array, block, index in ins if index]
    blocks += [(math.prod(block), dtype) for _, dtype, block, index in outs if index]
    blocks += [(math.prod(buffer.shape) // 2, buffer.dtype) for buffer in scratch]
    limit = sum(2 * n * jnp.dtype(dtype).itemsize for n, dtype in blocks) + (temporaries << 20)
    return pl.pallas_call(
        kernel,
        grid_spec=pltpu.PrefetchScalarGridSpec(
            num_scalar_prefetch=1,
            grid=grid,
            in_specs=[spec(block, index) for _, block, index in ins],
            out_specs=[spec(block, index) for _, _, block, index in outs],
            scratch_shapes=list(scratch),
        ),
        out_shape=[jax.ShapeDtypeStruct(shape, dtype) for shape, dtype, _, _ in outs],
        cost_estimate=cost(us),
        compiler_params=pltpu.CompilerParams(vmem_limit_bytes=min(limit, 60 << 20)),
        name=name,
    )(flags, *[array for array, _, _ in ins])


def fixed(array):
    return (array, array.shape, lambda i, f: (0,) * array.ndim)


def out_fixed(shape, dtype):
    return (shape, dtype, shape, lambda i, f: (0,) * len(shape))


def held(array):
    return (array, array.shape, None)


def out_held(shape, dtype):
    return (shape, dtype, shape, None)


def spec(block, index):
    return pl.BlockSpec(block, index) if index else pl.BlockSpec(memory_space=pltpu.VMEM)


def one_sequence(f):
    return f[0] == 1


def hidden_of(f, x_ref, emb_ref):
    return x_ref[...].astype(F32) + emb_ref[pl.ds(f[3], 1), :]


def centered(values):
    center = values - jnp.mean(values, axis=-1, keepdims=True)
    return center, lax.rsqrt(jnp.mean(center * center, axis=-1, keepdims=True) + EPS)


def write_part(part, refs, value):
    out_ref, *cross_refs = refs
    out_ref[...] = value
    for (low_ref, high_ref), first, heads in zip(
        (cross_refs[:2], cross_refs[2:]), FIRST_HEADS, PIECES, strict=True
    ):
        start, rows = first * HEAD_DIM, heads * HEAD_DIM

        @pl.when(part == 0)
        def _():
            high_ref[...] = value[HALF + start : HALF + start + rows]

        @pl.when(part > 0)
        def _():
            low_ref[pl.ds(pl.multiple_of((part - 1) * rows, rows), rows), :] = value[
                start : start + rows
            ]


def norm_project_kernel(f, x_ref, emb_ref, gain_ref, w_ref, normed_ref, *refs):
    part = pl.program_id(0)

    @pl.when(part == 0)
    def _():
        center, inv = centered(hidden_of(f, x_ref, emb_ref))
        normed_ref[...] = (center * inv * gain_ref[0:1]).T.astype(BF)

    write_part(part, refs, dot(w_ref[...], normed_ref[...], 0, 0).astype(BF))


def project_kernel(f, normed_ref, w_ref, *refs):
    write_part(pl.program_id(0), refs, dot(w_ref[...], normed_ref[...], 0, 0).astype(BF))


def projection_outs(length):
    outs = [((3 * GROUP, length), BF, (GROUP, length), lambda i, f: (i, 0))]
    for heads in PIECES:
        outs += [out_fixed((2 * heads * HEAD_DIM, length), BF), out_fixed((heads * HEAD_DIM, length), BF)]
    return outs


def mask_tail(scores):
    n = scores.shape[0]
    key = lax.broadcasted_iota(jnp.int32, (SHORT, SHORT), 0)
    query = lax.broadcasted_iota(jnp.int32, (SHORT, SHORT), 1)
    diag = jnp.where(key <= query, scores[n - SHORT :], -1e30)
    return diag if n == SHORT else jnp.concatenate([scores[: n - SHORT], diag], 0)


def sweep(f, length, tile, variants):
    for condition, units in variants:
        for whole in (True, False):

            @pl.when(condition & (one_sequence(f) == whole))
            def _():
                for at in range(length // SHORT):
                    for unit in units:
                        tile(unit, at, 0 if whole else at)


def spans(at, first):
    return slice(at * SHORT, (at + 1) * SHORT), slice(first * SHORT, (at + 1) * SHORT)


def softmax_tile(q_refs, k_refs, v_refs, o_refs, lse_ref, unit, at, first):
    qp, keys = unit
    qs, ks = spans(at, first)
    q = q_refs[qp][:, qs]
    scores = [mask_tail(dot(k_refs[kp][:, ks], q, 0, 0) * SCALE2) for kp in keys]
    top = functools.reduce(jnp.maximum, [jnp.max(s, axis=0, keepdims=True) for s in scores])
    raw = [jnp.exp2(s - top) for s in scores]
    total = functools.reduce(jnp.add, [jnp.sum(p, axis=0, keepdims=True) for p in raw])
    out = functools.reduce(
        jnp.add, [dot(v_refs[kp][:, ks], p.astype(BF), 1, 0) for kp, p in zip(keys, raw)]
    )
    o_refs[qp][:, qs] = (out * (1.0 / total)).astype(o_refs[qp].dtype)
    lse_ref[0, qp : qp + 1, qs] = top + jnp.log2(total)


LOCAL_UNITS = (
    lambda f: (f[1] == 0, [(0, [0]), (1, [0, 1])]),
    lambda f: (f[1] == 1, [(1, [1]), (0, [0, 1])]),
)
CROSS_UNITS = [(0, [0, 1]), (1, [0, 1])]


def local_kernel(f, q0, q1, k0, k1, v0, v1, o0, o1, lse_ref):
    sweep(
        f,
        q0.shape[1],
        functools.partial(softmax_tile, (q0, q1), (k0, k1), (v0, v1), (o0, o1), lse_ref),
        [unit(f) for unit in LOCAL_UNITS],
    )


def cross_kernel(f, *refs):
    ins, (o_ref, lse_ref) = refs[:12], refs[12:]
    outs = (o_ref.at[0], o_ref.at[1])
    for early, at in ((1, 0), (0, 6)):
        q0, q1, k0, k1, v0, v1 = ins[at : at + 6]
        sweep(
            f,
            q0.shape[1],
            functools.partial(softmax_tile, (q0, q1), (k0, k1), (v0, v1), outs, lse_ref),
            [(f[2] == early, CROSS_UNITS)],
        )


def head(array, at):
    return (array, (HEAD_DIM, array.shape[-1]), lambda h, f: (at + h, 0))


def lse_spec(array):
    return (array, (1,) + array.shape[1:], lambda h, f: (h, 0, 0))


def lse_out(heads, length):
    return ((heads, 2, length), F32, (1, 2, length), lambda h, f: (h, 0, 0))


def cross_inputs(early_q, own, other, late_kv, first, heads):
    high = HALF_HEADS + first
    return [
        head(early_q[0], 0),
        head(early_q[1], 0),
        head(own, 6 + high),
        head(other, 6 + high),
        head(own, 12 + high),
        head(other, 12 + high),
        head(own, first),
        head(other, first),
        head(late_kv[0], 0),
        head(late_kv[1], 0),
        head(late_kv[0], heads),
        head(late_kv[1], heads),
    ]


def merge_kernel(
    f, la0, la1, lsea, lb0, lb1, lseb, ca, lseca, cb, lsecb, ba, lseba, bb, lsebb,
    a0, a1, lse_out, high_ref, lse_high,
):
    def rows(h):
        return slice(h * HEAD_DIM, (h + 1) * HEAD_DIM)

    def put(h, i, value, lse):
        value = value.astype(BF)
        (a0, a1)[i][rows(h)] = value
        lse_out[h, i : i + 1] = lse
        if h >= HALF_HEADS:
            high_ref[i, rows(h - HALF_HEADS)] = value
            lse_high[h - HALF_HEADS, i : i + 1] = lse

    for h in range(2 * HALF_HEADS):
        local, lse_l, at = ((la0, la1), lsea, h) if h < 4 else ((lb0, lb1), lseb, h - 4)
        low, there = h < HALF_HEADS, h % HALF_HEADS
        if there < PIECES[0]:
            far, lse_c = (ca, lseca) if low else (ba, lseba)
        else:
            far, lse_c, there = (cb, lsecb, 0) if low else (bb, lsebb, 0)
        for i in (0, 1):
            near, lse_near = local[i][rows(at)], lse_l[at, i : i + 1]

            @pl.when(f[2] == 1)
            def _():
                put(h, i, near, lse_near)

            @pl.when(f[2] == 0)
            def _():
                lse_far = lse_c[there, i : i + 1]
                top = jnp.maximum(lse_near, lse_far)
                lse = top + jnp.log2(jnp.exp2(lse_near - top) + jnp.exp2(lse_far - top))
                value = near * jnp.exp2(lse_near - lse) + far[i, rows(there)].astype(F32) * jnp.exp2(
                    lse_far - lse
                )
                put(h, i, value, lse)


def gradient_tile(
    q_refs, k_refs, v_refs, g_refs, o_refs, lse_ref, dq_refs, dk_acc, dv_acc, unit, at, first
):
    qp, keys = unit
    qs, ks = spans(at, first)
    q, g = q_refs[qp][:, qs], g_refs[qp][:, qs]
    lse = lse_ref[0, qp : qp + 1, qs]
    delta = jnp.sum(g.astype(F32) * o_refs[qp][:, qs].astype(F32), axis=0, keepdims=True)
    dq = None
    for kp in keys:
        k, v = k_refs[kp][:, ks], v_refs[kp][:, ks]
        weights = jnp.exp2(mask_tail(dot(k, q, 0, 0) * SCALE2) - lse)
        ds = (weights * (dot(v, g, 0, 0) - delta)).astype(BF)
        term = dot(k, ds, 1, 0)
        dq = term if dq is None else dq + term
        dk_acc[kp, :, ks] += dot(q, ds, 1, 1)
        dv_acc[kp, :, ks] += dot(g, weights.astype(BF), 1, 1)
    dq_refs[qp][:, qs] = (dq * SCALE).astype(BF)


def local_back_kernel(
    f, q0, q1, k0, k1, v0, v1, g0, g1, o0, o1, lse_ref, d0, d1, dk_acc, dv_acc
):
    dk_acc[...] = jnp.zeros_like(dk_acc)
    dv_acc[...] = jnp.zeros_like(dv_acc)
    sweep(
        f,
        q0.shape[1],
        functools.partial(
            gradient_tile,
            (q0, q1),
            (k0, k1),
            (v0, v1),
            (g0, g1),
            (o0, o1),
            lse_ref,
            (d0.at[0], d1.at[0]),
            dk_acc,
            dv_acc,
        ),
        [unit(f) for unit in LOCAL_UNITS],
    )
    for i, ref in ((0, d0), (1, d1)):
        ref[1] = (dk_acc[i] * SCALE).astype(BF)
        ref[2] = dv_acc[i].astype(BF)


def cross_back_kernel(f, *refs):
    ins, more = refs[:12], refs[12:]
    (ga0, ga1, oa, lse_a, gb0, gb1, ob0, ob1, lse_b, dq_ref, dkv_ref, dk_acc, dv_acc) = more
    dk_acc[...] = jnp.zeros_like(dk_acc)
    dv_acc[...] = jnp.zeros_like(dv_acc)
    for early, at, grads, outs, lse_ref in (
        (1, 0, (ga0, ga1), (oa.at[0], oa.at[1]), lse_a),
        (0, 6, (gb0, gb1), (ob0, ob1), lse_b),
    ):
        q0, q1, k0, k1, v0, v1 = ins[at : at + 6]
        sweep(
            f,
            q0.shape[1],
            functools.partial(
                gradient_tile,
                (q0, q1),
                (k0, k1),
                (v0, v1),
                grads,
                outs,
                lse_ref,
                (dq_ref.at[0], dq_ref.at[1]),
                dk_acc,
                dv_acc,
            ),
            [(f[2] == early, CROSS_UNITS)],
        )
    for i in (0, 1):
        dkv_ref[0, i] = (dk_acc[i] * SCALE).astype(BF)
        dkv_ref[1, i] = dv_acc[i].astype(BF)


def gelu_pair(u):
    k = math.sqrt(2 / math.pi)
    square = u * u
    t = jnp.tanh(k * u * (1.0 + 0.044715 * square))
    half = 0.5 + 0.5 * t
    slope = half + 0.5 * u * (1.0 - t * t) * (k * (1.0 + 3 * 0.044715 * square))
    return u * half, slope


def chunks(length):
    return [slice(at, at + SHORT) for at in range(0, length, SHORT)]


def ff_tile(n_ref, cot_ref, wu_ref, wd_ref, y_ref, c_ref, act_ref, gup_ref):
    for at in chunks(n_ref.shape[0]):
        act, slope = gelu_pair(dot(n_ref[at], wu_ref[...], 1, 0))
        act = act.astype(BF)
        grad_up = (dot(cot_ref[at], wd_ref[...], 1, 1) * slope).astype(BF)
        act_ref[at], gup_ref[at] = act, grad_up
        y_ref[at] += dot(act, wd_ref[...], 1, 0)
        c_ref[at] += dot(grad_up, wu_ref[...], 1, 1)


def feed_kernel(
    f, x_ref, emb_ref, a_ref, b_ref, wa_ref, wb_ref, gain_ref, cot_ref, wu_ref, wd_ref,
    dds_ref, dus_ref, ddo_ref, duo_ref, out_ref, gres_ref, ga_ref, gb_ref, gah_ref, gbh_ref, dgain_ref, dwa_ref, dwb_ref,
    res_ref, n_ref, y_ref, c_ref, act_ref, gup_ref,
):
    step, steps = pl.program_id(0), pl.num_programs(0)

    @pl.when(step == 0)
    def _():
        for at in chunks(n_ref.shape[0]):
            residual = (
                x_ref[at].astype(F32)
                + emb_ref[pl.ds(f[3], 1), :]
                + dot(a_ref[:, at], wa_ref[...], 0, 0)
                + dot(b_ref[:, at], wb_ref[...], 0, 0)
            )
            res_ref[at] = residual
            center, inv = centered(residual)
            n_ref[at] = (center * inv * gain_ref[1:2]).astype(BF)
            y_ref[at] = residual
            c_ref[at] = jnp.zeros_like(residual)

    ff_tile(n_ref, cot_ref, wu_ref, wd_ref, y_ref, c_ref, act_ref, gup_ref)
    down = dot(act_ref[...], cot_ref[...], 0, 0).astype(BF)
    up = dot(n_ref[...], gup_ref[...], 0, 0).astype(BF)

    @pl.when(step < steps // 2)
    def _():
        dds_ref[...], dus_ref[...] = down, up

    @pl.when(step >= steps // 2)
    def _():
        ddo_ref[...], duo_ref[...] = down, up

    @pl.when(step == steps - 1)
    def _():
        dgain = None
        grads = []
        for at in chunks(n_ref.shape[0]):
            out_ref[at] = y_ref[at].astype(BF)
            center, inv = centered(res_ref[at])
            n2 = center * inv
            c = c_ref[at]
            part = jnp.sum(c * n2, axis=0, keepdims=True)
            dgain = part if dgain is None else dgain + part
            e = c * gain_ref[1:2]
            grad = cot_ref[at].astype(F32) + inv * (
                e
                - jnp.mean(e, axis=-1, keepdims=True)
                - n2 * jnp.mean(e * n2, axis=-1, keepdims=True)
            )
            gres_ref[at] = grad
            grad = grad.astype(BF)
            grads.append(grad)
            mine = dot(wa_ref[...], grad, 1, 1).astype(BF)
            theirs = dot(wb_ref[...], grad, 1, 1).astype(BF)
            ga_ref[:, at], gb_ref[:, at] = mine, theirs
            gah_ref[:, at], gbh_ref[:, at] = mine[HALF:], theirs[HALF:]
        dgain_ref[...] = dgain
        grad = jnp.concatenate(grads, 0)
        dwa_ref[...] = dot(a_ref[...], grad, 1, 0).astype(BF)
        dwb_ref[...] = dot(b_ref[...], grad, 1, 0).astype(BF)


def combine_kernel(f, da0, da1, db0, db1, dc0, dc1, dqc_ref, dqb_ref, dkvc_ref, dkvb_ref, g0, g1):
    part = pl.program_id(0)
    late, early = f[2] == 0, f[2] == 1

    def put(low, high):
        for i, (refs, g) in enumerate((((da0, db0, dc0), g0), ((da1, db1, dc1), g1))):
            local = jnp.concatenate([d[0] for d in refs], 0)
            if low is None:
                g[...] = local
            else:
                more = jnp.concatenate([low[0, i], high[0, i]], 0)
                g[...] = (local.astype(F32) + more.astype(F32)).astype(BF)

    @pl.when(late & (part == 0))
    def _():
        put(dqc_ref, dqb_ref)

    @pl.when(early & (part > 0))
    def _():
        put(dkvb_ref, dkvc_ref)

    @pl.when((late & (part > 0)) | (early & (part == 0)))
    def _():
        put(None, None)


def project_grad_kernel(f, g0, g1, n0_ref, n1_ref, s0_ref, k0_ref, s1_ref, k1_ref, *, at):
    value = dot(n0_ref[...], g0[...], 1, 1) + dot(n1_ref[...], g1[...], 1, 1)
    for i, (sent_ref, kept_ref) in enumerate(((s0_ref, k0_ref), (s1_ref, k1_ref))):
        sent, kept = pick(f[at[i]], value[i * (D // 2) : (i + 1) * (D // 2)])
        sent_ref[...] = sent.astype(BF)
        kept_ref[...] = kept.astype(BF)


def input_grad_kernel(
    f, g_ref, h_ref, wg_ref, wh_ref, x_ref, emb_ref, gain_ref, gres_ref, dgain_ref, gin_ref, sums_ref, acc
):
    part = pl.program_id(0)
    value = dot(wg_ref[...], g_ref[...], 1, 0) + dot(wh_ref[...], h_ref[...], 1, 0)

    @pl.when(part == 0)
    def _():
        acc[...] = value

    @pl.when(part > 0)
    def _():
        acc[...] += value

    @pl.when(part == pl.num_programs(0) - 1)
    def _():
        center, inv = centered(hidden_of(f, x_ref, emb_ref))
        n1 = center * inv
        grad = acc[...].T
        e = grad * gain_ref[0:1]
        total = gres_ref[...] + inv * (
            e - jnp.mean(e, axis=-1, keepdims=True) - n1 * jnp.mean(e * n1, axis=-1, keepdims=True)
        )
        gin_ref[...] = total.astype(BF)
        sums = jnp.sum(total, axis=0, keepdims=True)
        passes = sums_ref.shape[0] - 2
        for i in range(passes):
            sums_ref[i : i + 1] = jnp.where(f[3] == i, sums, 0.0)
        sums_ref[passes : passes + 1] = jnp.sum(grad * n1, axis=0, keepdims=True)
        sums_ref[passes + 1 :] = dgain_ref[...]


def assemble_first_kernel(f, d_own, d_oth, u_own, u_oth, m_own, m_oth, down_ref, up_ref, out_ref):
    step = pl.program_id(0)
    half, at = step // 4, step % 4
    for mine, d, u, m in ((True, d_own, u_own, m_own), (False, d_oth, u_oth, m_oth)):
        here = (half == f[1]) == mine

        @pl.when(here)
        def _():
            up_ref[...] = u[...].astype(F32)

        @pl.when(here & (at < 3))
        def _():
            down_ref[...] = d[...].astype(F32)

        @pl.when(here & (at == 3))
        def _():
            down_ref[...] = m[:GROUP].astype(F32)
            out_ref[...] = m[GROUP:].astype(F32)


def assemble_second_kernel(f, a_own, a_oth, b_own, b_oth, out_ref):
    for mine, a, b in ((True, a_own, b_own), (False, a_oth, b_oth)):

        @pl.when((pl.program_id(0) % 2 == f[1]) == mine)
        def _():
            out_ref[:GROUP] = a[...].astype(F32)
            out_ref[GROUP:] = b[...].astype(F32)


def swap(array, step):
    axis, mask, size, _ = step
    return lax.ppermute(array, axis, [(i, i ^ mask) for i in range(size)])


def tie(*groups):
    leaves, tree = jax.tree.flatten(groups)
    return jax.tree.unflatten(tree, lax.optimization_barrier(leaves))


def pick(here, total):
    half = total.shape[0] // 2
    low, high = total[:half], total[half:]
    return jnp.where(here == 0, high, low), jnp.where(here == 0, low, high)


def joined(here, own, other):
    return jnp.where(
        here == 0, jnp.concatenate([own, other], 0), jnp.concatenate([other, own], 0)
    )


def round_work(here, own, came, mode, riders):
    if mode == "join":
        cut = own.shape[0] - riders
        value = joined(here, own[:cut], came[:cut])
        return (jnp.concatenate([value, own[cut:] + came[cut:]], 0) if riders else value,)
    total = own + came
    return (total,) if mode == "sum" else pick(here, total)


def round_kernel(f, *refs, modes, at, riders):
    refs = list(refs)
    ins, outs = refs[: 2 * len(modes)], refs[2 * len(modes) :]
    for i, mode in enumerate(modes):
        own, came = ins[2 * i][...].astype(F32), ins[2 * i + 1][...].astype(F32)
        for value in round_work(f[at[i]], own, came, mode, riders[i]):
            outs.pop(0)[...] = value.astype(BF)


def whole_call(kernel, flags, ins, outs, name):
    vmem = pl.BlockSpec(memory_space=pltpu.VMEM)
    size = sum(math.prod(shape) for shape in [a.shape for a in ins] + outs)
    return pl.pallas_call(
        kernel,
        in_specs=[pl.BlockSpec(memory_space=pltpu.SMEM)] + [vmem] * len(ins),
        out_specs=[vmem] * len(outs),
        out_shape=[jax.ShapeDtypeStruct(shape, BF) for shape in outs],
        cost_estimate=cost(BRIEF),
        compiler_params=pltpu.CompilerParams(vmem_limit_bytes=2 * size + (8 << 20)),
        name=name,
    )(flags, *ins)


HALVE, FULL, JOIN = 0, 1, 2


class Chain:
    def __init__(self, steps, whole_steps, sent, kept):
        cut = len(steps) - whole_steps
        self.plan = (
            [(HALVE, step) for step in steps[:cut]]
            + [(FULL, step) for step in steps[cut:]]
            + [(JOIN, step) for step in reversed(steps[:cut])]
        )
        self.sent, self.kept, self.came, self.riders = sent, kept, None, 0

    def done(self):
        return not self.plan


def land(flags, chains):
    chains = [c for c in chains if c.came is not None]
    modes, at, ins, outs, riders = [], [], [], [], [c.riders for c in chains]
    for c in chains:
        what, step = c.plan.pop(0)
        own = c.kept if what == HALVE else c.sent
        rows, columns = own.shape
        if what == JOIN:
            modes.append("join")
            at.append(step[3])
            outs += [(2 * rows - c.riders, columns)]
        elif c.plan and c.plan[0][0] == HALVE:
            modes.append("split")
            at.append(c.plan[0][1][3])
            outs += [(rows // 2, columns)] * 2
        else:
            modes.append("sum")
            at.append(0)
            outs += [(rows, columns)]
        ins += [own, c.came]
    if all(shape[0] % 8 == 0 for shape in outs):
        kernel = functools.partial(round_kernel, modes=modes, at=at, riders=riders)
        results = list(whole_call(kernel, flags, ins, outs, "round"))
    else:
        results = []
        for i, mode in enumerate(modes):
            own, came = (a.astype(F32) for a in ins[2 * i : 2 * i + 2])
            results += [
                v.astype(BF) for v in round_work(flags[at[i]], own, came, mode, riders[i])
            ]
    for c, mode in zip(chains, modes, strict=True):
        c.came, c.sent = None, results.pop(0)
        if mode == "split":
            c.kept = results.pop(0)


def open_kernel(f, dd, ddr, du, dur, dw, dwr, *outs, at):
    def add(left, right):
        return left[...].astype(F32) + right[...].astype(F32)

    down, up, out = add(dd, ddr), add(du, dur), add(dw, dwr)
    cut = down.shape[0] - GROUP
    for i, value in enumerate((down[:cut], up, jnp.concatenate([down[cut:], out], 0))):
        sent, kept = pick(f[at[i]], value)
        outs[2 * i][...] = sent.astype(BF)
        outs[2 * i + 1][...] = kept.astype(BF)


def beside(chains, *more):
    chains = [c for c in chains if c.came is not None]
    arrays, more = tie([c.came for c in chains], more)
    for c, array in zip(chains, arrays, strict=True):
        c.came = array
    return more


def send(chains, *more):
    chains = [c for c in chains if not c.done()]
    loads, more = tie([c.sent for c in chains], more)
    for c, load in zip(chains, loads, strict=True):
        c.sent, c.came = load, swap(load, c.plan[0][1])
    return more


def on_device(
    sizes, block_input, segments, pass_emb, gain_attn, w_qkv, w_out, gain_mlp, w_up, w_down, cotangent
):
    passes, n_dp = sizes
    core = ("pass", 1, passes, 1)
    cross = ("pass", 2, passes, 4)
    lanes = [("dp", 1 << i, n_dp, 5 + i) for i in range(n_dp.bit_length() - 1)]
    ring = [cross] + lanes
    by_y = lanes[:1] + [cross] + lanes[:0:-1]
    orders = [ring, by_y, ring[2:] + ring[:2]]

    pass_here = lax.axis_index("pass")
    core_here = pass_here & 1
    length = segments.shape[0]
    flags = jnp.stack(
        [
            (segments[0] == segments[length - 1]).astype(jnp.int32),
            core_here.astype(jnp.int32),
            (pass_here < 2).astype(jnp.int32),
            pass_here.astype(jnp.int32),
        ]
        + [
            (lax.axis_index(axis) >> (mask.bit_length() - 1)) & 1 for axis, mask, _, _ in ring
        ]
    )

    def to_late(array, other=0):
        return lax.ppermute(array, "pass", [(0, 2 + other), (1, 3 - other)])

    def to_early(array, other=0):
        return lax.ppermute(array, "pass", [(2, other), (3, 1 - other)])

    x, cot = block_input[0], cotangent[0]
    emb = fixed(pass_emb)
    gains = jnp.stack([gain_attn, gain_mlp])

    normed, theirs, *theirs_cross = call(
        norm_project_kernel,
        flags,
        (3,),
        [fixed(x), emb, fixed(gains), (w_qkv, (D, GROUP), lambda i, f: (0, 2 * i + 1 - f[1]))],
        [out_fixed((D, length), BF)] + projection_outs(length),
        BRIEF,
        "norm_project",
    )
    other = swap(theirs, core)
    own, *own_cross = call(
        project_kernel,
        flags,
        (3,),
        [fixed(normed), (w_qkv, (D, GROUP), lambda i, f: (0, 2 * i + f[1]))],
        projection_outs(length),
        BRIEF,
        "project_own",
    )

    def exchange(piece):
        (low_o, high_o), (low_t, high_t) = (
            array[2 * piece : 2 * piece + 2] for array in (own_cross, theirs_cross)
        )
        return (to_late(low_o), to_late(low_t, 1)), (to_early(high_o), to_early(high_t, 1))

    def attend_local(first, heads):
        return call(
            local_kernel,
            flags,
            (heads,),
            [head(a, at + first) for at in (0, 6, 12) for a in (own, other)],
            [((heads * HEAD_DIM, length), F32, (HEAD_DIM, length), lambda h, f: (h, 0))] * 2
            + [lse_out(heads, length)],
            BRIEF,
            "attend_local",
        )

    def attend_cross(piece, late_kv, early_q):
        heads = PIECES[piece]
        return call(
            cross_kernel,
            flags,
            (heads,),
            cross_inputs(early_q, own, other, late_kv, FIRST_HEADS[piece], heads),
            [
                ((2, heads * HEAD_DIM, length), BF, (2, HEAD_DIM, length), lambda h, f: (0, h, 0)),
                lse_out(heads, length),
            ],
            BRIEF,
            "attend_cross",
        )

    far_0 = exchange(0)
    local_0 = attend_local(0, 4)
    far_0, local_0, own_cross, theirs_cross = tie(far_0, local_0, own_cross, theirs_cross)
    far_1 = exchange(1)
    normed_other = swap(normed, core)
    cross_0 = attend_cross(0, *far_0)
    far_1, cross_0 = tie(far_1, cross_0)
    o_back_0 = to_late(cross_0[0])
    cross_1 = attend_cross(1, *far_1)
    cross_1, own, other = tie(cross_1, own, other)
    o_back_1, lse_back_1, lse_back_0 = to_late(cross_1[0]), to_late(cross_1[1]), to_late(cross_0[1])
    local_1 = attend_local(4, 2)
    o_back_0, o_back_1, lse_back_0, lse_back_1, local_1 = tie(
        o_back_0, o_back_1, lse_back_0, lse_back_1, local_1
    )
    half_rows = (HALF, length)
    att_own, att_pair, lse, att_high, lse_high = call(
        merge_kernel,
        flags,
        (1,),
        [
            fixed(a)
            for a in (*local_0, *local_1, *cross_0, *cross_1, o_back_0, lse_back_0, o_back_1, lse_back_1)
        ],
        [out_fixed((GROUP, length), BF)] * 2
        + [
            out_fixed((HEADS // 2, 2, length), F32),
            out_fixed((2, HALF, length), BF),
            out_fixed((HALF_HEADS, 2, length), F32),
        ],
        BRIEF,
        "merge",
    )
    late_kv = [
        jnp.concatenate([a[: 2 * HEAD_DIM], b[:HEAD_DIM], a[2 * HEAD_DIM :], b[HEAD_DIM:]])
        for a, b in zip(far_0[0], far_1[0], strict=True)
    ]
    early_q = [jnp.concatenate(pieces) for pieces in zip(far_0[1], far_1[1], strict=True)]
    cross_in = cross_inputs(early_q, own, other, late_kv, 0, HALF_HEADS)
    pair_out = ((2, HALF, length), BF, (2, HEAD_DIM, length), lambda h, f: (0, h, 0))
    att_other = swap(att_pair, core)
    att_early, lse_early = to_early(att_high), to_early(lse_high)
    att_own, att_other, normed_other = tie(att_own, att_other, normed_other)

    w_half = [(w_out, (GROUP, D), lambda i, f: (f[1], 0)), (w_out, (GROUP, D), lambda i, f: (1 - f[1], 0))]
    ff_half = w_up.shape[1] // 2
    steps = ff_half // FF_TILE

    def tile_at(i, f):
        return jnp.where(i < steps, 1 - f[1], f[1]) * steps + i % steps

    sent_at, own_at = lambda i: jnp.minimum(i, steps - 1), lambda i: jnp.maximum(i - steps, 0)
    tokens = (length, D)
    (
        down_sent, up_sent, down_own, up_own, output, grad_residual, g_own, g_theirs, g_own_high, g_theirs_high,
        dgain_mlp, out_own, out_sent,
    ) = call(
        feed_kernel,
        flags,
        (2 * steps,),
        [held(x), emb, held(att_own), held(att_other)]
        + w_half
        + [held(gains), held(cot)]
        + [
            (w_up, (D, FF_TILE), lambda i, f: (0, tile_at(i, f))),
            (w_down, (FF_TILE, D), lambda i, f: (tile_at(i, f), 0)),
        ],
        [
            ((ff_half, D), BF, (FF_TILE, D), lambda i, f: (sent_at(i), 0)),
            ((D, ff_half), BF, (D, FF_TILE), lambda i, f: (0, sent_at(i))),
            ((ff_half, D), BF, (FF_TILE, D), lambda i, f: (own_at(i), 0)),
            ((D, ff_half), BF, (D, FF_TILE), lambda i, f: (0, own_at(i))),
            (tokens, BF, tokens, lambda i, f: (0, 0)),
            (tokens, F32, tokens, lambda i, f: (0, 0)),
            out_held((GROUP, length), BF),
            out_held((GROUP, length), BF),
            out_held(half_rows, BF),
            out_held(half_rows, BF),
            out_held((1, D), F32),
            out_held((GROUP, D), BF),
            out_held((GROUP, D), BF),
        ],
        BRIEF,
        "feed",
        [pltpu.VMEM(tokens, F32), pltpu.VMEM(tokens, BF)]
        + [pltpu.VMEM(tokens, F32)] * 2
        + [pltpu.VMEM((length, FF_TILE), BF)] * 2,
        6,
    )
    (
        down_sent, up_sent, down_own, up_own, output, grad_residual, g_own, g_theirs, g_own_high, g_theirs_high,
        dgain_mlp, out_own, out_sent, att_early, lse_early,
    ) = tie(
        down_sent, up_sent, down_own, up_own, output, grad_residual, g_own, g_theirs, g_own_high, g_theirs_high,
        dgain_mlp, out_own, out_sent, att_early, lse_early,
    )
    g_other = swap(g_theirs, core)
    early_g = (to_early(g_own_high), to_early(g_theirs_high, 1))
    g_other, down_sent, up_sent, out_sent = tie(g_other, down_sent, up_sent, out_sent)
    out_recv, down_recv, up_recv = (swap(a, core) for a in (out_sent, down_sent, up_sent))

    accumulators = [pltpu.VMEM((2, HEAD_DIM, length), F32)] * 2

    def local_back(at, heads, g0, g1):
        return call(
            local_back_kernel,
            flags,
            (heads,),
            [head(a, base + at) for base in (0, 6, 12) for a in (own, other)]
            + [head(a, at) for a in (g0, g1, att_own, att_pair)]
            + [(lse, (1, 2, length), lambda h, f: (at + h, 0, 0))],
            [((3, heads * HEAD_DIM, length), BF, (3, HEAD_DIM, length), lambda h, f: (0, h, 0))] * 2,
            BRIEF,
            "attend_back_local",
            accumulators,
        )

    d_0 = local_back(0, 2, g_own, g_other)
    d_0, early_g_own, out_own = tie(d_0, early_g[0], out_own)
    early_g = (early_g_own, early_g[1])
    opened = whole_call(
        functools.partial(open_kernel, at=[steps_[0][3] for steps_ in orders]),
        flags,
        [down_own, down_recv, up_own, up_recv, out_own, out_recv],
        [shape for shape in (((ff_half - GROUP) // 2, D), (GROUP, ff_half), (GROUP, D)) for _ in (0, 1)],
        "open",
    )
    first = [Chain(orders[i], 1, *opened[2 * i : 2 * i + 2]) for i in range(3)]
    (early_g,) = send(first, early_g)
    dq_cross, dkv_cross = call(
        cross_back_kernel,
        flags,
        (HALF_HEADS,),
        cross_in
        + [
            head(early_g[0], 0),
            head(early_g[1], 0),
            (att_early, (2, HEAD_DIM, length), lambda h, f: (0, h, 0)),
            lse_spec(lse_early),
            head(g_own, 0),
            head(g_other, 0),
            head(att_own, 0),
            head(att_pair, 0),
            lse_spec(lse),
        ],
        [
            pair_out,
            (
                (2, 2, HALF, length),
                BF,
                (2, 2, HEAD_DIM, length),
                lambda h, f: (0, 0, h, 0),
            ),
        ],
        BRIEF,
        "attend_back_cross",
        accumulators,
    )
    dq_cross, dkv_cross, g_own, g_other = tie(dq_cross, dkv_cross, g_own, g_other)
    dq_back, dkv_back = to_late(dq_cross), to_early(dkv_cross)
    d_1 = local_back(2, 2, g_own, g_other)
    (d_1,) = beside(first, d_1)
    land(flags, first)
    g_own, g_other = send(first, g_own, g_other)
    d_2 = local_back(4, 2, g_own, g_other)
    d_2, dq_back, dkv_back = beside(first, d_2, dq_back, dkv_back)
    land(flags, first)
    d_2, dq_back, dkv_back = send(first, d_2, dq_back, dkv_back)
    few = (1, 2 * HEAD_DIM, length)
    one_q = (1, 2, HALF, length)
    gp_own, gp_pair = call(
        combine_kernel,
        flags,
        (3,),
        [(d, few, lambda i, f: (i, 0, 0)) for d in (*d_0, *d_1, *d_2)]
        + [
            fixed(dq_cross.reshape(one_q)),
            fixed(dq_back.reshape(one_q)),
            (dkv_cross, one_q, lambda i, f: (jnp.maximum(i - 1, 0), 0, 0, 0)),
            (dkv_back, one_q, lambda i, f: (jnp.maximum(i - 1, 0), 0, 0, 0)),
        ],
        [((3 * GROUP, length), BF, (GROUP, length), lambda i, f: (i, 0))] * 2,
        BRIEF,
        "combine",
    )
    gp_other = swap(gp_pair, core)
    opened = call(
        functools.partial(project_grad_kernel, at=[ring[0][3], by_y[0][3]]),
        flags,
        (3,),
        [(g, (GROUP, length), lambda i, f: (i, 0)) for g in (gp_own, gp_pair)]
        + [fixed(normed), fixed(normed_other)],
        [((D // 4, 3 * GROUP), BF, (D // 4, GROUP), lambda i, f: (0, i))] * 4,
        BRIEF,
        "project_grad",
    )
    gp_own, gp_other, opened = beside(first, gp_own, gp_other, opened)
    second = [Chain(order, 2, *opened[2 * i : 2 * i + 2]) for i, order in enumerate((ring, lanes[:1] + [cross] + lanes[1:]))]
    land(flags, first)
    send(first + second)
    land(flags, first + second)
    gp_own, gp_other = send(first + second, gp_own, gp_other)
    grad_input, sums = call(
        input_grad_kernel,
        flags,
        (3,),
        [
            (gp_own, (GROUP, length), lambda i, f: (i, 0)),
            (gp_other, (GROUP, length), lambda i, f: (i, 0)),
            (w_qkv, (D, GROUP), lambda i, f: (0, 2 * i + f[1])),
            (w_qkv, (D, GROUP), lambda i, f: (0, 2 * i + 1 - f[1])),
            fixed(x),
            emb,
            fixed(gains),
            fixed(grad_residual),
            fixed(dgain_mlp),
        ],
        [out_fixed(tokens, BF), out_fixed((passes + 2, D), F32)],
        BRIEF,
        "input_grad",
        [pltpu.VMEM((D, length), F32)],
    )
    grad_input, sums = beside(first + second, grad_input, sums)
    land(flags, first + second)
    while second[1].plan[0][0] == HALVE:
        send(first + second)
        land(flags, first + second)
    rider = jnp.pad(sums, ((0, 8 - passes - 2), (0, 3 * GROUP - D))).astype(BF)
    second[1].sent, second[1].riders = jnp.concatenate([second[1].sent, rider]), 8
    while not first[0].done():
        send(first + second)
        land(flags, first + second)
    send(second)
    pairs = [(c.sent, swap(c.sent, core)) for c in first]
    (pairs,) = beside(second, pairs)
    land(flags, second)
    third = [a for pair in pairs for a in pair]
    at_most = [
        (third[i], (GROUP, D), lambda j, f: (jnp.minimum(j % 4, 2), 0)) for i in (0, 1)
    ] + [(third[i], (D, GROUP), lambda j, f: (0, j % 4)) for i in (2, 3)]
    down_total, up_total, out_total = call(
        assemble_first_kernel,
        flags,
        (8,),
        at_most + [fixed(third[4]), fixed(third[5])],
        [
            ((4 * D, D), F32, (GROUP, D), lambda j, f: (j, 0)),
            ((D, 4 * D), F32, (D, GROUP), lambda j, f: (0, j)),
            ((D, D), F32, (GROUP, D), lambda j, f: (j // 4, 0)),
        ],
        BRIEF,
        "assemble_first",
    )
    while not second[0].done():
        send(second)
        down_total, up_total, out_total = beside(second, down_total, up_total, out_total)
        land(flags, second)
    lasts = [(c.sent, swap(c.sent, core)) for c in second]
    small = sum(a[D // 2 :, :D].astype(F32) for a in lasts[1])
    qkv_total = call(
        assemble_second_kernel,
        flags,
        (6,),
        [
            (a, (GROUP, GROUP), lambda j, f: (0, j // 2))
            for pair in lasts
            for a in pair
        ],
        [((D, 3 * D), F32, (D, GROUP), lambda j, f: (0, j))],
        BRIEF,
        "assemble_second",
    )[0]
    return (
        output[None],
        grad_input[None],
        small[:passes],
        small[passes],
        qkv_total,
        out_total,
        small[passes + 1],
        up_total,
        down_total,
    )


def solution(mesh):
    sizes = (mesh.shape["pass"], mesh.shape["dp"])
    tokens = P("pass", "dp", None)
    in_specs = (tokens, P("dp")) + (P(),) * 7 + (tokens,)
    out_specs = (tokens, tokens) + (P(),) * 7
    return jax.shard_map(
        functools.partial(on_device, sizes),
        mesh=mesh,
        in_specs=in_specs,
        out_specs=out_specs,
        check_vma=False,
    )
```

```python
import functools
import math

import jax
import jax.numpy as jnp
from jax import lax
from jax.experimental import pallas as pl
from jax.experimental.pallas import tpu as pltpu
from jax.sharding import PartitionSpec as P

D = 768
HEADS = 12
HEAD_DIM = 64
SHORT = 256
FF_TILE = 512
GROUP = D // 2
HALF = GROUP // 2
HALF_HEADS = HEADS // 4
EPS = 1e-05
SCALE = HEAD_DIM**-0.5
SCALE2 = SCALE * math.log2(math.e)
BF = jnp.bfloat16
F32 = jnp.float32
PIECES, FIRST_HEADS = (2, 1), (0, 2)
BRIEF = 0.2


def dot(a, b, ca, cb):
    return lax.dot_general(a, b, (((ca,), (cb,)), ((), ())), preferred_element_type=F32)


def cost(us):
    return pl.CostEstimate(flops=int(us * 1.1e9), bytes_accessed=1 << 20, transcendentals=0)


def call(kernel, flags, grid, ins, outs, us, name, scratch=(), temporaries=8):
    blocks = [(math.prod(block), array.dtype) for array, block, index in ins if index]
    blocks += [(math.prod(block), dtype) for _, dtype, block, index in outs if index]
    blocks += [(math.prod(buffer.shape) // 2, buffer.dtype) for buffer in scratch]
    limit = sum(2 * n * jnp.dtype(dtype).itemsize for n, dtype in blocks) + (temporaries << 20)
    return pl.pallas_call(
        kernel,
        grid_spec=pltpu.PrefetchScalarGridSpec(
            num_scalar_prefetch=1,
            grid=grid,
            in_specs=[spec(block, index) for _, block, index in ins],
            out_specs=[spec(block, index) for _, _, block, index in outs],
            scratch_shapes=list(scratch),
        ),
        out_shape=[jax.ShapeDtypeStruct(shape, dtype) for shape, dtype, _, _ in outs],
        cost_estimate=cost(us),
        compiler_params=pltpu.CompilerParams(vmem_limit_bytes=min(limit, 60 << 20)),
        name=name,
    )(flags, *[array for array, _, _ in ins])


def fixed(array):
    return (array, array.shape, lambda i, f: (0,) * array.ndim)


def out_fixed(shape, dtype):
    return (shape, dtype, shape, lambda i, f: (0,) * len(shape))


def held(array):
    return (array, array.shape, None)


def out_held(shape, dtype):
    return (shape, dtype, shape, None)


def spec(block, index):
    return pl.BlockSpec(block, index) if index else pl.BlockSpec(memory_space=pltpu.VMEM)


def one_sequence(f):
    return f[0] == 1


def hidden_of(f, x_ref, emb_ref):
    return x_ref[...].astype(F32) + emb_ref[pl.ds(f[3], 1), :]


def centered(values):
    center = values - jnp.mean(values, axis=-1, keepdims=True)
    return center, lax.rsqrt(jnp.mean(center * center, axis=-1, keepdims=True) + EPS)


def write_part(f, part, refs, value):
    out_ref, *cross_refs = refs
    out_ref[...] = value
    for ref, first, heads in zip(cross_refs, FIRST_HEADS, PIECES, strict=True):
        start, rows = first * HEAD_DIM, heads * HEAD_DIM

        @pl.when((f[2] == 1) & (part > 0))
        def _():
            ref[pl.ds(pl.multiple_of((part - 1) * rows, rows), rows), :] = value[start : start + rows]

        @pl.when((f[2] == 0) & (part == 0))
        def _():
            ref[:rows] = value[HALF + start : HALF + start + rows]
            ref[rows:] = jnp.zeros_like(ref[rows:])


def norm_project_kernel(f, x_ref, emb_ref, gain_ref, w_ref, normed_ref, *refs):
    part = pl.program_id(0)

    @pl.when(part == 0)
    def _():
        center, inv = centered(hidden_of(f, x_ref, emb_ref))
        normed_ref[...] = (center * inv * gain_ref[0:1]).T.astype(BF)

    write_part(f, part, refs, dot(w_ref[...], normed_ref[...], 0, 0).astype(BF))


def project_kernel(f, normed_ref, w_ref, *refs):
    write_part(f, pl.program_id(0), refs, dot(w_ref[...], normed_ref[...], 0, 0).astype(BF))


def projection_outs(length):
    outs = [((3 * GROUP, length), BF, (GROUP, length), lambda i, f: (i, 0))]
    for heads in PIECES:
        outs.append(out_fixed((2 * heads * HEAD_DIM, length), BF))
    return outs


def mask_tail(scores):
    n = scores.shape[0]
    key = lax.broadcasted_iota(jnp.int32, (SHORT, SHORT), 0)
    query = lax.broadcasted_iota(jnp.int32, (SHORT, SHORT), 1)
    diag = jnp.where(key <= query, scores[n - SHORT :], -1e30)
    return diag if n == SHORT else jnp.concatenate([scores[: n - SHORT], diag], 0)


def sweep(f, length, tile, variants):
    for condition, units in variants:
        for whole in (True, False):

            @pl.when(condition & (one_sequence(f) == whole))
            def _():
                for at in range(length // SHORT):
                    for unit in units:
                        tile(unit, at, 0 if whole else at)


def spans(at, first):
    return slice(at * SHORT, (at + 1) * SHORT), slice(first * SHORT, (at + 1) * SHORT)


def softmax_tile(q_refs, k_refs, v_refs, o_refs, lse_ref, unit, at, first):
    qp, keys = unit
    qs, ks = spans(at, first)
    q = q_refs[qp][:, qs]
    scores = [mask_tail(dot(k_refs[kp][:, ks], q, 0, 0) * SCALE2) for kp in keys]
    top = functools.reduce(jnp.maximum, [jnp.max(s, axis=0, keepdims=True) for s in scores])
    raw = [jnp.exp2(s - top) for s in scores]
    total = functools.reduce(jnp.add, [jnp.sum(p, axis=0, keepdims=True) for p in raw])
    out = functools.reduce(
        jnp.add, [dot(v_refs[kp][:, ks], p.astype(BF), 1, 0) for kp, p in zip(keys, raw)]
    )
    o_refs[qp][:, qs] = (out * (1.0 / total)).astype(o_refs[qp].dtype)
    lse_ref[0, qp : qp + 1, qs] = top + jnp.log2(total)


LOCAL_UNITS = (
    lambda f: (f[1] == 0, [(0, [0]), (1, [0, 1])]),
    lambda f: (f[1] == 1, [(1, [1]), (0, [0, 1])]),
)
CROSS_UNITS = [(0, [0, 1]), (1, [0, 1])]


def local_kernel(f, q0, q1, k0, k1, v0, v1, o0, o1, lse_ref):
    sweep(
        f,
        q0.shape[1],
        functools.partial(softmax_tile, (q0, q1), (k0, k1), (v0, v1), (o0, o1), lse_ref),
        [unit(f) for unit in LOCAL_UNITS],
    )


def cross_kernel(f, *refs):
    ins, (o_ref, lse_ref) = refs[:12], refs[12:]
    outs = (o_ref.at[0], o_ref.at[1])
    for early, at in ((1, 0), (0, 6)):
        q0, q1, k0, k1, v0, v1 = ins[at : at + 6]
        sweep(
            f,
            q0.shape[1],
            functools.partial(softmax_tile, (q0, q1), (k0, k1), (v0, v1), outs, lse_ref),
            [(f[2] == early, CROSS_UNITS)],
        )


def head(array, at):
    return (array, (HEAD_DIM, array.shape[-1]), lambda h, f: (at + h, 0))


def lse_spec(array):
    return (array, (1,) + array.shape[1:], lambda h, f: (h, 0, 0))


def lse_out(heads, length):
    return ((heads, 2, length), F32, (1, 2, length), lambda h, f: (h, 0, 0))


def cross_inputs(far, own, other, first, heads):
    high = HALF_HEADS + first
    return [
        head(far[0], 0),
        head(far[1], 0),
        head(own, 6 + high),
        head(other, 6 + high),
        head(own, 12 + high),
        head(other, 12 + high),
        head(own, first),
        head(other, first),
        head(far[0], 0),
        head(far[1], 0),
        head(far[0], heads),
        head(far[1], heads),
    ]


def merge_kernel(
    f, la0, la1, lsea, lb0, lb1, lseb, ca, lseca, cb, lsecb, ba, lseba, bb, lsebb,
    a0, a1, lse_out, high_ref, lse_high,
):
    def rows(h):
        return slice(h * HEAD_DIM, (h + 1) * HEAD_DIM)

    def put(h, i, value, lse):
        value = value.astype(BF)
        (a0, a1)[i][rows(h)] = value
        lse_out[h, i : i + 1] = lse
        if h >= HALF_HEADS:
            high_ref[i, rows(h - HALF_HEADS)] = value
            lse_high[h - HALF_HEADS, i : i + 1] = lse

    for h in range(2 * HALF_HEADS):
        local, lse_l, at = ((la0, la1), lsea, h) if h < 4 else ((lb0, lb1), lseb, h - 4)
        low, there = h < HALF_HEADS, h % HALF_HEADS
        if there < PIECES[0]:
            far, lse_c = (ca, lseca) if low else (ba, lseba)
        else:
            far, lse_c, there = (cb, lsecb, 0) if low else (bb, lsebb, 0)
        for i in (0, 1):
            near, lse_near = local[i][rows(at)], lse_l[at, i : i + 1]

            @pl.when(f[2] == 1)
            def _():
                put(h, i, near, lse_near)

            @pl.when(f[2] == 0)
            def _():
                lse_far = lse_c[there, i : i + 1]
                top = jnp.maximum(lse_near, lse_far)
                lse = top + jnp.log2(jnp.exp2(lse_near - top) + jnp.exp2(lse_far - top))
                value = near * jnp.exp2(lse_near - lse) + far[i, rows(there)].astype(F32) * jnp.exp2(
                    lse_far - lse
                )
                put(h, i, value, lse)


def gradient_tile(
    q_refs, k_refs, v_refs, g_refs, o_refs, lse_ref, dq_refs, dk_acc, dv_acc, unit, at, first
):
    qp, keys = unit
    qs, ks = spans(at, first)
    q, g = q_refs[qp][:, qs], g_refs[qp][:, qs]
    lse = lse_ref[0, qp : qp + 1, qs]
    delta = jnp.sum(g.astype(F32) * o_refs[qp][:, qs].astype(F32), axis=0, keepdims=True)
    dq = None
    for kp in keys:
        k, v = k_refs[kp][:, ks], v_refs[kp][:, ks]
        weights = jnp.exp2(mask_tail(dot(k, q, 0, 0) * SCALE2) - lse)
        ds = (weights * (dot(v, g, 0, 0) - delta)).astype(BF)
        term = dot(k, ds, 1, 0)
        dq = term if dq is None else dq + term
        dk_acc[kp, :, ks] += dot(q, ds, 1, 1)
        dv_acc[kp, :, ks] += dot(g, weights.astype(BF), 1, 1)
    dq_refs[qp][:, qs] = (dq * SCALE).astype(BF)


def local_back_kernel(
    f, q0, q1, k0, k1, v0, v1, g0, g1, o0, o1, lse_ref, d0, d1, dk_acc, dv_acc
):
    dk_acc[...] = jnp.zeros_like(dk_acc)
    dv_acc[...] = jnp.zeros_like(dv_acc)
    sweep(
        f,
        q0.shape[1],
        functools.partial(
            gradient_tile,
            (q0, q1),
            (k0, k1),
            (v0, v1),
            (g0, g1),
            (o0, o1),
            lse_ref,
            (d0.at[0], d1.at[0]),
            dk_acc,
            dv_acc,
        ),
        [unit(f) for unit in LOCAL_UNITS],
    )
    for i, ref in ((0, d0), (1, d1)):
        ref[1] = (dk_acc[i] * SCALE).astype(BF)
        ref[2] = dv_acc[i].astype(BF)


def cross_back_kernel(f, *refs):
    ins, more = refs[:12], refs[12:]
    (ga0, ga1, oa, lse_a, gb0, gb1, ob0, ob1, lse_b, kept_ref, sent_ref, dk_acc, dv_acc) = more
    dk_acc[...] = jnp.zeros_like(dk_acc)
    dv_acc[...] = jnp.zeros_like(dv_acc)
    for early, at, grads, outs, lse_ref, dq_ref in (
        (1, 0, (ga0, ga1), (oa.at[0], oa.at[1]), lse_a, sent_ref),
        (0, 6, (gb0, gb1), (ob0, ob1), lse_b, kept_ref),
    ):
        q0, q1, k0, k1, v0, v1 = ins[at : at + 6]
        sweep(
            f,
            q0.shape[1],
            functools.partial(
                gradient_tile,
                (q0, q1),
                (k0, k1),
                (v0, v1),
                grads,
                outs,
                lse_ref,
                (dq_ref.at[0, 0], dq_ref.at[0, 1]),
                dk_acc,
                dv_acc,
            ),
            [(f[2] == early, CROSS_UNITS)],
        )
    for early, dkv_ref, dq_ref in ((1, kept_ref, sent_ref), (0, sent_ref, kept_ref)):

        @pl.when(f[2] == early)
        def _():
            for i in (0, 1):
                dkv_ref[0, i] = (dk_acc[i] * SCALE).astype(BF)
                dkv_ref[1, i] = dv_acc[i].astype(BF)
            dq_ref[1] = jnp.zeros_like(dq_ref[1])


def gelu_pair(u):
    k = math.sqrt(2 / math.pi)
    square = u * u
    t = jnp.tanh(k * u * (1.0 + 0.044715 * square))
    half = 0.5 + 0.5 * t
    slope = half + 0.5 * u * (1.0 - t * t) * (k * (1.0 + 3 * 0.044715 * square))
    return u * half, slope


def chunks(length):
    return [slice(at, at + SHORT) for at in range(0, length, SHORT)]


def ff_tile(n_ref, cot_ref, wu_ref, wd_ref, y_ref, c_ref, act_ref, gup_ref):
    for at in chunks(n_ref.shape[0]):
        act, slope = gelu_pair(dot(n_ref[at], wu_ref[...], 1, 0))
        act = act.astype(BF)
        grad_up = (dot(cot_ref[at], wd_ref[...], 1, 1) * slope).astype(BF)
        act_ref[at], gup_ref[at] = act, grad_up
        y_ref[at] += dot(act, wd_ref[...], 1, 0)
        c_ref[at] += dot(grad_up, wu_ref[...], 1, 1)


def feed_kernel(
    f, x_ref, emb_ref, a_ref, b_ref, wa_ref, wb_ref, gain_ref, cot_ref, wu_ref, wd_ref,
    dds_ref, dus_ref, ddo_ref, duo_ref, out_ref, gres_ref, ga_ref, gb_ref, gah_ref, gbh_ref, dgain_ref, dwa_ref, dwb_ref,
    res_ref, n_ref, nt_ref, y_ref, c_ref, act_ref, gup_ref,
):
    step, steps = pl.program_id(0), pl.num_programs(0)

    @pl.when(step == 0)
    def _():
        for at in chunks(n_ref.shape[0]):
            residual = (
                x_ref[at].astype(F32)
                + emb_ref[pl.ds(f[3], 1), :]
                + dot(a_ref[:, at], wa_ref[...], 0, 0)
                + dot(b_ref[:, at], wb_ref[...], 0, 0)
            )
            res_ref[at] = residual
            center, inv = centered(residual)
            normed2 = center * inv * gain_ref[1:2]
            n_ref[at] = normed2.astype(BF)
            nt_ref[:, at] = normed2.T.astype(BF)
            y_ref[at] = residual
            c_ref[at] = jnp.zeros_like(residual)

    ff_tile(n_ref, cot_ref, wu_ref, wd_ref, y_ref, c_ref, act_ref, gup_ref)
    down = dot(act_ref[...], cot_ref[...], 0, 0).astype(BF)
    up = dot(nt_ref[...], gup_ref[...], 1, 0).astype(BF)

    @pl.when(step < steps // 2)
    def _():
        dds_ref[...], dus_ref[...] = down, up

    @pl.when(step >= steps // 2)
    def _():
        ddo_ref[...], duo_ref[...] = down, up

    @pl.when(step == steps - 1)
    def _():
        dgain = None
        grads = []
        for at in chunks(n_ref.shape[0]):
            out_ref[at] = y_ref[at].astype(BF)
            center, inv = centered(res_ref[at])
            n2 = center * inv
            c = c_ref[at]
            part = jnp.sum(c * n2, axis=0, keepdims=True)
            dgain = part if dgain is None else dgain + part
            e = c * gain_ref[1:2]
            grad = cot_ref[at].astype(F32) + inv * (
                e
                - jnp.mean(e, axis=-1, keepdims=True)
                - n2 * jnp.mean(e * n2, axis=-1, keepdims=True)
            )
            gres_ref[at] = grad
            grad = grad.astype(BF)
            grads.append(grad)
            mine = dot(wa_ref[...], grad, 1, 1).astype(BF)
            theirs = dot(wb_ref[...], grad, 1, 1).astype(BF)
            ga_ref[:, at], gb_ref[:, at] = mine, theirs
            gah_ref[:, at], gbh_ref[:, at] = mine[HALF:], theirs[HALF:]
        dgain_ref[...] = dgain
        grad = jnp.concatenate(grads, 0)
        dwa_ref[...] = dot(a_ref[...], grad, 1, 0).astype(BF)
        dwb_ref[...] = dot(b_ref[...], grad, 1, 0).astype(BF)


def combine_kernel(f, da0, da1, db0, db1, dc0, dc1, kept_ref, came_ref, g0, g1):
    part = pl.program_id(0)
    late, early = f[2] == 0, f[2] == 1

    def put(low, high):
        for i, (refs, g) in enumerate((((da0, db0, dc0), g0), ((da1, db1, dc1), g1))):
            local = jnp.concatenate([d[0] for d in refs], 0)
            if low is None:
                g[...] = local
            else:
                more = jnp.concatenate([low[0, i], high[0, i]], 0)
                g[...] = (local.astype(F32) + more.astype(F32)).astype(BF)

    @pl.when(late & (part == 0))
    def _():
        put(kept_ref, came_ref)

    @pl.when(early & (part > 0))
    def _():
        put(came_ref, kept_ref)

    @pl.when((late & (part > 0)) | (early & (part == 0)))
    def _():
        put(None, None)


def project_grad_kernel(f, g0, g1, n0_ref, n1_ref, s0_ref, k0_ref, s1_ref, k1_ref, *, at):
    value = dot(n0_ref[...], g0[...], 1, 1) + dot(n1_ref[...], g1[...], 1, 1)
    for i, (sent_ref, kept_ref) in enumerate(((s0_ref, k0_ref), (s1_ref, k1_ref))):
        sent, kept = pick(f[at[i]], value[i * (D // 2) : (i + 1) * (D // 2)])
        sent_ref[...] = sent.astype(BF)
        kept_ref[...] = kept.astype(BF)


def input_grad_kernel(
    f, g_ref, h_ref, wg_ref, wh_ref, x_ref, emb_ref, gain_ref, gres_ref, dgain_ref, gin_ref, sums_ref, acc
):
    part = pl.program_id(0)
    value = dot(wg_ref[...], g_ref[...], 1, 0) + dot(wh_ref[...], h_ref[...], 1, 0)

    @pl.when(part == 0)
    def _():
        acc[...] = value

    @pl.when(part > 0)
    def _():
        acc[...] += value

    @pl.when(part == pl.num_programs(0) - 1)
    def _():
        center, inv = centered(hidden_of(f, x_ref, emb_ref))
        n1 = center * inv
        grad = acc[...].T
        e = grad * gain_ref[0:1]
        total = gres_ref[...] + inv * (
            e - jnp.mean(e, axis=-1, keepdims=True) - n1 * jnp.mean(e * n1, axis=-1, keepdims=True)
        )
        gin_ref[...] = total.astype(BF)
        sums = jnp.sum(total, axis=0, keepdims=True)
        passes = sums_ref.shape[0] - 2
        for i in range(passes):
            sums_ref[i : i + 1] = jnp.where(f[3] == i, sums, 0.0)
        sums_ref[passes : passes + 1] = jnp.sum(grad * n1, axis=0, keepdims=True)
        sums_ref[passes + 1 :] = dgain_ref[...]


def assemble_first_kernel(f, d_own, d_oth, u_own, u_oth, m_own, m_oth, down_ref, up_ref, out_ref):
    step = pl.program_id(0)
    half, at = step // 4, step % 4
    for mine, d, u, m in ((True, d_own, u_own, m_own), (False, d_oth, u_oth, m_oth)):
        here = (half == f[1]) == mine

        @pl.when(here)
        def _():
            up_ref[...] = u[...].astype(F32)

        @pl.when(here & (at < 3))
        def _():
            down_ref[...] = d[...].astype(F32)

        @pl.when(here & (at == 3))
        def _():
            down_ref[...] = m[:GROUP].astype(F32)
            out_ref[...] = m[GROUP:].astype(F32)


def assemble_second_kernel(f, a_own, a_oth, b_own, b_oth, out_ref):
    for mine, a, b in ((True, a_own, b_own), (False, a_oth, b_oth)):

        @pl.when((pl.program_id(0) % 2 == f[1]) == mine)
        def _():
            out_ref[:GROUP] = a[...].astype(F32)
            out_ref[GROUP:] = b[...].astype(F32)


def swap(array, step):
    axis, mask, size, _ = step
    return lax.ppermute(array, axis, [(i, i ^ mask) for i in range(size)])


def tie(*groups):
    leaves, tree = jax.tree.flatten(groups)
    return jax.tree.unflatten(tree, lax.optimization_barrier(leaves))


def pick(here, total):
    half = total.shape[0] // 2
    low, high = total[:half], total[half:]
    return jnp.where(here == 0, high, low), jnp.where(here == 0, low, high)


def joined(here, own, other):
    return jnp.where(
        here == 0, jnp.concatenate([own, other], 0), jnp.concatenate([other, own], 0)
    )


def round_work(here, own, came, mode, riders):
    if mode == "join":
        cut = own.shape[0] - riders
        value = joined(here, own[:cut], came[:cut])
        return (jnp.concatenate([value, own[cut:] + came[cut:]], 0) if riders else value,)
    total = own + came
    return (total,) if mode == "sum" else pick(here, total)


def round_kernel(f, *refs, modes, at, riders):
    refs = list(refs)
    ins, outs = refs[: 2 * len(modes)], refs[2 * len(modes) :]
    for i, mode in enumerate(modes):
        own, came = ins[2 * i][...].astype(F32), ins[2 * i + 1][...].astype(F32)
        for value in round_work(f[at[i]], own, came, mode, riders[i]):
            outs.pop(0)[...] = value.astype(BF)


def whole_call(kernel, flags, ins, outs, name):
    vmem = pl.BlockSpec(memory_space=pltpu.VMEM)
    size = sum(math.prod(shape) for shape in [a.shape for a in ins] + outs)
    return pl.pallas_call(
        kernel,
        in_specs=[pl.BlockSpec(memory_space=pltpu.SMEM)] + [vmem] * len(ins),
        out_specs=[vmem] * len(outs),
        out_shape=[jax.ShapeDtypeStruct(shape, BF) for shape in outs],
        cost_estimate=cost(BRIEF),
        compiler_params=pltpu.CompilerParams(vmem_limit_bytes=2 * size + (8 << 20)),
        name=name,
    )(flags, *ins)


HALVE, FULL, JOIN = 0, 1, 2


class Chain:
    def __init__(self, steps, whole_steps, sent, kept):
        cut = len(steps) - whole_steps
        self.plan = (
            [(HALVE, step) for step in steps[:cut]]
            + [(FULL, step) for step in steps[cut:]]
            + [(JOIN, step) for step in reversed(steps[:cut])]
        )
        self.sent, self.kept, self.came, self.riders = sent, kept, None, 0

    def done(self):
        return not self.plan


def land(flags, chains):
    chains = [c for c in chains if c.came is not None]
    modes, at, ins, outs, riders = [], [], [], [], [c.riders for c in chains]
    for c in chains:
        what, step = c.plan.pop(0)
        own = c.kept if what == HALVE else c.sent
        rows, columns = own.shape
        if what == JOIN:
            modes.append("join")
            at.append(step[3])
            outs += [(2 * rows - c.riders, columns)]
        elif c.plan and c.plan[0][0] == HALVE:
            modes.append("split")
            at.append(c.plan[0][1][3])
            outs += [(rows // 2, columns)] * 2
        else:
            modes.append("sum")
            at.append(0)
            outs += [(rows, columns)]
        ins += [own, c.came]
    if all(shape[0] % 8 == 0 for shape in outs):
        kernel = functools.partial(round_kernel, modes=modes, at=at, riders=riders)
        results = list(whole_call(kernel, flags, ins, outs, "round"))
    else:
        results = []
        for i, mode in enumerate(modes):
            own, came = (a.astype(F32) for a in ins[2 * i : 2 * i + 2])
            results += [
                v.astype(BF) for v in round_work(flags[at[i]], own, came, mode, riders[i])
            ]
    for c, mode in zip(chains, modes, strict=True):
        c.came, c.sent = None, results.pop(0)
        if mode == "split":
            c.kept = results.pop(0)


def open_kernel(f, dd, ddr, du, dur, dw, dwr, *outs, at):
    def add(left, right):
        return left[...].astype(F32) + right[...].astype(F32)

    down, up, out = add(dd, ddr), add(du, dur), add(dw, dwr)
    cut = down.shape[0] - GROUP
    for i, value in enumerate((down[:cut], up, jnp.concatenate([down[cut:], out], 0))):
        sent, kept = pick(f[at[i]], value)
        outs[2 * i][...] = sent.astype(BF)
        outs[2 * i + 1][...] = kept.astype(BF)


def beside(chains, *more):
    chains = [c for c in chains if c.came is not None]
    arrays, more = tie([c.came for c in chains], more)
    for c, array in zip(chains, arrays, strict=True):
        c.came = array
    return more


def send(chains, *more):
    chains = [c for c in chains if not c.done()]
    loads, more = tie([c.sent for c in chains], more)
    for c, load in zip(chains, loads, strict=True):
        c.sent, c.came = load, swap(load, c.plan[0][1])
    return more


def on_device(
    sizes, block_input, segments, pass_emb, gain_attn, w_qkv, w_out, gain_mlp, w_up, w_down, cotangent
):
    passes, n_dp = sizes
    core = ("pass", 1, passes, 1)
    cross = ("pass", 2, passes, 4)
    lanes = [("dp", 1 << i, n_dp, 5 + i) for i in range(n_dp.bit_length() - 1)]
    ring = [cross] + lanes
    by_y = lanes[:1] + [cross] + lanes[:0:-1]
    orders = [ring, by_y, ring[2:] + ring[:2]]

    pass_here = lax.axis_index("pass")
    core_here = pass_here & 1
    length = segments.shape[0]
    flags = jnp.stack(
        [
            (segments[0] == segments[length - 1]).astype(jnp.int32),
            core_here.astype(jnp.int32),
            (pass_here < 2).astype(jnp.int32),
            pass_here.astype(jnp.int32),
        ]
        + [
            (lax.axis_index(axis) >> (mask.bit_length() - 1)) & 1 for axis, mask, _, _ in ring
        ]
    )

    x, cot = block_input[0], cotangent[0]
    emb = fixed(pass_emb)
    gains = jnp.stack([gain_attn, gain_mlp])

    normed, theirs, *theirs_cross = call(
        norm_project_kernel,
        flags,
        (3,),
        [fixed(x), emb, fixed(gains), (w_qkv, (D, GROUP), lambda i, f: (0, 2 * i + 1 - f[1]))],
        [out_fixed((D, length), BF)] + projection_outs(length),
        BRIEF,
        "norm_project",
    )
    other = swap(theirs, core)
    own, *own_cross = call(
        project_kernel,
        flags,
        (3,),
        [fixed(normed), (w_qkv, (D, GROUP), lambda i, f: (0, 2 * i + f[1]))],
        projection_outs(length),
        BRIEF,
        "project_own",
    )

    across = ("pass", 3, passes, 0)

    def exchange(piece):
        return swap(own_cross[piece], cross), swap(theirs_cross[piece], across)

    def attend_local(first, heads):
        return call(
            local_kernel,
            flags,
            (heads,),
            [head(a, at + first) for at in (0, 6, 12) for a in (own, other)],
            [((heads * HEAD_DIM, length), F32, (HEAD_DIM, length), lambda h, f: (h, 0))] * 2
            + [lse_out(heads, length)],
            BRIEF,
            "attend_local",
        )

    def attend_cross(piece, far):
        heads = PIECES[piece]
        return call(
            cross_kernel,
            flags,
            (heads,),
            cross_inputs(far, own, other, FIRST_HEADS[piece], heads),
            [
                ((2, heads * HEAD_DIM, length), BF, (2, HEAD_DIM, length), lambda h, f: (0, h, 0)),
                lse_out(heads, length),
            ],
            BRIEF,
            "attend_cross",
        )

    far_0 = exchange(0)
    local_0 = attend_local(0, 4)
    far_0, local_0, own_cross, theirs_cross = tie(far_0, local_0, own_cross, theirs_cross)
    far_1 = exchange(1)
    normed_other = swap(normed, core)
    cross_0 = attend_cross(0, far_0)
    far_1, cross_0 = tie(far_1, cross_0)
    o_back_0 = swap(cross_0[0], cross)
    cross_1 = attend_cross(1, far_1)
    cross_1, own, other = tie(cross_1, own, other)
    o_back_1, lse_back_1, lse_back_0 = (
        swap(a, cross) for a in (cross_1[0], cross_1[1], cross_0[1])
    )
    local_1 = attend_local(4, 2)
    o_back_0, o_back_1, lse_back_0, lse_back_1, local_1 = tie(
        o_back_0, o_back_1, lse_back_0, lse_back_1, local_1
    )
    half_rows = (HALF, length)
    att_own, att_pair, lse, att_high, lse_high = call(
        merge_kernel,
        flags,
        (1,),
        [
            fixed(a)
            for a in (*local_0, *local_1, *cross_0, *cross_1, o_back_0, lse_back_0, o_back_1, lse_back_1)
        ],
        [out_fixed((GROUP, length), BF)] * 2
        + [
            out_fixed((HEADS // 2, 2, length), F32),
            out_fixed((2, HALF, length), BF),
            out_fixed((HALF_HEADS, 2, length), F32),
        ],
        BRIEF,
        "merge",
    )
    far = [
        jnp.concatenate([a[: 2 * HEAD_DIM], b[:HEAD_DIM], a[2 * HEAD_DIM :], b[HEAD_DIM:]])
        for a, b in zip(far_0, far_1, strict=True)
    ]
    cross_in = cross_inputs(far, own, other, 0, HALF_HEADS)
    att_other = swap(att_pair, core)
    att_early, lse_early = swap(att_high, cross), swap(lse_high, cross)
    att_own, att_other, normed_other = tie(att_own, att_other, normed_other)

    w_half = [(w_out, (GROUP, D), lambda i, f: (f[1], 0)), (w_out, (GROUP, D), lambda i, f: (1 - f[1], 0))]
    ff_half = w_up.shape[1] // 2
    steps = ff_half // FF_TILE

    def tile_at(i, f):
        return jnp.where(i < steps, 1 - f[1], f[1]) * steps + i % steps

    sent_at, own_at = lambda i: jnp.minimum(i, steps - 1), lambda i: jnp.maximum(i - steps, 0)
    tokens = (length, D)
    (
        down_sent, up_sent, down_own, up_own, output, grad_residual, g_own, g_theirs, g_own_high, g_theirs_high,
        dgain_mlp, out_own, out_sent,
    ) = call(
        feed_kernel,
        flags,
        (2 * steps,),
        [held(x), emb, held(att_own), held(att_other)]
        + w_half
        + [held(gains), held(cot)]
        + [
            (w_up, (D, FF_TILE), lambda i, f: (0, tile_at(i, f))),
            (w_down, (FF_TILE, D), lambda i, f: (tile_at(i, f), 0)),
        ],
        [
            ((ff_half, D), BF, (FF_TILE, D), lambda i, f: (sent_at(i), 0)),
            ((D, ff_half), BF, (D, FF_TILE), lambda i, f: (0, sent_at(i))),
            ((ff_half, D), BF, (FF_TILE, D), lambda i, f: (own_at(i), 0)),
            ((D, ff_half), BF, (D, FF_TILE), lambda i, f: (0, own_at(i))),
            (tokens, BF, tokens, lambda i, f: (0, 0)),
            (tokens, F32, tokens, lambda i, f: (0, 0)),
            out_held((GROUP, length), BF),
            out_held((GROUP, length), BF),
            out_held(half_rows, BF),
            out_held(half_rows, BF),
            out_held((1, D), F32),
            out_held((GROUP, D), BF),
            out_held((GROUP, D), BF),
        ],
        BRIEF,
        "feed",
        [pltpu.VMEM(tokens, F32), pltpu.VMEM(tokens, BF), pltpu.VMEM((D, length), BF)]
        + [pltpu.VMEM(tokens, F32)] * 2
        + [pltpu.VMEM((length, FF_TILE), BF)] * 2,
        6,
    )
    (
        down_sent, up_sent, down_own, up_own, output, grad_residual, g_own, g_theirs, g_own_high, g_theirs_high,
        dgain_mlp, out_own, out_sent, att_early, lse_early,
    ) = tie(
        down_sent, up_sent, down_own, up_own, output, grad_residual, g_own, g_theirs, g_own_high, g_theirs_high,
        dgain_mlp, out_own, out_sent, att_early, lse_early,
    )
    g_other = swap(g_theirs, core)
    early_g = (swap(g_own_high, cross), swap(g_theirs_high, across))
    g_other, down_sent, up_sent, out_sent = tie(g_other, down_sent, up_sent, out_sent)
    out_recv, down_recv, up_recv = (swap(a, core) for a in (out_sent, down_sent, up_sent))

    accumulators = [pltpu.VMEM((2, HEAD_DIM, length), F32)] * 2

    def local_back(at, heads, g0, g1):
        return call(
            local_back_kernel,
            flags,
            (heads,),
            [head(a, base + at) for base in (0, 6, 12) for a in (own, other)]
            + [head(a, at) for a in (g0, g1, att_own, att_pair)]
            + [(lse, (1, 2, length), lambda h, f: (at + h, 0, 0))],
            [((3, heads * HEAD_DIM, length), BF, (3, HEAD_DIM, length), lambda h, f: (0, h, 0))] * 2,
            BRIEF,
            "attend_back_local",
            accumulators,
        )

    d_0 = local_back(0, 2, g_own, g_other)
    d_0, early_g_own, out_own = tie(d_0, early_g[0], out_own)
    early_g = (early_g_own, early_g[1])
    opened = whole_call(
        functools.partial(open_kernel, at=[steps_[0][3] for steps_ in orders]),
        flags,
        [down_own, down_recv, up_own, up_recv, out_own, out_recv],
        [shape for shape in (((ff_half - GROUP) // 2, D), (GROUP, ff_half), (GROUP, D)) for _ in (0, 1)],
        "open",
    )
    first = [Chain(orders[i], 1, *opened[2 * i : 2 * i + 2]) for i in range(3)]
    (early_g,) = send(first, early_g)
    cross_kept, cross_sent = call(
        cross_back_kernel,
        flags,
        (HALF_HEADS,),
        cross_in
        + [
            head(early_g[0], 0),
            head(early_g[1], 0),
            (att_early, (2, HEAD_DIM, length), lambda h, f: (0, h, 0)),
            lse_spec(lse_early),
            head(g_own, 0),
            head(g_other, 0),
            head(att_own, 0),
            head(att_pair, 0),
            lse_spec(lse),
        ],
        [((2, 2, HALF, length), BF, (2, 2, HEAD_DIM, length), lambda h, f: (0, 0, h, 0))] * 2,
        BRIEF,
        "attend_back_cross",
        accumulators,
    )
    cross_kept, cross_sent, g_own, g_other = tie(cross_kept, cross_sent, g_own, g_other)
    cross_came = swap(cross_sent, cross)
    d_1 = local_back(2, 2, g_own, g_other)
    (d_1,) = beside(first, d_1)
    land(flags, first)
    g_own, g_other = send(first, g_own, g_other)
    d_2 = local_back(4, 2, g_own, g_other)
    d_2, cross_came = beside(first, d_2, cross_came)
    land(flags, first)
    d_2, cross_came = send(first, d_2, cross_came)
    few = (1, 2 * HEAD_DIM, length)
    one_part = (1, 2, HALF, length)
    gp_own, gp_pair = call(
        combine_kernel,
        flags,
        (3,),
        [(d, few, lambda i, f: (i, 0, 0)) for d in (*d_0, *d_1, *d_2)]
        + [
            (array, one_part, lambda i, f: (jnp.maximum(i - 1, 0), 0, 0, 0))
            for array in (cross_kept, cross_came)
        ],
        [((3 * GROUP, length), BF, (GROUP, length), lambda i, f: (i, 0))] * 2,
        BRIEF,
        "combine",
    )
    gp_other = swap(gp_pair, core)
    opened = call(
        functools.partial(project_grad_kernel, at=[ring[0][3], by_y[0][3]]),
        flags,
        (3,),
        [(g, (GROUP, length), lambda i, f: (i, 0)) for g in (gp_own, gp_pair)]
        + [fixed(normed), fixed(normed_other)],
        [((D // 4, 3 * GROUP), BF, (D // 4, GROUP), lambda i, f: (0, i))] * 4,
        BRIEF,
        "project_grad",
    )
    gp_own, gp_other, opened = beside(first, gp_own, gp_other, opened)
    second = [Chain(order, 2, *opened[2 * i : 2 * i + 2]) for i, order in enumerate((ring, lanes[:1] + [cross] + lanes[1:]))]
    land(flags, first)
    send(first + second)
    land(flags, first + second)
    gp_own, gp_other = send(first + second, gp_own, gp_other)
    grad_input, sums = call(
        input_grad_kernel,
        flags,
        (3,),
        [
            (gp_own, (GROUP, length), lambda i, f: (i, 0)),
            (gp_other, (GROUP, length), lambda i, f: (i, 0)),
            (w_qkv, (D, GROUP), lambda i, f: (0, 2 * i + f[1])),
            (w_qkv, (D, GROUP), lambda i, f: (0, 2 * i + 1 - f[1])),
            fixed(x),
            emb,
            fixed(gains),
            fixed(grad_residual),
            fixed(dgain_mlp),
        ],
        [out_fixed(tokens, BF), out_fixed((passes + 2, D), F32)],
        BRIEF,
        "input_grad",
        [pltpu.VMEM((D, length), F32)],
    )
    grad_input, sums = beside(first + second, grad_input, sums)
    land(flags, first + second)
    while second[1].plan[0][0] == HALVE:
        send(first + second)
        land(flags, first + second)
    rider = jnp.pad(sums, ((0, 8 - passes - 2), (0, 3 * GROUP - D))).astype(BF)
    second[1].sent, second[1].riders = jnp.concatenate([second[1].sent, rider]), 8
    while not first[0].done():
        send(first + second)
        land(flags, first + second)
    send(second)
    pairs = [(c.sent, swap(c.sent, core)) for c in first]
    (pairs,) = beside(second, pairs)
    land(flags, second)
    third = [a for pair in pairs for a in pair]
    at_most = [
        (third[i], (GROUP, D), lambda j, f: (jnp.minimum(j % 4, 2), 0)) for i in (0, 1)
    ] + [(third[i], (D, GROUP), lambda j, f: (0, j % 4)) for i in (2, 3)]
    down_total, up_total, out_total = call(
        assemble_first_kernel,
        flags,
        (8,),
        at_most + [fixed(third[4]), fixed(third[5])],
        [
            ((4 * D, D), F32, (GROUP, D), lambda j, f: (j, 0)),
            ((D, 4 * D), F32, (D, GROUP), lambda j, f: (0, j)),
            ((D, D), F32, (GROUP, D), lambda j, f: (j // 4, 0)),
        ],
        BRIEF,
        "assemble_first",
    )
    while not second[0].done():
        send(second)
        down_total, up_total, out_total = beside(second, down_total, up_total, out_total)
        land(flags, second)
    lasts = [(c.sent, swap(c.sent, core)) for c in second]
    small = sum(a[D // 2 :, :D].astype(F32) for a in lasts[1])
    qkv_total = call(
        assemble_second_kernel,
        flags,
        (6,),
        [
            (a, (GROUP, GROUP), lambda j, f: (0, j // 2))
            for pair in lasts
            for a in pair
        ],
        [((D, 3 * D), F32, (D, GROUP), lambda j, f: (0, j))],
        BRIEF,
        "assemble_second",
    )[0]
    return (
        output[None],
        grad_input[None],
        small[:passes],
        small[passes],
        qkv_total,
        out_total,
        small[passes + 1],
        up_total,
        down_total,
    )


def solution(mesh):
    sizes = (mesh.shape["pass"], mesh.shape["dp"])
    tokens = P("pass", "dp", None)
    in_specs = (tokens, P("dp")) + (P(),) * 7 + (tokens,)
    out_specs = (tokens, tokens) + (P(),) * 7
    return jax.shard_map(
        functools.partial(on_device, sizes),
        mesh=mesh,
        in_specs=in_specs,
        out_specs=out_specs,
        check_vma=False,
    )
```

```python
import functools
import math

import jax
import jax.numpy as jnp
from jax import lax
from jax.experimental import pallas as pl
from jax.experimental.pallas import tpu as pltpu
from jax.sharding import PartitionSpec as P

D = 768
HEADS = 12
HEAD_DIM = 64
SHORT = 256
FF_TILE = 512
GROUP = D // 2
HALF = GROUP // 2
HALF_HEADS = HEADS // 4
EPS = 1e-05
SCALE = HEAD_DIM**-0.5
SCALE2 = SCALE * math.log2(math.e)
BF = jnp.bfloat16
F32 = jnp.float32
PIECES, FIRST_HEADS = (2, 1), (0, 2)
BRIEF = 0.2


def dot(a, b, ca, cb):
    return lax.dot_general(a, b, (((ca,), (cb,)), ((), ())), preferred_element_type=F32)


def cost(us):
    return pl.CostEstimate(flops=int(us * 1.1e9), bytes_accessed=1 << 20, transcendentals=0)


def call(kernel, flags, grid, ins, outs, us, name, scratch=(), temporaries=8):
    blocks = [(math.prod(block), array.dtype) for array, block, index in ins if index]
    blocks += [(math.prod(block), dtype) for _, dtype, block, index in outs if index]
    blocks += [(math.prod(buffer.shape) // 2, buffer.dtype) for buffer in scratch]
    limit = sum(2 * n * jnp.dtype(dtype).itemsize for n, dtype in blocks) + (temporaries << 20)
    return pl.pallas_call(
        kernel,
        grid_spec=pltpu.PrefetchScalarGridSpec(
            num_scalar_prefetch=1,
            grid=grid,
            in_specs=[spec(block, index) for _, block, index in ins],
            out_specs=[spec(block, index) for _, _, block, index in outs],
            scratch_shapes=list(scratch),
        ),
        out_shape=[jax.ShapeDtypeStruct(shape, dtype) for shape, dtype, _, _ in outs],
        cost_estimate=cost(us),
        compiler_params=pltpu.CompilerParams(vmem_limit_bytes=min(limit, 60 << 20)),
        name=name,
    )(flags, *[array for array, _, _ in ins])


def fixed(array):
    return (array, array.shape, lambda i, f: (0,) * array.ndim)


def out_fixed(shape, dtype):
    return (shape, dtype, shape, lambda i, f: (0,) * len(shape))


def held(array):
    return (array, array.shape, None)


def out_held(shape, dtype):
    return (shape, dtype, shape, None)


def spec(block, index):
    return pl.BlockSpec(block, index) if index else pl.BlockSpec(memory_space=pltpu.VMEM)


def one_sequence(f):
    return f[0] == 1


def hidden_of(f, x_ref, emb_ref):
    return x_ref[...].astype(F32) + emb_ref[pl.ds(f[3], 1), :]


def centered(values):
    center = values - jnp.mean(values, axis=-1, keepdims=True)
    return center, lax.rsqrt(jnp.mean(center * center, axis=-1, keepdims=True) + EPS)


def write_part(f, part, refs, value):
    out_ref, *cross_refs = refs
    out_ref[...] = value
    for ref, first, heads in zip(cross_refs, FIRST_HEADS, PIECES, strict=True):
        start, rows = first * HEAD_DIM, heads * HEAD_DIM

        @pl.when((f[2] == 1) & (part > 0))
        def _():
            ref[pl.ds(pl.multiple_of((part - 1) * rows, rows), rows), :] = value[start : start + rows]

        @pl.when((f[2] == 0) & (part == 0))
        def _():
            ref[:rows] = value[HALF + start : HALF + start + rows]
            ref[rows:] = jnp.zeros_like(ref[rows:])


def norm_project_kernel(f, x_ref, emb_ref, gain_ref, w_ref, normed_ref, *refs):
    part = pl.program_id(0)

    @pl.when(part == 0)
    def _():
        center, inv = centered(hidden_of(f, x_ref, emb_ref))
        normed_ref[...] = (center * inv * gain_ref[0:1]).T.astype(BF)

    write_part(f, part, refs, dot(w_ref[...], normed_ref[...], 0, 0).astype(BF))


def project_kernel(f, normed_ref, w_ref, *refs):
    write_part(f, pl.program_id(0), refs, dot(w_ref[...], normed_ref[...], 0, 0).astype(BF))


def projection_outs(length):
    outs = [((3 * GROUP, length), BF, (GROUP, length), lambda i, f: (i, 0))]
    for heads in PIECES:
        outs.append(out_fixed((2 * heads * HEAD_DIM, length), BF))
    return outs


def mask_tail(scores):
    n = scores.shape[0]
    key = lax.broadcasted_iota(jnp.int32, (SHORT, SHORT), 0)
    query = lax.broadcasted_iota(jnp.int32, (SHORT, SHORT), 1)
    diag = jnp.where(key <= query, scores[n - SHORT :], -1e30)
    return diag if n == SHORT else jnp.concatenate([scores[: n - SHORT], diag], 0)


def sweep(f, length, tile, variants):
    for condition, units in variants:
        for whole in (True, False):

            @pl.when(condition & (one_sequence(f) == whole))
            def _():
                for at in range(length // SHORT):
                    for unit in units:
                        tile(unit, at, 0 if whole else at)


def spans(at, first):
    return slice(at * SHORT, (at + 1) * SHORT), slice(first * SHORT, (at + 1) * SHORT)


def softmax_tile(q_refs, k_refs, v_refs, o_refs, lse_ref, unit, at, first):
    qp, keys = unit
    qs, ks = spans(at, first)
    q = q_refs[qp][:, qs]
    scores = [mask_tail(dot(k_refs[kp][:, ks], q, 0, 0) * SCALE2) for kp in keys]
    top = functools.reduce(jnp.maximum, [jnp.max(s, axis=0, keepdims=True) for s in scores])
    raw = [jnp.exp2(s - top) for s in scores]
    total = functools.reduce(jnp.add, [jnp.sum(p, axis=0, keepdims=True) for p in raw])
    out = functools.reduce(
        jnp.add, [dot(v_refs[kp][:, ks], p.astype(BF), 1, 0) for kp, p in zip(keys, raw)]
    )
    o_refs[qp][:, qs] = (out * (1.0 / total)).astype(o_refs[qp].dtype)
    lse_ref[0, qp : qp + 1, qs] = top + jnp.log2(total)


LOCAL_UNITS = (
    lambda f: (f[1] == 0, [(0, [0]), (1, [0, 1])]),
    lambda f: (f[1] == 1, [(1, [1]), (0, [0, 1])]),
)
CROSS_UNITS = [(0, [0, 1]), (1, [0, 1])]


def local_kernel(f, q0, q1, k0, k1, v0, v1, o0, o1, lse_ref):
    sweep(
        f,
        q0.shape[1],
        functools.partial(softmax_tile, (q0, q1), (k0, k1), (v0, v1), (o0, o1), lse_ref),
        [unit(f) for unit in LOCAL_UNITS],
    )


def cross_kernel(f, *refs):
    ins, (o_ref, lse_ref) = refs[:12], refs[12:]
    outs = (o_ref.at[0], o_ref.at[1])
    for early, at in ((1, 0), (0, 6)):
        q0, q1, k0, k1, v0, v1 = ins[at : at + 6]
        sweep(
            f,
            q0.shape[1],
            functools.partial(softmax_tile, (q0, q1), (k0, k1), (v0, v1), outs, lse_ref),
            [(f[2] == early, CROSS_UNITS)],
        )


def head(array, at):
    return (array, (HEAD_DIM, array.shape[-1]), lambda h, f: (at + h, 0))


def lse_spec(array):
    return (array, (1,) + array.shape[1:], lambda h, f: (h, 0, 0))


def lse_out(heads, length):
    return ((heads, 2, length), F32, (1, 2, length), lambda h, f: (h, 0, 0))


def cross_inputs(far, own, other, first, heads):
    high = HALF_HEADS + first
    return [
        head(far[0], 0),
        head(far[1], 0),
        head(own, 6 + high),
        head(other, 6 + high),
        head(own, 12 + high),
        head(other, 12 + high),
        head(own, first),
        head(other, first),
        head(far[0], 0),
        head(far[1], 0),
        head(far[0], heads),
        head(far[1], heads),
    ]


def merge_kernel(
    f, la0, la1, lsea, lb0, lb1, lseb, ca, lseca, cb, lsecb, ba, lseba, bb, lsebb,
    a0, a1, lse_out, high_ref, lse_high,
):
    def rows(h):
        return slice(h * HEAD_DIM, (h + 1) * HEAD_DIM)

    def put(h, i, value, lse):
        value = value.astype(BF)
        (a0, a1)[i][rows(h)] = value
        lse_out[h, i : i + 1] = lse
        if h >= HALF_HEADS:
            high_ref[i, rows(h - HALF_HEADS)] = value
            lse_high[h - HALF_HEADS, i : i + 1] = lse

    for h in range(2 * HALF_HEADS):
        local, lse_l, at = ((la0, la1), lsea, h) if h < 4 else ((lb0, lb1), lseb, h - 4)
        low, there = h < HALF_HEADS, h % HALF_HEADS
        if there < PIECES[0]:
            far, lse_c = (ca, lseca) if low else (ba, lseba)
        else:
            far, lse_c, there = (cb, lsecb, 0) if low else (bb, lsebb, 0)
        for i in (0, 1):
            near, lse_near = local[i][rows(at)], lse_l[at, i : i + 1]

            @pl.when(f[2] == 1)
            def _():
                put(h, i, near, lse_near)

            @pl.when(f[2] == 0)
            def _():
                lse_far = lse_c[there, i : i + 1]
                top = jnp.maximum(lse_near, lse_far)
                lse = top + jnp.log2(jnp.exp2(lse_near - top) + jnp.exp2(lse_far - top))
                value = near * jnp.exp2(lse_near - lse) + far[i, rows(there)].astype(F32) * jnp.exp2(
                    lse_far - lse
                )
                put(h, i, value, lse)


def gradient_tile(
    q_refs, k_refs, v_refs, g_refs, o_refs, lse_ref, dq_refs, dk_acc, dv_acc, unit, at, first
):
    qp, keys = unit
    qs, ks = spans(at, first)
    q, g = q_refs[qp][:, qs], g_refs[qp][:, qs]
    lse = lse_ref[0, qp : qp + 1, qs]
    delta = jnp.sum(g.astype(F32) * o_refs[qp][:, qs].astype(F32), axis=0, keepdims=True)
    dq = None
    for kp in keys:
        k, v = k_refs[kp][:, ks], v_refs[kp][:, ks]
        weights = jnp.exp2(mask_tail(dot(k, q, 0, 0) * SCALE2) - lse)
        ds = (weights * (dot(v, g, 0, 0) - delta)).astype(BF)
        term = dot(k, ds, 1, 0)
        dq = term if dq is None else dq + term
        dk_acc[kp, :, ks] += dot(q, ds, 1, 1)
        dv_acc[kp, :, ks] += dot(g, weights.astype(BF), 1, 1)
    dq_refs[qp][:, qs] = (dq * SCALE).astype(BF)


def local_back_kernel(
    f, q0, q1, k0, k1, v0, v1, g0, g1, o0, o1, lse_ref, d0, d1, dk_acc, dv_acc
):
    dk_acc[...] = jnp.zeros_like(dk_acc)
    dv_acc[...] = jnp.zeros_like(dv_acc)
    sweep(
        f,
        q0.shape[1],
        functools.partial(
            gradient_tile,
            (q0, q1),
            (k0, k1),
            (v0, v1),
            (g0, g1),
            (o0, o1),
            lse_ref,
            (d0.at[0], d1.at[0]),
            dk_acc,
            dv_acc,
        ),
        [unit(f) for unit in LOCAL_UNITS],
    )
    for i, ref in ((0, d0), (1, d1)):
        ref[1] = (dk_acc[i] * SCALE).astype(BF)
        ref[2] = dv_acc[i].astype(BF)


def cross_back_kernel(f, *refs):
    ins, more = refs[:12], refs[12:]
    (ga0, ga1, oa, lse_a, gb0, gb1, ob0, ob1, lse_b, kept_ref, sent_ref, dk_acc, dv_acc) = more
    dk_acc[...] = jnp.zeros_like(dk_acc)
    dv_acc[...] = jnp.zeros_like(dv_acc)
    for early, at, grads, outs, lse_ref, dq_ref in (
        (1, 0, (ga0, ga1), (oa.at[0], oa.at[1]), lse_a, sent_ref),
        (0, 6, (gb0, gb1), (ob0, ob1), lse_b, kept_ref),
    ):
        q0, q1, k0, k1, v0, v1 = ins[at : at + 6]
        sweep(
            f,
            q0.shape[1],
            functools.partial(
                gradient_tile,
                (q0, q1),
                (k0, k1),
                (v0, v1),
                grads,
                outs,
                lse_ref,
                (dq_ref.at[0, 0], dq_ref.at[0, 1]),
                dk_acc,
                dv_acc,
            ),
            [(f[2] == early, CROSS_UNITS)],
        )
    for early, dkv_ref, dq_ref in ((1, kept_ref, sent_ref), (0, sent_ref, kept_ref)):

        @pl.when(f[2] == early)
        def _():
            for i in (0, 1):
                dkv_ref[0, i] = (dk_acc[i] * SCALE).astype(BF)
                dkv_ref[1, i] = dv_acc[i].astype(BF)
            dq_ref[1] = jnp.zeros_like(dq_ref[1])


def gelu_pair(u):
    k = math.sqrt(2 / math.pi)
    square = u * u
    t = jnp.tanh(k * u * (1.0 + 0.044715 * square))
    half = 0.5 + 0.5 * t
    slope = half + 0.5 * u * (1.0 - t * t) * (k * (1.0 + 3 * 0.044715 * square))
    return u * half, slope


def chunks(length):
    return [slice(at, at + SHORT) for at in range(0, length, SHORT)]


def ff_tile(n_ref, cot_ref, wu_ref, wd_ref, y_ref, c_ref, act_ref, gup_ref):
    for at in chunks(n_ref.shape[0]):
        act, slope = gelu_pair(dot(n_ref[at], wu_ref[...], 1, 0))
        act = act.astype(BF)
        grad_up = (dot(cot_ref[at], wd_ref[...], 1, 1) * slope).astype(BF)
        act_ref[at], gup_ref[at] = act, grad_up
        y_ref[at] += dot(act, wd_ref[...], 1, 0)
        c_ref[at] += dot(grad_up, wu_ref[...], 1, 1)


def feed_kernel(
    f, x_ref, emb_ref, a_ref, b_ref, wa_ref, wb_ref, gain_ref, cot_ref, wu_ref, wd_ref,
    dds_ref, dus_ref, ddo_ref, duo_ref, out_ref, gres_ref, ga_ref, gb_ref, gah_ref, gbh_ref, dgain_ref, dwa_ref, dwb_ref,
    res_ref, n_ref, nt_ref, y_ref, c_ref, act_ref, gup_ref,
):
    step, steps = pl.program_id(0), pl.num_programs(0)

    @pl.when(step == 0)
    def _():
        for at in chunks(n_ref.shape[0]):
            residual = (
                x_ref[at].astype(F32)
                + emb_ref[pl.ds(f[3], 1), :]
                + dot(a_ref[:, at], wa_ref[...], 0, 0)
                + dot(b_ref[:, at], wb_ref[...], 0, 0)
            )
            res_ref[at] = residual
            center, inv = centered(residual)
            normed2 = center * inv * gain_ref[1:2]
            n_ref[at] = normed2.astype(BF)
            nt_ref[:, at] = normed2.T.astype(BF)
            y_ref[at] = residual
            c_ref[at] = jnp.zeros_like(residual)

    ff_tile(n_ref, cot_ref, wu_ref, wd_ref, y_ref, c_ref, act_ref, gup_ref)
    down = dot(act_ref[...], cot_ref[...], 0, 0).astype(BF)
    up = dot(nt_ref[...], gup_ref[...], 1, 0).astype(BF)

    @pl.when(step < steps // 2)
    def _():
        dds_ref[...], dus_ref[...] = down, up

    @pl.when(step >= steps // 2)
    def _():
        ddo_ref[...], duo_ref[...] = down, up

    @pl.when(step == steps - 1)
    def _():
        dgain = None
        grads = []
        for at in chunks(n_ref.shape[0]):
            out_ref[at] = y_ref[at].astype(BF)
            center, inv = centered(res_ref[at])
            n2 = center * inv
            c = c_ref[at]
            part = jnp.sum(c * n2, axis=0, keepdims=True)
            dgain = part if dgain is None else dgain + part
            e = c * gain_ref[1:2]
            grad = cot_ref[at].astype(F32) + inv * (
                e
                - jnp.mean(e, axis=-1, keepdims=True)
                - n2 * jnp.mean(e * n2, axis=-1, keepdims=True)
            )
            gres_ref[at] = grad
            grad = grad.astype(BF)
            grads.append(grad)
            mine = dot(wa_ref[...], grad, 1, 1).astype(BF)
            theirs = dot(wb_ref[...], grad, 1, 1).astype(BF)
            ga_ref[:, at], gb_ref[:, at] = mine, theirs
            gah_ref[:, at], gbh_ref[:, at] = mine[HALF:], theirs[HALF:]
        dgain_ref[...] = dgain
        grad = jnp.concatenate(grads, 0)
        dwa_ref[...] = dot(a_ref[...], grad, 1, 0).astype(BF)
        dwb_ref[...] = dot(b_ref[...], grad, 1, 0).astype(BF)


def combine_kernel(f, da0, da1, db0, db1, dc0, dc1, kept_ref, came_ref, g0, g1):
    part = pl.program_id(0)
    late, early = f[2] == 0, f[2] == 1

    def put(low, high):
        for i, (refs, g) in enumerate((((da0, db0, dc0), g0), ((da1, db1, dc1), g1))):
            local = jnp.concatenate([d[0] for d in refs], 0)
            if low is None:
                g[...] = local
            else:
                more = jnp.concatenate([low[0, i], high[0, i]], 0)
                g[...] = (local.astype(F32) + more.astype(F32)).astype(BF)

    @pl.when(late & (part == 0))
    def _():
        put(kept_ref, came_ref)

    @pl.when(early & (part > 0))
    def _():
        put(came_ref, kept_ref)

    @pl.when((late & (part > 0)) | (early & (part == 0)))
    def _():
        put(None, None)


def project_grad_kernel(f, g0, g1, n0_ref, n1_ref, s0_ref, k0_ref, s1_ref, k1_ref, *, at):
    value = dot(n0_ref[...], g0[...], 1, 1) + dot(n1_ref[...], g1[...], 1, 1)
    for i, (sent_ref, kept_ref) in enumerate(((s0_ref, k0_ref), (s1_ref, k1_ref))):
        sent, kept = pick(f[at[i]], value[i * (D // 2) : (i + 1) * (D // 2)])
        sent_ref[...] = sent.astype(BF)
        kept_ref[...] = kept.astype(BF)


def input_grad_kernel(
    f, g_ref, h_ref, wg_ref, wh_ref, x_ref, emb_ref, gain_ref, gres_ref, dgain_ref, gin_ref, sums_ref, acc
):
    part = pl.program_id(0)
    value = dot(wg_ref[...], g_ref[...], 1, 0) + dot(wh_ref[...], h_ref[...], 1, 0)

    @pl.when(part == 0)
    def _():
        acc[...] = value

    @pl.when(part > 0)
    def _():
        acc[...] += value

    @pl.when(part == pl.num_programs(0) - 1)
    def _():
        center, inv = centered(hidden_of(f, x_ref, emb_ref))
        n1 = center * inv
        grad = acc[...].T
        e = grad * gain_ref[0:1]
        total = gres_ref[...] + inv * (
            e - jnp.mean(e, axis=-1, keepdims=True) - n1 * jnp.mean(e * n1, axis=-1, keepdims=True)
        )
        gin_ref[...] = total.astype(BF)
        sums = jnp.sum(total, axis=0, keepdims=True)
        passes = sums_ref.shape[0] - 2
        for i in range(passes):
            sums_ref[i : i + 1] = jnp.where(f[3] == i, sums, 0.0)
        sums_ref[passes : passes + 1] = jnp.sum(grad * n1, axis=0, keepdims=True)
        sums_ref[passes + 1 :] = dgain_ref[...]


def assemble_first_kernel(f, d_own, d_oth, u_own, u_oth, m_own, m_oth, down_ref, up_ref, out_ref):
    step = pl.program_id(0)
    half, at = step // 4, step % 4
    for mine, d, u, m in ((True, d_own, u_own, m_own), (False, d_oth, u_oth, m_oth)):
        here = (half == f[1]) == mine

        @pl.when(here)
        def _():
            up_ref[...] = u[...].astype(F32)

        @pl.when(here & (at < 3))
        def _():
            down_ref[...] = d[...].astype(F32)

        @pl.when(here & (at == 3))
        def _():
            down_ref[...] = m[:GROUP].astype(F32)
            out_ref[...] = m[GROUP:].astype(F32)


def assemble_second_kernel(f, a_own, a_oth, b_own, b_oth, out_ref):
    for mine, a, b in ((True, a_own, b_own), (False, a_oth, b_oth)):

        @pl.when((pl.program_id(0) % 2 == f[1]) == mine)
        def _():
            out_ref[:GROUP] = a[...].astype(F32)
            out_ref[GROUP:] = b[...].astype(F32)


def swap(array, step):
    axis, mask, size, _ = step
    return lax.ppermute(array, axis, [(i, i ^ mask) for i in range(size)])


def tie(*groups):
    leaves, tree = jax.tree.flatten(groups)
    return jax.tree.unflatten(tree, lax.optimization_barrier(leaves))


def pick(here, total):
    half = total.shape[0] // 2
    low, high = total[:half], total[half:]
    return jnp.where(here == 0, high, low), jnp.where(here == 0, low, high)


def joined(here, own, other):
    return jnp.where(
        here == 0, jnp.concatenate([own, other], 0), jnp.concatenate([other, own], 0)
    )


def round_work(here, own, came, mode, riders):
    if mode == "join":
        cut = own.shape[0] - riders
        value = joined(here, own[:cut], came[:cut])
        return (jnp.concatenate([value, own[cut:] + came[cut:]], 0) if riders else value,)
    total = own + came
    return (total,) if mode == "sum" else pick(here, total)


def round_kernel(f, *refs, modes, at, riders):
    refs = list(refs)
    ins, outs = refs[: 2 * len(modes)], refs[2 * len(modes) :]
    for i, mode in enumerate(modes):
        own, came = ins[2 * i][...].astype(F32), ins[2 * i + 1][...].astype(F32)
        for value in round_work(f[at[i]], own, came, mode, riders[i]):
            outs.pop(0)[...] = value.astype(BF)


def whole_call(kernel, flags, ins, outs, name):
    vmem = pl.BlockSpec(memory_space=pltpu.VMEM)
    size = sum(math.prod(shape) for shape in [a.shape for a in ins] + outs)
    return pl.pallas_call(
        kernel,
        in_specs=[pl.BlockSpec(memory_space=pltpu.SMEM)] + [vmem] * len(ins),
        out_specs=[vmem] * len(outs),
        out_shape=[jax.ShapeDtypeStruct(shape, BF) for shape in outs],
        cost_estimate=cost(BRIEF),
        compiler_params=pltpu.CompilerParams(vmem_limit_bytes=2 * size + (8 << 20)),
        name=name,
    )(flags, *ins)


HALVE, FULL, JOIN = 0, 1, 2


class Chain:
    def __init__(self, steps, whole_steps, sent, kept):
        cut = len(steps) - whole_steps
        self.plan = (
            [(HALVE, step) for step in steps[:cut]]
            + [(FULL, step) for step in steps[cut:]]
            + [(JOIN, step) for step in reversed(steps[:cut])]
        )
        self.sent, self.kept, self.came, self.riders = sent, kept, None, 0

    def done(self):
        return not self.plan


def land(flags, chains):
    chains = [c for c in chains if c.came is not None]
    modes, at, ins, outs, riders = [], [], [], [], [c.riders for c in chains]
    for c in chains:
        what, step = c.plan.pop(0)
        own = c.kept if what == HALVE else c.sent
        rows, columns = own.shape
        if what == JOIN:
            modes.append("join")
            at.append(step[3])
            outs += [(2 * rows - c.riders, columns)]
        elif c.plan and c.plan[0][0] == HALVE:
            modes.append("split")
            at.append(c.plan[0][1][3])
            outs += [(rows // 2, columns)] * 2
        else:
            modes.append("sum")
            at.append(0)
            outs += [(rows, columns)]
        ins += [own, c.came]
    if all(shape[0] % 8 == 0 for shape in outs):
        kernel = functools.partial(round_kernel, modes=modes, at=at, riders=riders)
        results = list(whole_call(kernel, flags, ins, outs, "round"))
    else:
        results = []
        for i, mode in enumerate(modes):
            own, came = (a.astype(F32) for a in ins[2 * i : 2 * i + 2])
            results += [
                v.astype(BF) for v in round_work(flags[at[i]], own, came, mode, riders[i])
            ]
    for c, mode in zip(chains, modes, strict=True):
        c.came, c.sent = None, results.pop(0)
        if mode == "split":
            c.kept = results.pop(0)


def open_kernel(f, dd, ddr, du, dur, dw, dwr, *outs, at):
    def add(left, right):
        return left[...].astype(F32) + right[...].astype(F32)

    down, up, out = add(dd, ddr), add(du, dur), add(dw, dwr)
    cut = down.shape[0] - GROUP
    for i, value in enumerate((down[:cut], up, jnp.concatenate([down[cut:], out], 0))):
        sent, kept = pick(f[at[i]], value)
        outs[2 * i][...] = sent.astype(BF)
        outs[2 * i + 1][...] = kept.astype(BF)


def beside(chains, *more):
    chains = [c for c in chains if c.came is not None]
    arrays, more = tie([c.came for c in chains], more)
    for c, array in zip(chains, arrays, strict=True):
        c.came = array
    return more


def send(chains, *more):
    chains = [c for c in chains if not c.done()]
    loads, more = tie([c.sent for c in chains], more)
    for c, load in zip(chains, loads, strict=True):
        c.sent, c.came = load, swap(load, c.plan[0][1])
    return more


def on_device(
    sizes, block_input, segments, pass_emb, gain_attn, w_qkv, w_out, gain_mlp, w_up, w_down, cotangent
):
    passes, n_dp = sizes
    core = ("pass", 1, passes, 1)
    cross = ("pass", 2, passes, 4)
    lanes = [("dp", 1 << i, n_dp, 5 + i) for i in range(n_dp.bit_length() - 1)]
    ring = [cross] + lanes
    by_y = lanes[:1] + [cross] + lanes[:0:-1]
    orders = [ring, by_y, ring[2:] + ring[:2]]

    pass_here = lax.axis_index("pass")
    core_here = pass_here & 1
    length = segments.shape[0]
    place = [core_here, (pass_here < 2).astype(jnp.int32), pass_here] + [
        (lax.axis_index(axis) >> (mask.bit_length() - 1)) & 1 for axis, mask, _, _ in ring
    ]
    start_flags = jnp.stack([jnp.zeros_like(core_here)] + place)

    x, cot = block_input[0], cotangent[0]
    emb = fixed(pass_emb)
    gains = jnp.stack([gain_attn, gain_mlp])

    normed, theirs, *theirs_cross = call(
        norm_project_kernel,
        start_flags,
        (3,),
        [fixed(x), emb, fixed(gains), (w_qkv, (D, GROUP), lambda i, f: (0, 2 * i + 1 - f[1]))],
        [out_fixed((D, length), BF)] + projection_outs(length),
        BRIEF,
        "norm_project",
    )
    other = swap(theirs, core)
    own, *own_cross = call(
        project_kernel,
        start_flags,
        (3,),
        [fixed(normed), (w_qkv, (D, GROUP), lambda i, f: (0, 2 * i + f[1]))],
        projection_outs(length),
        BRIEF,
        "project_own",
    )

    across = ("pass", 3, passes, 0)

    def exchange(piece):
        return swap(own_cross[piece], cross), swap(theirs_cross[piece], across)

    def attend_local(first, heads):
        return call(
            local_kernel,
            flags,
            (heads,),
            [head(a, at + first) for at in (0, 6, 12) for a in (own, other)],
            [((heads * HEAD_DIM, length), F32, (HEAD_DIM, length), lambda h, f: (h, 0))] * 2
            + [lse_out(heads, length)],
            BRIEF,
            "attend_local",
        )

    def attend_cross(piece, far):
        heads = PIECES[piece]
        return call(
            cross_kernel,
            flags,
            (heads,),
            cross_inputs(far, own, other, FIRST_HEADS[piece], heads),
            [
                ((2, heads * HEAD_DIM, length), BF, (2, HEAD_DIM, length), lambda h, f: (0, h, 0)),
                lse_out(heads, length),
            ],
            BRIEF,
            "attend_cross",
        )

    same, start_flags = tie((segments[0] == segments[length - 1]).astype(jnp.int32), start_flags)
    flags = start_flags.at[0].set(same)
    far_0 = exchange(0)
    local_0 = attend_local(0, 4)
    far_0, local_0, own_cross, theirs_cross = tie(far_0, local_0, own_cross, theirs_cross)
    far_1 = exchange(1)
    normed_other = swap(normed, core)
    cross_0 = attend_cross(0, far_0)
    far_1, cross_0 = tie(far_1, cross_0)
    o_back_0 = swap(cross_0[0], cross)
    cross_1 = attend_cross(1, far_1)
    cross_1, own, other = tie(cross_1, own, other)
    o_back_1, lse_back_1, lse_back_0 = (
        swap(a, cross) for a in (cross_1[0], cross_1[1], cross_0[1])
    )
    local_1 = attend_local(4, 2)
    o_back_0, o_back_1, lse_back_0, lse_back_1, local_1 = tie(
        o_back_0, o_back_1, lse_back_0, lse_back_1, local_1
    )
    half_rows = (HALF, length)
    att_own, att_pair, lse, att_high, lse_high = call(
        merge_kernel,
        flags,
        (1,),
        [
            fixed(a)
            for a in (*local_0, *local_1, *cross_0, *cross_1, o_back_0, lse_back_0, o_back_1, lse_back_1)
        ],
        [out_fixed((GROUP, length), BF)] * 2
        + [
            out_fixed((HEADS // 2, 2, length), F32),
            out_fixed((2, HALF, length), BF),
            out_fixed((HALF_HEADS, 2, length), F32),
        ],
        BRIEF,
        "merge",
    )
    far = [
        jnp.concatenate([a[: 2 * HEAD_DIM], b[:HEAD_DIM], a[2 * HEAD_DIM :], b[HEAD_DIM:]])
        for a, b in zip(far_0, far_1, strict=True)
    ]
    cross_in = cross_inputs(far, own, other, 0, HALF_HEADS)
    att_other = swap(att_pair, core)
    att_early, lse_early = swap(att_high, cross), swap(lse_high, cross)
    att_own, att_other, normed_other = tie(att_own, att_other, normed_other)

    w_half = [(w_out, (GROUP, D), lambda i, f: (f[1], 0)), (w_out, (GROUP, D), lambda i, f: (1 - f[1], 0))]
    ff_half = w_up.shape[1] // 2
    steps = ff_half // FF_TILE

    def tile_at(i, f):
        return jnp.where(i < steps, 1 - f[1], f[1]) * steps + i % steps

    sent_at, own_at = lambda i: jnp.minimum(i, steps - 1), lambda i: jnp.maximum(i - steps, 0)
    tokens = (length, D)
    (
        down_sent, up_sent, down_own, up_own, output, grad_residual, g_own, g_theirs, g_own_high, g_theirs_high,
        dgain_mlp, out_own, out_sent,
    ) = call(
        feed_kernel,
        flags,
        (2 * steps,),
        [held(x), emb, held(att_own), held(att_other)]
        + w_half
        + [held(gains), held(cot)]
        + [
            (w_up, (D, FF_TILE), lambda i, f: (0, tile_at(i, f))),
            (w_down, (FF_TILE, D), lambda i, f: (tile_at(i, f), 0)),
        ],
        [
            ((ff_half, D), BF, (FF_TILE, D), lambda i, f: (sent_at(i), 0)),
            ((D, ff_half), BF, (D, FF_TILE), lambda i, f: (0, sent_at(i))),
            ((ff_half, D), BF, (FF_TILE, D), lambda i, f: (own_at(i), 0)),
            ((D, ff_half), BF, (D, FF_TILE), lambda i, f: (0, own_at(i))),
            (tokens, BF, tokens, lambda i, f: (0, 0)),
            (tokens, F32, tokens, lambda i, f: (0, 0)),
            out_held((GROUP, length), BF),
            out_held((GROUP, length), BF),
            out_held(half_rows, BF),
            out_held(half_rows, BF),
            out_held((1, D), F32),
            out_held((GROUP, D), BF),
            out_held((GROUP, D), BF),
        ],
        BRIEF,
        "feed",
        [pltpu.VMEM(tokens, F32), pltpu.VMEM(tokens, BF), pltpu.VMEM((D, length), BF)]
        + [pltpu.VMEM(tokens, F32)] * 2
        + [pltpu.VMEM((length, FF_TILE), BF)] * 2,
        6,
    )
    (
        down_sent, up_sent, down_own, up_own, output, grad_residual, g_own, g_theirs, g_own_high, g_theirs_high,
        dgain_mlp, out_own, out_sent, att_early, lse_early,
    ) = tie(
        down_sent, up_sent, down_own, up_own, output, grad_residual, g_own, g_theirs, g_own_high, g_theirs_high,
        dgain_mlp, out_own, out_sent, att_early, lse_early,
    )
    g_other = swap(g_theirs, core)
    early_g = (swap(g_own_high, cross), swap(g_theirs_high, across))
    g_other, down_sent, up_sent, out_sent = tie(g_other, down_sent, up_sent, out_sent)
    out_recv, down_recv, up_recv = (swap(a, core) for a in (out_sent, down_sent, up_sent))

    accumulators = [pltpu.VMEM((2, HEAD_DIM, length), F32)] * 2

    def local_back(at, heads, g0, g1):
        return call(
            local_back_kernel,
            flags,
            (heads,),
            [head(a, base + at) for base in (0, 6, 12) for a in (own, other)]
            + [head(a, at) for a in (g0, g1, att_own, att_pair)]
            + [(lse, (1, 2, length), lambda h, f: (at + h, 0, 0))],
            [((3, heads * HEAD_DIM, length), BF, (3, HEAD_DIM, length), lambda h, f: (0, h, 0))] * 2,
            BRIEF,
            "attend_back_local",
            accumulators,
        )

    d_0 = local_back(0, 2, g_own, g_other)
    d_0, early_g_own, out_own = tie(d_0, early_g[0], out_own)
    early_g = (early_g_own, early_g[1])
    opened = whole_call(
        functools.partial(open_kernel, at=[steps_[0][3] for steps_ in orders]),
        flags,
        [down_own, down_recv, up_own, up_recv, out_own, out_recv],
        [shape for shape in (((ff_half - GROUP) // 2, D), (GROUP, ff_half), (GROUP, D)) for _ in (0, 1)],
        "open",
    )
    first = [Chain(orders[i], 1, *opened[2 * i : 2 * i + 2]) for i in range(3)]
    (early_g,) = send(first, early_g)
    cross_kept, cross_sent = call(
        cross_back_kernel,
        flags,
        (HALF_HEADS,),
        cross_in
        + [
            head(early_g[0], 0),
            head(early_g[1], 0),
            (att_early, (2, HEAD_DIM, length), lambda h, f: (0, h, 0)),
            lse_spec(lse_early),
            head(g_own, 0),
            head(g_other, 0),
            head(att_own, 0),
            head(att_pair, 0),
            lse_spec(lse),
        ],
        [((2, 2, HALF, length), BF, (2, 2, HEAD_DIM, length), lambda h, f: (0, 0, h, 0))] * 2,
        BRIEF,
        "attend_back_cross",
        accumulators,
    )
    cross_kept, cross_sent, g_own, g_other = tie(cross_kept, cross_sent, g_own, g_other)
    cross_came = swap(cross_sent, cross)
    d_1 = local_back(2, 2, g_own, g_other)
    (d_1,) = beside(first, d_1)
    land(flags, first)
    g_own, g_other = send(first, g_own, g_other)
    d_2 = local_back(4, 2, g_own, g_other)
    d_2, cross_came = beside(first, d_2, cross_came)
    land(flags, first)
    d_2, cross_came = send(first, d_2, cross_came)
    few = (1, 2 * HEAD_DIM, length)
    one_part = (1, 2, HALF, length)
    gp_own, gp_pair = call(
        combine_kernel,
        flags,
        (3,),
        [(d, few, lambda i, f: (i, 0, 0)) for d in (*d_0, *d_1, *d_2)]
        + [
            (array, one_part, lambda i, f: (jnp.maximum(i - 1, 0), 0, 0, 0))
            for array in (cross_kept, cross_came)
        ],
        [((3 * GROUP, length), BF, (GROUP, length), lambda i, f: (i, 0))] * 2,
        BRIEF,
        "combine",
    )
    gp_other = swap(gp_pair, core)
    opened = call(
        functools.partial(project_grad_kernel, at=[ring[0][3], by_y[0][3]]),
        flags,
        (3,),
        [(g, (GROUP, length), lambda i, f: (i, 0)) for g in (gp_own, gp_pair)]
        + [fixed(normed), fixed(normed_other)],
        [((D // 4, 3 * GROUP), BF, (D // 4, GROUP), lambda i, f: (0, i))] * 4,
        BRIEF,
        "project_grad",
    )
    gp_own, gp_other, opened = beside(first, gp_own, gp_other, opened)
    second = [Chain(order, 2, *opened[2 * i : 2 * i + 2]) for i, order in enumerate((ring, lanes[:1] + [cross] + lanes[1:]))]
    land(flags, first)
    gp_own, gp_other = send(first + second, gp_own, gp_other)
    grad_input, sums = call(
        input_grad_kernel,
        flags,
        (3,),
        [
            (gp_own, (GROUP, length), lambda i, f: (i, 0)),
            (gp_other, (GROUP, length), lambda i, f: (i, 0)),
            (w_qkv, (D, GROUP), lambda i, f: (0, 2 * i + f[1])),
            (w_qkv, (D, GROUP), lambda i, f: (0, 2 * i + 1 - f[1])),
            fixed(x),
            emb,
            fixed(gains),
            fixed(grad_residual),
            fixed(dgain_mlp),
        ],
        [out_fixed(tokens, BF), out_fixed((passes + 2, D), F32)],
        BRIEF,
        "input_grad",
        [pltpu.VMEM((D, length), F32)],
    )
    grad_input, sums = beside(first + second, grad_input, sums)
    land(flags, first + second)
    while second[1].plan[0][0] == HALVE:
        send(first + second)
        land(flags, first + second)
    rider = jnp.pad(sums, ((0, 8 - passes - 2), (0, 3 * GROUP - D))).astype(BF)
    second[1].sent, second[1].riders = jnp.concatenate([second[1].sent, rider]), 8
    while not first[0].done():
        send(first + second)
        land(flags, first + second)
    send(second)
    pairs = [(c.sent, swap(c.sent, core)) for c in first]
    (pairs,) = beside(second, pairs)
    land(flags, second)
    third = [a for pair in pairs for a in pair]
    at_most = [
        (third[i], (GROUP, D), lambda j, f: (jnp.minimum(j % 4, 2), 0)) for i in (0, 1)
    ] + [(third[i], (D, GROUP), lambda j, f: (0, j % 4)) for i in (2, 3)]
    down_total, up_total, out_total = call(
        assemble_first_kernel,
        flags,
        (8,),
        at_most + [fixed(third[4]), fixed(third[5])],
        [
            ((4 * D, D), F32, (GROUP, D), lambda j, f: (j, 0)),
            ((D, 4 * D), F32, (D, GROUP), lambda j, f: (0, j)),
            ((D, D), F32, (GROUP, D), lambda j, f: (j // 4, 0)),
        ],
        BRIEF,
        "assemble_first",
    )
    while not second[0].done():
        send(second)
        down_total, up_total, out_total = beside(second, down_total, up_total, out_total)
        land(flags, second)
    lasts = [(c.sent, swap(c.sent, core)) for c in second]
    small = sum(a[D // 2 :, :D].astype(F32) for a in lasts[1])
    qkv_total = call(
        assemble_second_kernel,
        flags,
        (6,),
        [
            (a, (GROUP, GROUP), lambda j, f: (0, j // 2))
            for pair in lasts
            for a in pair
        ],
        [((D, 3 * D), F32, (D, GROUP), lambda j, f: (0, j))],
        BRIEF,
        "assemble_second",
    )[0]
    return (
        output[None],
        grad_input[None],
        small[:passes],
        small[passes],
        qkv_total,
        out_total,
        small[passes + 1],
        up_total,
        down_total,
    )


def solution(mesh):
    sizes = (mesh.shape["pass"], mesh.shape["dp"])
    tokens = P("pass", "dp", None)
    in_specs = (tokens, P("dp")) + (P(),) * 7 + (tokens,)
    out_specs = (tokens, tokens) + (P(),) * 7
    return jax.shard_map(
        functools.partial(on_device, sizes),
        mesh=mesh,
        in_specs=in_specs,
        out_specs=out_specs,
        check_vma=False,
    )
```

```python
import functools
import math

import jax
import jax.numpy as jnp
from jax import lax
from jax.experimental import pallas as pl
from jax.experimental.pallas import tpu as pltpu
from jax.sharding import PartitionSpec as P

D = 768
HEADS = 12
HEAD_DIM = 64
SHORT = 256
FF_TILE = 512
GROUP = D // 2
HALF = GROUP // 2
HALF_HEADS = HEADS // 4
EPS = 1e-05
SCALE = HEAD_DIM**-0.5
SCALE2 = SCALE * math.log2(math.e)
BF = jnp.bfloat16
F32 = jnp.float32
PIECES, FIRST_HEADS = (2, 1), (0, 2)
BRIEF = 0.2


def dot(a, b, ca, cb):
    return lax.dot_general(a, b, (((ca,), (cb,)), ((), ())), preferred_element_type=F32)


def cost(us):
    return pl.CostEstimate(flops=int(us * 1.1e9), bytes_accessed=1 << 20, transcendentals=0)


def call(kernel, flags, grid, ins, outs, us, name, scratch=(), temporaries=8):
    blocks = [(math.prod(block), array.dtype) for array, block, index in ins if index]
    blocks += [(math.prod(block), dtype) for _, dtype, block, index in outs if index]
    blocks += [(math.prod(buffer.shape) // 2, buffer.dtype) for buffer in scratch]
    limit = sum(2 * n * jnp.dtype(dtype).itemsize for n, dtype in blocks) + (temporaries << 20)
    return pl.pallas_call(
        kernel,
        grid_spec=pltpu.PrefetchScalarGridSpec(
            num_scalar_prefetch=1,
            grid=grid,
            in_specs=[spec(block, index) for _, block, index in ins],
            out_specs=[spec(block, index) for _, _, block, index in outs],
            scratch_shapes=list(scratch),
        ),
        out_shape=[jax.ShapeDtypeStruct(shape, dtype) for shape, dtype, _, _ in outs],
        cost_estimate=cost(us),
        compiler_params=pltpu.CompilerParams(vmem_limit_bytes=min(limit, 60 << 20)),
        name=name,
    )(flags, *[array for array, _, _ in ins])


def fixed(array):
    return (array, array.shape, lambda i, f: (0,) * array.ndim)


def out_fixed(shape, dtype):
    return (shape, dtype, shape, lambda i, f: (0,) * len(shape))


def held(array):
    return (array, array.shape, None)


def out_held(shape, dtype):
    return (shape, dtype, shape, None)


def spec(block, index):
    return pl.BlockSpec(block, index) if index else pl.BlockSpec(memory_space=pltpu.VMEM)


def one_sequence(f):
    return f[0] == 1


def hidden_of(f, x_ref, emb_ref):
    return x_ref[...].astype(F32) + emb_ref[pl.ds(f[3], 1), :]


def centered(values):
    center = values - jnp.mean(values, axis=-1, keepdims=True)
    return center, lax.rsqrt(jnp.mean(center * center, axis=-1, keepdims=True) + EPS)


def write_part(f, part, refs, value):
    out_ref, *cross_refs = refs
    out_ref[...] = value
    for ref, first, heads in zip(cross_refs, FIRST_HEADS, PIECES, strict=True):
        start, rows = first * HEAD_DIM, heads * HEAD_DIM

        @pl.when((f[2] == 1) & (part > 0))
        def _():
            ref[pl.ds(pl.multiple_of((part - 1) * rows, rows), rows), :] = value[start : start + rows]

        @pl.when((f[2] == 0) & (part == 0))
        def _():
            ref[:rows] = value[HALF + start : HALF + start + rows]
            ref[rows:] = jnp.zeros_like(ref[rows:])


def norm_project_kernel(f, x_ref, emb_ref, gain_ref, w_ref, normed_ref, *refs):
    part = pl.program_id(0)

    @pl.when(part == 0)
    def _():
        center, inv = centered(hidden_of(f, x_ref, emb_ref))
        normed_ref[...] = (center * inv * gain_ref[0:1]).T.astype(BF)

    write_part(f, part, refs, dot(w_ref[...], normed_ref[...], 0, 0).astype(BF))


def project_kernel(f, normed_ref, w_ref, *refs):
    write_part(f, pl.program_id(0), refs, dot(w_ref[...], normed_ref[...], 0, 0).astype(BF))


def projection_outs(length):
    outs = [((3 * GROUP, length), BF, (GROUP, length), lambda i, f: (i, 0))]
    for heads in PIECES:
        outs.append(out_fixed((2 * heads * HEAD_DIM, length), BF))
    return outs


def mask_tail(scores):
    n = scores.shape[0]
    key = lax.broadcasted_iota(jnp.int32, (SHORT, SHORT), 0)
    query = lax.broadcasted_iota(jnp.int32, (SHORT, SHORT), 1)
    diag = jnp.where(key <= query, scores[n - SHORT :], -1e30)
    return diag if n == SHORT else jnp.concatenate([scores[: n - SHORT], diag], 0)


def sweep(f, length, tile, variants):
    for condition, units in variants:
        for whole in (True, False):

            @pl.when(condition & (one_sequence(f) == whole))
            def _():
                for at in range(length // SHORT):
                    for unit in units:
                        tile(unit, at, 0 if whole else at)


def spans(at, first):
    return slice(at * SHORT, (at + 1) * SHORT), slice(first * SHORT, (at + 1) * SHORT)


def softmax_tile(q_refs, k_refs, v_refs, o_refs, lse_ref, unit, at, first):
    qp, keys = unit
    qs, ks = spans(at, first)
    q = q_refs[qp][:, qs]
    scores = [mask_tail(dot(k_refs[kp][:, ks], q, 0, 0) * SCALE2) for kp in keys]
    top = functools.reduce(jnp.maximum, [jnp.max(s, axis=0, keepdims=True) for s in scores])
    raw = [jnp.exp2(s - top) for s in scores]
    total = functools.reduce(jnp.add, [jnp.sum(p, axis=0, keepdims=True) for p in raw])
    out = functools.reduce(
        jnp.add, [dot(v_refs[kp][:, ks], p.astype(BF), 1, 0) for kp, p in zip(keys, raw)]
    )
    o_refs[qp][:, qs] = (out * (1.0 / total)).astype(o_refs[qp].dtype)
    lse_ref[0, qp : qp + 1, qs] = top + jnp.log2(total)


LOCAL_UNITS = (
    lambda f: (f[1] == 0, [(0, [0]), (1, [0, 1])]),
    lambda f: (f[1] == 1, [(1, [1]), (0, [0, 1])]),
)
CROSS_UNITS = [(0, [0, 1]), (1, [0, 1])]


def local_kernel(f, q0, q1, k0, k1, v0, v1, o0, o1, lse_ref):
    sweep(
        f,
        q0.shape[1],
        functools.partial(softmax_tile, (q0, q1), (k0, k1), (v0, v1), (o0, o1), lse_ref),
        [unit(f) for unit in LOCAL_UNITS],
    )


def cross_kernel(f, *refs):
    ins, (o_ref, lse_ref) = refs[:12], refs[12:]
    outs = (o_ref.at[0], o_ref.at[1])
    for early, at in ((1, 0), (0, 6)):
        q0, q1, k0, k1, v0, v1 = ins[at : at + 6]
        sweep(
            f,
            q0.shape[1],
            functools.partial(softmax_tile, (q0, q1), (k0, k1), (v0, v1), outs, lse_ref),
            [(f[2] == early, CROSS_UNITS)],
        )


def head(array, at):
    return (array, (HEAD_DIM, array.shape[-1]), lambda h, f: (at + h, 0))


def lse_spec(array):
    return (array, (1,) + array.shape[1:], lambda h, f: (h, 0, 0))


def lse_out(heads, length):
    return ((heads, 2, length), F32, (1, 2, length), lambda h, f: (h, 0, 0))


def cross_inputs(far, own, other, first, heads):
    high = HALF_HEADS + first
    return [
        head(far[0], 0),
        head(far[1], 0),
        head(own, 6 + high),
        head(other, 6 + high),
        head(own, 12 + high),
        head(other, 12 + high),
        head(own, first),
        head(other, first),
        head(far[0], 0),
        head(far[1], 0),
        head(far[0], heads),
        head(far[1], heads),
    ]


def merge_kernel(
    f, la0, la1, lsea, lb0, lb1, lseb, ca, lseca, cb, lsecb, ba, lseba, bb, lsebb,
    a0, a1, lse_out, high_ref, lse_high,
):
    def rows(h):
        return slice(h * HEAD_DIM, (h + 1) * HEAD_DIM)

    def put(h, i, value, lse):
        value = value.astype(BF)
        (a0, a1)[i][rows(h)] = value
        lse_out[h, i : i + 1] = lse
        if h >= HALF_HEADS:
            high_ref[i, rows(h - HALF_HEADS)] = value
            lse_high[h - HALF_HEADS, i : i + 1] = lse

    for h in range(2 * HALF_HEADS):
        local, lse_l, at = ((la0, la1), lsea, h) if h < 4 else ((lb0, lb1), lseb, h - 4)
        low, there = h < HALF_HEADS, h % HALF_HEADS
        if there < PIECES[0]:
            far, lse_c = (ca, lseca) if low else (ba, lseba)
        else:
            far, lse_c, there = (cb, lsecb, 0) if low else (bb, lsebb, 0)
        for i in (0, 1):
            near, lse_near = local[i][rows(at)], lse_l[at, i : i + 1]

            @pl.when(f[2] == 1)
            def _():
                put(h, i, near, lse_near)

            @pl.when(f[2] == 0)
            def _():
                lse_far = lse_c[there, i : i + 1]
                top = jnp.maximum(lse_near, lse_far)
                lse = top + jnp.log2(jnp.exp2(lse_near - top) + jnp.exp2(lse_far - top))
                value = near * jnp.exp2(lse_near - lse) + far[i, rows(there)].astype(F32) * jnp.exp2(
                    lse_far - lse
                )
                put(h, i, value, lse)


def gradient_tile(
    q_refs, k_refs, v_refs, g_refs, o_refs, lse_ref, dq_refs, dk_acc, dv_acc, unit, at, first
):
    qp, keys = unit
    qs, ks = spans(at, first)
    q, g = q_refs[qp][:, qs], g_refs[qp][:, qs]
    lse = lse_ref[0, qp : qp + 1, qs]
    delta = jnp.sum(g.astype(F32) * o_refs[qp][:, qs].astype(F32), axis=0, keepdims=True)
    dq = None
    for kp in keys:
        k, v = k_refs[kp][:, ks], v_refs[kp][:, ks]
        weights = jnp.exp2(mask_tail(dot(k, q, 0, 0) * SCALE2) - lse)
        ds = (weights * (dot(v, g, 0, 0) - delta)).astype(BF)
        term = dot(k, ds, 1, 0)
        dq = term if dq is None else dq + term
        dk_acc[kp, :, ks] += dot(q, ds, 1, 1)
        dv_acc[kp, :, ks] += dot(g, weights.astype(BF), 1, 1)
    dq_refs[qp][:, qs] = (dq * SCALE).astype(BF)


def local_back_kernel(
    f, q0, q1, k0, k1, v0, v1, g0, g1, o0, o1, lse_ref, d0, d1, dk_acc, dv_acc
):
    dk_acc[...] = jnp.zeros_like(dk_acc)
    dv_acc[...] = jnp.zeros_like(dv_acc)
    sweep(
        f,
        q0.shape[1],
        functools.partial(
            gradient_tile,
            (q0, q1),
            (k0, k1),
            (v0, v1),
            (g0, g1),
            (o0, o1),
            lse_ref,
            (d0.at[0], d1.at[0]),
            dk_acc,
            dv_acc,
        ),
        [unit(f) for unit in LOCAL_UNITS],
    )
    for i, ref in ((0, d0), (1, d1)):
        ref[1] = (dk_acc[i] * SCALE).astype(BF)
        ref[2] = dv_acc[i].astype(BF)


def cross_back_kernel(f, *refs):
    ins, more = refs[:12], refs[12:]
    (ga0, ga1, oa, lse_a, gb0, gb1, ob0, ob1, lse_b, kept_0, kept_1, sent_0, sent_1, dk_acc, dv_acc) = more
    dk_acc[...] = jnp.zeros_like(dk_acc)
    dv_acc[...] = jnp.zeros_like(dv_acc)
    for early, at, grads, outs, lse_ref, dq_ref in (
        (1, 0, (ga0, ga1), (oa.at[0], oa.at[1]), lse_a, sent_0),
        (0, 6, (gb0, gb1), (ob0, ob1), lse_b, kept_0),
    ):
        q0, q1, k0, k1, v0, v1 = ins[at : at + 6]
        sweep(
            f,
            q0.shape[1],
            functools.partial(
                gradient_tile,
                (q0, q1),
                (k0, k1),
                (v0, v1),
                grads,
                outs,
                lse_ref,
                (dq_ref.at[0], dq_ref.at[1]),
                dk_acc,
                dv_acc,
            ),
            [(f[2] == early, CROSS_UNITS)],
        )
    for early, dk_ref, dv_ref, rest_ref in ((1, kept_0, kept_1, sent_1), (0, sent_0, sent_1, kept_1)):

        @pl.when(f[2] == early)
        def _():
            for i in (0, 1):
                dk_ref[i] = (dk_acc[i] * SCALE).astype(BF)
                dv_ref[i] = dv_acc[i].astype(BF)
            rest_ref[...] = jnp.zeros_like(rest_ref)


def gelu_pair(u):
    k = math.sqrt(2 / math.pi)
    square = u * u
    t = jnp.tanh(k * u * (1.0 + 0.044715 * square))
    half = 0.5 + 0.5 * t
    slope = half + 0.5 * u * (1.0 - t * t) * (k * (1.0 + 3 * 0.044715 * square))
    return u * half, slope


def chunks(length):
    return [slice(at, at + SHORT) for at in range(0, length, SHORT)]


def ff_tile(n_ref, cot_ref, wu_ref, wd_ref, y_ref, c_ref, act_ref, gup_ref):
    for at in chunks(n_ref.shape[0]):
        act, slope = gelu_pair(dot(n_ref[at], wu_ref[...], 1, 0))
        act = act.astype(BF)
        grad_up = (dot(cot_ref[at], wd_ref[...], 1, 1) * slope).astype(BF)
        act_ref[at], gup_ref[at] = act, grad_up
        y_ref[at] += dot(act, wd_ref[...], 1, 0)
        c_ref[at] += dot(grad_up, wu_ref[...], 1, 1)


def feed_kernel(
    f, x_ref, emb_ref, a_ref, b_ref, wa_ref, wb_ref, gain_ref, cot_ref, wu_ref, wd_ref,
    dds_ref, dus_ref, ddo_ref, duo_ref, out_ref, gres_ref, ga_ref, gb_ref, gah_ref, gbh_ref, dgain_ref, dwa_ref, dwb_ref,
    res_ref, n_ref, nt_ref, y_ref, c_ref, act_ref, gup_ref,
):
    step, steps = pl.program_id(0), pl.num_programs(0)

    @pl.when(step == 0)
    def _():
        for at in chunks(n_ref.shape[0]):
            residual = (
                x_ref[at].astype(F32)
                + emb_ref[pl.ds(f[3], 1), :]
                + dot(a_ref[:, at], wa_ref[...], 0, 0)
                + dot(b_ref[:, at], wb_ref[...], 0, 0)
            )
            res_ref[at] = residual
            center, inv = centered(residual)
            normed2 = center * inv * gain_ref[1:2]
            n_ref[at] = normed2.astype(BF)
            nt_ref[:, at] = normed2.T.astype(BF)
            y_ref[at] = residual
            c_ref[at] = jnp.zeros_like(residual)

    ff_tile(n_ref, cot_ref, wu_ref, wd_ref, y_ref, c_ref, act_ref, gup_ref)
    down = dot(act_ref[...], cot_ref[...], 0, 0).astype(BF)
    up = dot(nt_ref[...], gup_ref[...], 1, 0).astype(BF)

    @pl.when(step < steps // 2)
    def _():
        dds_ref[...], dus_ref[...] = down, up

    @pl.when(step >= steps // 2)
    def _():
        ddo_ref[...], duo_ref[...] = down, up

    @pl.when(step == steps - 1)
    def _():
        dgain = None
        grads = []
        for at in chunks(n_ref.shape[0]):
            out_ref[at] = y_ref[at].astype(BF)
            center, inv = centered(res_ref[at])
            n2 = center * inv
            c = c_ref[at]
            part = jnp.sum(c * n2, axis=0, keepdims=True)
            dgain = part if dgain is None else dgain + part
            e = c * gain_ref[1:2]
            grad = cot_ref[at].astype(F32) + inv * (
                e
                - jnp.mean(e, axis=-1, keepdims=True)
                - n2 * jnp.mean(e * n2, axis=-1, keepdims=True)
            )
            gres_ref[at] = grad
            grad = grad.astype(BF)
            grads.append(grad)
            mine = dot(wa_ref[...], grad, 1, 1).astype(BF)
            theirs = dot(wb_ref[...], grad, 1, 1).astype(BF)
            ga_ref[:, at], gb_ref[:, at] = mine, theirs
            gah_ref[:, at], gbh_ref[:, at] = mine[HALF:], theirs[HALF:]
        dgain_ref[...] = dgain
        grad = jnp.concatenate(grads, 0)
        dwa_ref[...] = dot(a_ref[...], grad, 1, 0).astype(BF)
        dwb_ref[...] = dot(b_ref[...], grad, 1, 0).astype(BF)


def combine_kernel(f, da0, da1, db0, db1, dc0, dc1, kept_0, kept_1, came_0, came_1, g0, g1):
    part = pl.program_id(0)
    late, early = f[2] == 0, f[2] == 1

    def put(low, high):
        for i, (refs, g) in enumerate((((da0, db0, dc0), g0), ((da1, db1, dc1), g1))):
            local = jnp.concatenate([d[0] for d in refs], 0)
            if low is None:
                g[...] = local
            else:
                more = jnp.concatenate([low[i], high[i]], 0)
                g[...] = (local.astype(F32) + more.astype(F32)).astype(BF)

    @pl.when(late & (part == 0))
    def _():
        put(kept_0, came_0)

    @pl.when(early & (part == 1))
    def _():
        put(came_0, kept_0)

    @pl.when(early & (part == 2))
    def _():
        put(came_1, kept_1)

    @pl.when((late & (part > 0)) | (early & (part == 0)))
    def _():
        put(None, None)


def project_grad_kernel(f, g0, g1, n0_ref, n1_ref, s0_ref, k0_ref, s1_ref, k1_ref, *, at):
    value = dot(n0_ref[...], g0[...], 1, 1) + dot(n1_ref[...], g1[...], 1, 1)
    for i, (sent_ref, kept_ref) in enumerate(((s0_ref, k0_ref), (s1_ref, k1_ref))):
        sent, kept = pick(f[at[i]], value[i * (D // 2) : (i + 1) * (D // 2)])
        sent_ref[...] = sent.astype(BF)
        kept_ref[...] = kept.astype(BF)


def input_grad_kernel(
    f, g_ref, h_ref, wg_ref, wh_ref, x_ref, emb_ref, gain_ref, gres_ref, dgain_ref, gin_ref, sums_ref, acc
):
    part = pl.program_id(0)
    value = dot(wg_ref[...], g_ref[...], 1, 0) + dot(wh_ref[...], h_ref[...], 1, 0)

    @pl.when(part == 0)
    def _():
        acc[...] = value

    @pl.when(part > 0)
    def _():
        acc[...] += value

    @pl.when(part == pl.num_programs(0) - 1)
    def _():
        center, inv = centered(hidden_of(f, x_ref, emb_ref))
        n1 = center * inv
        grad = acc[...].T
        e = grad * gain_ref[0:1]
        total = gres_ref[...] + inv * (
            e - jnp.mean(e, axis=-1, keepdims=True) - n1 * jnp.mean(e * n1, axis=-1, keepdims=True)
        )
        gin_ref[...] = total.astype(BF)
        sums = jnp.sum(total, axis=0, keepdims=True)
        passes = sums_ref.shape[0] - 2
        for i in range(passes):
            sums_ref[i : i + 1] = jnp.where(f[3] == i, sums, 0.0)
        sums_ref[passes : passes + 1] = jnp.sum(grad * n1, axis=0, keepdims=True)
        sums_ref[passes + 1 :] = dgain_ref[...]


def assemble_first_kernel(f, d_own, d_oth, u_own, u_oth, m_own, m_oth, down_ref, up_ref, out_ref):
    step = pl.program_id(0)
    half, at = step // 4, step % 4
    for mine, d, u, m in ((True, d_own, u_own, m_own), (False, d_oth, u_oth, m_oth)):
        here = (half == f[1]) == mine

        @pl.when(here)
        def _():
            up_ref[...] = u[...].astype(F32)

        @pl.when(here & (at < 3))
        def _():
            down_ref[...] = d[...].astype(F32)

        @pl.when(here & (at == 3))
        def _():
            down_ref[...] = m[:GROUP].astype(F32)
            out_ref[...] = m[GROUP:].astype(F32)


def assemble_second_kernel(f, a_own, a_oth, b_own, b_oth, out_ref):
    for mine, a, b in ((True, a_own, b_own), (False, a_oth, b_oth)):

        @pl.when((pl.program_id(0) % 2 == f[1]) == mine)
        def _():
            out_ref[:GROUP] = a[...].astype(F32)
            out_ref[GROUP:] = b[...].astype(F32)


def swap(array, step):
    axis, mask, size, _ = step
    return lax.ppermute(array, axis, [(i, i ^ mask) for i in range(size)])


def tie(*groups):
    leaves, tree = jax.tree.flatten(groups)
    return jax.tree.unflatten(tree, lax.optimization_barrier(leaves))


def pick(here, total):
    half = total.shape[0] // 2
    low, high = total[:half], total[half:]
    return jnp.where(here == 0, high, low), jnp.where(here == 0, low, high)


def joined(here, own, other):
    return jnp.where(
        here == 0, jnp.concatenate([own, other], 0), jnp.concatenate([other, own], 0)
    )


def round_work(here, own, came, mode, riders):
    if mode == "join":
        cut = own.shape[0] - riders
        value = joined(here, own[:cut], came[:cut])
        return (jnp.concatenate([value, own[cut:] + came[cut:]], 0) if riders else value,)
    total = own + came
    return (total,) if mode == "sum" else pick(here, total)


def round_kernel(f, *refs, modes, at, riders):
    refs = list(refs)
    ins, outs = refs[: 2 * len(modes)], refs[2 * len(modes) :]
    for i, mode in enumerate(modes):
        own, came = ins[2 * i][...].astype(F32), ins[2 * i + 1][...].astype(F32)
        for value in round_work(f[at[i]], own, came, mode, riders[i]):
            outs.pop(0)[...] = value.astype(BF)


def whole_call(kernel, flags, ins, outs, name):
    vmem = pl.BlockSpec(memory_space=pltpu.VMEM)
    size = sum(math.prod(shape) for shape in [a.shape for a in ins] + outs)
    return pl.pallas_call(
        kernel,
        in_specs=[pl.BlockSpec(memory_space=pltpu.SMEM)] + [vmem] * len(ins),
        out_specs=[vmem] * len(outs),
        out_shape=[jax.ShapeDtypeStruct(shape, BF) for shape in outs],
        cost_estimate=cost(BRIEF),
        compiler_params=pltpu.CompilerParams(vmem_limit_bytes=2 * size + (8 << 20)),
        name=name,
    )(flags, *ins)


HALVE, FULL, JOIN = 0, 1, 2


class Chain:
    def __init__(self, steps, whole_steps, sent, kept):
        cut = len(steps) - whole_steps
        self.plan = (
            [(HALVE, step) for step in steps[:cut]]
            + [(FULL, step) for step in steps[cut:]]
            + [(JOIN, step) for step in reversed(steps[:cut])]
        )
        self.sent, self.kept, self.came, self.riders = sent, kept, None, 0

    def done(self):
        return not self.plan


def land(flags, chains):
    chains = [c for c in chains if c.came is not None]
    modes, at, ins, outs, riders = [], [], [], [], [c.riders for c in chains]
    for c in chains:
        what, step = c.plan.pop(0)
        own = c.kept if what == HALVE else c.sent
        rows, columns = own.shape
        if what == JOIN:
            modes.append("join")
            at.append(step[3])
            outs += [(2 * rows - c.riders, columns)]
        elif c.plan and c.plan[0][0] == HALVE:
            modes.append("split")
            at.append(c.plan[0][1][3])
            outs += [(rows // 2, columns)] * 2
        else:
            modes.append("sum")
            at.append(0)
            outs += [(rows, columns)]
        ins += [own, c.came]
    if all(shape[0] % 8 == 0 for shape in outs):
        kernel = functools.partial(round_kernel, modes=modes, at=at, riders=riders)
        results = list(whole_call(kernel, flags, ins, outs, "round"))
    else:
        results = []
        for i, mode in enumerate(modes):
            own, came = (a.astype(F32) for a in ins[2 * i : 2 * i + 2])
            results += [
                v.astype(BF) for v in round_work(flags[at[i]], own, came, mode, riders[i])
            ]
    for c, mode in zip(chains, modes, strict=True):
        c.came, c.sent = None, results.pop(0)
        if mode == "split":
            c.kept = results.pop(0)


def open_kernel(f, dd, ddr, du, dur, dw, dwr, *outs, at):
    def add(left, right):
        return left[...].astype(F32) + right[...].astype(F32)

    down, up, out = add(dd, ddr), add(du, dur), add(dw, dwr)
    cut = down.shape[0] - GROUP
    for i, value in enumerate((down[:cut], up, jnp.concatenate([down[cut:], out], 0))):
        sent, kept = pick(f[at[i]], value)
        outs[2 * i][...] = sent.astype(BF)
        outs[2 * i + 1][...] = kept.astype(BF)


def beside(chains, *more):
    chains = [c for c in chains if c.came is not None]
    arrays, more = tie([c.came for c in chains], more)
    for c, array in zip(chains, arrays, strict=True):
        c.came = array
    return more


def send(chains, *more):
    chains = [c for c in chains if not c.done()]
    loads, more = tie([c.sent for c in chains], more)
    for c, load in zip(chains, loads, strict=True):
        c.sent, c.came = load, swap(load, c.plan[0][1])
    return more


def on_device(
    sizes, block_input, segments, pass_emb, gain_attn, w_qkv, w_out, gain_mlp, w_up, w_down, cotangent
):
    passes, n_dp = sizes
    core = ("pass", 1, passes, 1)
    cross = ("pass", 2, passes, 4)
    lanes = [("dp", 1 << i, n_dp, 5 + i) for i in range(n_dp.bit_length() - 1)]
    ring = [cross] + lanes
    by_y = lanes[:1] + [cross] + lanes[:0:-1]
    orders = [ring, by_y, ring[2:] + [lanes[0], cross]]

    pass_here = lax.axis_index("pass")
    core_here = pass_here & 1
    length = segments.shape[0]
    place = [core_here, (pass_here < 2).astype(jnp.int32), pass_here] + [
        (lax.axis_index(axis) >> (mask.bit_length() - 1)) & 1 for axis, mask, _, _ in ring
    ]
    start_flags = jnp.stack([jnp.zeros_like(core_here)] + place)

    x, cot = block_input[0], cotangent[0]
    emb = fixed(pass_emb)
    gains = jnp.stack([gain_attn, gain_mlp])

    normed, theirs, *theirs_cross = call(
        norm_project_kernel,
        start_flags,
        (3,),
        [fixed(x), emb, fixed(gains), (w_qkv, (D, GROUP), lambda i, f: (0, 2 * i + 1 - f[1]))],
        [out_fixed((D, length), BF)] + projection_outs(length),
        BRIEF,
        "norm_project",
    )
    other = swap(theirs, core)
    own, *own_cross = call(
        project_kernel,
        start_flags,
        (3,),
        [fixed(normed), (w_qkv, (D, GROUP), lambda i, f: (0, 2 * i + f[1]))],
        projection_outs(length),
        BRIEF,
        "project_own",
    )

    across = ("pass", 3, passes, 0)

    def exchange(piece):
        return swap(own_cross[piece], cross), swap(theirs_cross[piece], across)

    def attend_local(first, heads):
        return call(
            local_kernel,
            flags,
            (heads,),
            [head(a, at + first) for at in (0, 6, 12) for a in (own, other)],
            [((heads * HEAD_DIM, length), F32, (HEAD_DIM, length), lambda h, f: (h, 0))] * 2
            + [lse_out(heads, length)],
            BRIEF,
            "attend_local",
        )

    def attend_cross(piece, far):
        heads = PIECES[piece]
        return call(
            cross_kernel,
            flags,
            (heads,),
            cross_inputs(far, own, other, FIRST_HEADS[piece], heads),
            [
                ((2, heads * HEAD_DIM, length), BF, (2, HEAD_DIM, length), lambda h, f: (0, h, 0)),
                lse_out(heads, length),
            ],
            BRIEF,
            "attend_cross",
        )

    same, start_flags = tie((segments[0] == segments[length - 1]).astype(jnp.int32), start_flags)
    flags = start_flags.at[0].set(same)
    far_0 = exchange(0)
    local_0 = attend_local(0, 4)
    far_0, local_0, own_cross, theirs_cross = tie(far_0, local_0, own_cross, theirs_cross)
    far_1 = exchange(1)
    normed_other = swap(normed, core)
    cross_0 = attend_cross(0, far_0)
    far_1, cross_0 = tie(far_1, cross_0)
    o_back_0 = swap(cross_0[0], cross)
    cross_1 = attend_cross(1, far_1)
    cross_1, own, other = tie(cross_1, own, other)
    o_back_1, lse_back_1, lse_back_0 = (
        swap(a, cross) for a in (cross_1[0], cross_1[1], cross_0[1])
    )
    local_1 = attend_local(4, 2)
    o_back_0, o_back_1, lse_back_0, lse_back_1, local_1 = tie(
        o_back_0, o_back_1, lse_back_0, lse_back_1, local_1
    )
    half_rows = (HALF, length)
    att_own, att_pair, lse, att_high, lse_high = call(
        merge_kernel,
        flags,
        (1,),
        [
            fixed(a)
            for a in (*local_0, *local_1, *cross_0, *cross_1, o_back_0, lse_back_0, o_back_1, lse_back_1)
        ],
        [out_fixed((GROUP, length), BF)] * 2
        + [
            out_fixed((HEADS // 2, 2, length), F32),
            out_fixed((2, HALF, length), BF),
            out_fixed((HALF_HEADS, 2, length), F32),
        ],
        BRIEF,
        "merge",
    )
    far = [
        jnp.concatenate([a[: 2 * HEAD_DIM], b[:HEAD_DIM], a[2 * HEAD_DIM :], b[HEAD_DIM:]])
        for a, b in zip(far_0, far_1, strict=True)
    ]
    cross_in = cross_inputs(far, own, other, 0, HALF_HEADS)
    att_other = swap(att_pair, core)
    att_early, lse_early = swap(att_high, cross), swap(lse_high, cross)
    att_own, att_other, normed_other = tie(att_own, att_other, normed_other)

    w_half = [(w_out, (GROUP, D), lambda i, f: (f[1], 0)), (w_out, (GROUP, D), lambda i, f: (1 - f[1], 0))]
    ff_half = w_up.shape[1] // 2
    steps = ff_half // FF_TILE

    def tile_at(i, f):
        return jnp.where(i < steps, 1 - f[1], f[1]) * steps + i % steps

    sent_at, own_at = lambda i: jnp.minimum(i, steps - 1), lambda i: jnp.maximum(i - steps, 0)
    tokens = (length, D)
    (
        down_sent, up_sent, down_own, up_own, output, grad_residual, g_own, g_theirs, g_own_high, g_theirs_high,
        dgain_mlp, out_own, out_sent,
    ) = call(
        feed_kernel,
        flags,
        (2 * steps,),
        [held(x), emb, held(att_own), held(att_other)]
        + w_half
        + [held(gains), held(cot)]
        + [
            (w_up, (D, FF_TILE), lambda i, f: (0, tile_at(i, f))),
            (w_down, (FF_TILE, D), lambda i, f: (tile_at(i, f), 0)),
        ],
        [
            ((ff_half, D), BF, (FF_TILE, D), lambda i, f: (sent_at(i), 0)),
            ((D, ff_half), BF, (D, FF_TILE), lambda i, f: (0, sent_at(i))),
            ((ff_half, D), BF, (FF_TILE, D), lambda i, f: (own_at(i), 0)),
            ((D, ff_half), BF, (D, FF_TILE), lambda i, f: (0, own_at(i))),
            (tokens, BF, tokens, lambda i, f: (0, 0)),
            (tokens, F32, tokens, lambda i, f: (0, 0)),
            out_held((GROUP, length), BF),
            out_held((GROUP, length), BF),
            out_held(half_rows, BF),
            out_held(half_rows, BF),
            out_held((1, D), F32),
            out_held((GROUP, D), BF),
            out_held((GROUP, D), BF),
        ],
        BRIEF,
        "feed",
        [pltpu.VMEM(tokens, F32), pltpu.VMEM(tokens, BF), pltpu.VMEM((D, length), BF)]
        + [pltpu.VMEM(tokens, F32)] * 2
        + [pltpu.VMEM((length, FF_TILE), BF)] * 2,
        6,
    )
    (
        down_sent, up_sent, down_own, up_own, output, grad_residual, g_own, g_theirs, g_own_high, g_theirs_high,
        dgain_mlp, out_own, out_sent, att_early, lse_early,
    ) = tie(
        down_sent, up_sent, down_own, up_own, output, grad_residual, g_own, g_theirs, g_own_high, g_theirs_high,
        dgain_mlp, out_own, out_sent, att_early, lse_early,
    )
    g_other = swap(g_theirs, core)
    early_g = (swap(g_own_high, cross), swap(g_theirs_high, across))
    g_other, down_sent, up_sent, out_sent = tie(g_other, down_sent, up_sent, out_sent)
    out_recv, down_recv, up_recv = (swap(a, core) for a in (out_sent, down_sent, up_sent))

    accumulators = [pltpu.VMEM((2, HEAD_DIM, length), F32)] * 2

    def local_back(at, heads, g0, g1):
        return call(
            local_back_kernel,
            flags,
            (heads,),
            [head(a, base + at) for base in (0, 6, 12) for a in (own, other)]
            + [head(a, at) for a in (g0, g1, att_own, att_pair)]
            + [(lse, (1, 2, length), lambda h, f: (at + h, 0, 0))],
            [((3, heads * HEAD_DIM, length), BF, (3, HEAD_DIM, length), lambda h, f: (0, h, 0))] * 2,
            BRIEF,
            "attend_back_local",
            accumulators,
        )

    d_0 = local_back(0, 2, g_own, g_other)
    d_0, early_g_own, out_own = tie(d_0, early_g[0], out_own)
    early_g = (early_g_own, early_g[1])
    opened = whole_call(
        functools.partial(open_kernel, at=[steps_[0][3] for steps_ in orders]),
        flags,
        [down_own, down_recv, up_own, up_recv, out_own, out_recv],
        [shape for shape in (((ff_half - GROUP) // 2, D), (GROUP, ff_half), (GROUP, D)) for _ in (0, 1)],
        "open",
    )
    first = [Chain(orders[i], 1, *opened[2 * i : 2 * i + 2]) for i in range(3)]
    (early_g,) = send(first, early_g)
    *cross_kept, sent_0, sent_1 = call(
        cross_back_kernel,
        flags,
        (HALF_HEADS,),
        cross_in
        + [
            head(early_g[0], 0),
            head(early_g[1], 0),
            (att_early, (2, HEAD_DIM, length), lambda h, f: (0, h, 0)),
            lse_spec(lse_early),
            head(g_own, 0),
            head(g_other, 0),
            head(att_own, 0),
            head(att_pair, 0),
            lse_spec(lse),
        ],
        [((2, HALF, length), BF, (2, HEAD_DIM, length), lambda h, f: (0, h, 0))] * 4,
        BRIEF,
        "attend_back_cross",
        accumulators,
    )
    cross_kept, sent_0, g_own, g_other = tie(cross_kept, sent_0, g_own, g_other)
    came_0 = swap(sent_0, cross)
    d_1 = local_back(2, 2, g_own, g_other)
    (d_1,) = beside(first, d_1)
    land(flags, first)
    g_own, g_other, sent_1 = send(first, g_own, g_other, sent_1)
    came_1 = swap(sent_1, cross)
    d_2 = local_back(4, 2, g_own, g_other)
    d_2, came_0 = beside(first, d_2, came_0)
    land(flags, first)
    d_2, came_0 = send(first, d_2, came_0)
    (came_1,) = beside(first, came_1)
    few = (1, 2 * HEAD_DIM, length)
    gp_own, gp_pair = call(
        combine_kernel,
        flags,
        (3,),
        [(d, few, lambda i, f: (i, 0, 0)) for d in (*d_0, *d_1, *d_2)]
        + [
            fixed(array) for array in (*cross_kept, came_0, came_1)
        ],
        [((3 * GROUP, length), BF, (GROUP, length), lambda i, f: (i, 0))] * 2,
        BRIEF,
        "combine",
    )
    gp_other = swap(gp_pair, core)
    opened = call(
        functools.partial(project_grad_kernel, at=[ring[0][3], by_y[0][3]]),
        flags,
        (3,),
        [(g, (GROUP, length), lambda i, f: (i, 0)) for g in (gp_own, gp_pair)]
        + [fixed(normed), fixed(normed_other)],
        [((D // 4, 3 * GROUP), BF, (D // 4, GROUP), lambda i, f: (0, i))] * 4,
        BRIEF,
        "project_grad",
    )
    gp_own, gp_other, opened = beside(first, gp_own, gp_other, opened)
    second = [Chain(order, 2, *opened[2 * i : 2 * i + 2]) for i, order in enumerate((ring, lanes[:1] + [cross] + lanes[1:]))]
    land(flags, first)
    gp_own, gp_other = send(first + second, gp_own, gp_other)
    grad_input, sums = call(
        input_grad_kernel,
        flags,
        (3,),
        [
            (gp_own, (GROUP, length), lambda i, f: (i, 0)),
            (gp_other, (GROUP, length), lambda i, f: (i, 0)),
            (w_qkv, (D, GROUP), lambda i, f: (0, 2 * i + f[1])),
            (w_qkv, (D, GROUP), lambda i, f: (0, 2 * i + 1 - f[1])),
            fixed(x),
            emb,
            fixed(gains),
            fixed(grad_residual),
            fixed(dgain_mlp),
        ],
        [out_fixed(tokens, BF), out_fixed((passes + 2, D), F32)],
        BRIEF,
        "input_grad",
        [pltpu.VMEM((D, length), F32)],
    )
    grad_input, sums = beside(first + second, grad_input, sums)
    land(flags, first + second)
    while second[1].plan[0][0] == HALVE:
        send(first + second)
        land(flags, first + second)
    rider = jnp.pad(sums, ((0, 8 - passes - 2), (0, 3 * GROUP - D))).astype(BF)
    second[1].sent, second[1].riders = jnp.concatenate([second[1].sent, rider]), 8
    while not first[0].done():
        send(first + second)
        land(flags, first + second)
    send(second)
    pairs = [(c.sent, swap(c.sent, core)) for c in first]
    (pairs,) = beside(second, pairs)
    land(flags, second)
    third = [a for pair in pairs for a in pair]
    at_most = [
        (third[i], (GROUP, D), lambda j, f: (jnp.minimum(j % 4, 2), 0)) for i in (0, 1)
    ] + [(third[i], (D, GROUP), lambda j, f: (0, j % 4)) for i in (2, 3)]
    down_total, up_total, out_total = call(
        assemble_first_kernel,
        flags,
        (8,),
        at_most + [fixed(third[4]), fixed(third[5])],
        [
            ((4 * D, D), F32, (GROUP, D), lambda j, f: (j, 0)),
            ((D, 4 * D), F32, (D, GROUP), lambda j, f: (0, j)),
            ((D, D), F32, (GROUP, D), lambda j, f: (j // 4, 0)),
        ],
        BRIEF,
        "assemble_first",
    )
    while not second[0].done():
        send(second)
        down_total, up_total, out_total = beside(second, down_total, up_total, out_total)
        land(flags, second)
    lasts = [(c.sent, swap(c.sent, core)) for c in second]
    small = sum(a[D // 2 :, :D].astype(F32) for a in lasts[1])
    qkv_total = call(
        assemble_second_kernel,
        flags,
        (6,),
        [
            (a, (GROUP, GROUP), lambda j, f: (0, j // 2))
            for pair in lasts
            for a in pair
        ],
        [((D, 3 * D), F32, (D, GROUP), lambda j, f: (0, j))],
        BRIEF,
        "assemble_second",
    )[0]
    return (
        output[None],
        grad_input[None],
        small[:passes],
        small[passes],
        qkv_total,
        out_total,
        small[passes + 1],
        up_total,
        down_total,
    )


def solution(mesh):
    sizes = (mesh.shape["pass"], mesh.shape["dp"])
    tokens = P("pass", "dp", None)
    in_specs = (tokens, P("dp")) + (P(),) * 7 + (tokens,)
    out_specs = (tokens, tokens) + (P(),) * 7
    return jax.shard_map(
        functools.partial(on_device, sizes),
        mesh=mesh,
        in_specs=in_specs,
        out_specs=out_specs,
        check_vma=False,
    )
```
